32 devices in a mesh: groups: 1, gx: 32 (over z, y, x, core).
Axes of the slice: x: 2, y: 2, z: 4, core: 2. Of those that a mesh axis runs over, the one named last changes fastest.
Arguments:
- plume_state: bfloat16 [128, 20, 256, 2, 128], P(('groups', 'gx')), may hold values from -6 to 6
- out_cotangent: bfloat16 [128, 20, 256, 2, 128], P(('groups', 'gx')), may hold values from -6 to 6
- spectral_weight: bfloat16 [20, 20, 2, 24, 1152], P(None, None, None, None, 'gx'), may hold values from -12 to 12
- pointwise_weight: bfloat16 [20, 20], replicated, may hold values from -1.25 to 1.25
Outputs:
- state_grad: bfloat16 [128, 20, 256, 2, 128], P(('groups', 'gx'))
- spectral_grad: float32 [20, 20, 2, 24, 1152], P('groups', None, None, None, 'gx')
- pointwise_grad: float32 [20, 20], P('groups')
The draws below stay inside these ranges and needn't reach their ends.
All inputs are finite; a program needn't handle non-finite values.
Results may differ from the reference program's by a relative error of at most 0.012.
Values may be sent and summed in bfloat16 or wider, within the bound.
No kernel may reach another device: no remote copies, remote signals or barrier semaphores. Data moves between devices by JAX's collectives and lax.ppermute only.
A program may use at most 256 MiB of HBM per device.

```python
import math
import jax
import jax.numpy as jnp
from jax import lax

C = 20
NX = 128
NY = 256
NZ = 128
NT = 2
KX = 24
KY = 24
KZ = 24
MODES = 1152


def block_levels(rng, shape, cuts, smallest, largest):
    loudness = 1.0
    for position, shards_of in cuts:
        draws = jax.random.uniform(jax.random.fold_in(jax.random.fold_in(rng, 6), position), (shards_of,), jnp.float32, smallest / len(cuts), largest / len(cuts))
        loudness = loudness * jnp.repeat(jnp.exp(draws), shape[position] // shards_of).reshape((-1,) + (1,) * (len(shape) - 1 - position))
    return loudness


def bell_draw(key, shape, scale, most, shards=(), kind=jnp.bfloat16):
    gain = block_levels(key, shape, shards, -0.22, 0.18) if shards else 1.0
    entries = jax.random.normal(key, shape, jnp.float32) * scale * gain
    return jnp.minimum(jnp.maximum(entries, -most), most).astype(kind)


def setup_inputs(seed: int = 0, part: int = 0) -> dict:
    streams_of = jax.random.split(jax.random.key(seed), 5)
    part_keys = jax.random.split(jax.random.fold_in(streams_of[4], part), 5)
    plume_state = bell_draw(part_keys[0], (NX, C, NY, NT, NZ), 1.0, 6.0, ((0, 32),))
    out_cotangent = bell_draw(part_keys[1], (NX, C, NY, NT, NZ), 1.0, 6.0, ((0, 32),))
    spectral_weight = bell_draw(streams_of[2], (C, C, 2, KX, MODES), 2.0, 12.0, ((4, 32),))
    pointwise_weight = bell_draw(streams_of[3], (C, C), C ** -0.5, 1.25)
    return dict(plume_state=plume_state, out_cotangent=out_cotangent, spectral_weight=spectral_weight, pointwise_weight=pointwise_weight)


def depth_basis(steps_t, cells_z, kept_z):
    depth_pos = jnp.arange(cells_z, dtype=jnp.int32)
    column = jnp.arange(kept_z, dtype=jnp.int32)
    half_kept = kept_z // 2
    frequency = jnp.where(column < half_kept, column, column - half_kept + 1)
    turns = depth_pos[:, None] * frequency[None, :] % cells_z
    angle = 2.0 * math.pi / cells_z * turns.astype(jnp.float32)
    depth_part = jnp.where(column[None, :] < half_kept, jnp.cos(angle), jnp.sin(angle)) * math.sqrt(2.0 / cells_z)
    time_pos = jnp.arange(steps_t, dtype=jnp.int32)
    parity = (1 - 2 * (time_pos % 2)).astype(jnp.float32)
    time_part = jnp.stack([jnp.ones((steps_t,), jnp.float32), parity], axis=1) * math.sqrt(0.5)
    joined = time_part[:, None, :, None] * depth_part[None, :, None, :]
    return joined.reshape(steps_t * cells_z, 2 * kept_z).astype(jnp.bfloat16)

def wave_basis(positions, cells, kept):
    frequency = jnp.arange(kept, dtype=jnp.int32) - kept // 2
    turns = frequency[:, None] * positions[None, :] % cells
    angle = 2.0 * math.pi / cells * turns.astype(jnp.float32)
    scale = 1.0 / math.sqrt(cells)
    return ((jnp.cos(angle) * scale).astype(jnp.bfloat16), (jnp.sin(angle) * scale).astype(jnp.bfloat16))

def einsum_high(form, left, right):
    return jnp.einsum(form, left, right, precision=lax.Precision.HIGHEST)

def forward_modes(fields, basis, y_cosine, y_sine, x_cosine, x_sine):
    width_x, channels, width_y, width_t, width_z = fields.shape
    flat = fields.reshape(width_x, channels, width_y, width_t * width_z).astype(jnp.float32)
    y_table = jnp.concatenate([y_cosine, -y_sine], axis=0).astype(jnp.float32)
    projected = einsum_high('by,xcyn->xcbn', y_table, flat).astype(jnp.bfloat16)
    y_coeffs = einsum_high('xcbn,nq->xcbq', projected.astype(jnp.float32), basis.astype(jnp.float32)).astype(jnp.bfloat16)
    y_coeffs = y_coeffs.reshape(width_x, channels, 2, -1).astype(jnp.float32)
    real_in = y_coeffs[:, :, 0]
    imag_in = y_coeffs[:, :, 1]
    x_cos = x_cosine.astype(jnp.float32)
    x_sin = x_sine.astype(jnp.float32)
    real_out = einsum_high('ax,xcm->cam', x_cos, real_in) + einsum_high('ax,xcm->cam', x_sin, imag_in)
    imag_out = einsum_high('ax,xcm->cam', x_cos, imag_in) - einsum_high('ax,xcm->cam', x_sin, real_in)
    return jnp.stack([real_out, imag_out], axis=1)

def inverse_modes(coefficients, basis, y_cosine, y_sine, x_cosine, x_sine, shape):
    width_x, channels, width_y, width_t, width_z = shape
    real_in = coefficients[:, 0].astype(jnp.float32)
    imag_in = coefficients[:, 1].astype(jnp.float32)
    x_cos = x_cosine.astype(jnp.float32)
    x_sin = x_sine.astype(jnp.float32)
    real_out = einsum_high('ax,cam->xcm', x_cos, real_in) - einsum_high('ax,cam->xcm', x_sin, imag_in)
    imag_out = einsum_high('ax,cam->xcm', x_sin, real_in) + einsum_high('ax,cam->xcm', x_cos, imag_in)
    x_rows = jnp.stack([real_out, imag_out], axis=2).astype(jnp.bfloat16)
    x_rows = x_rows.reshape(width_x, channels, 2 * y_cosine.shape[0], -1).astype(jnp.float32)
    depth_rows = einsum_high('xcbq,nq->xcbn', x_rows, basis.astype(jnp.float32)).astype(jnp.bfloat16)
    y_table = jnp.concatenate([y_cosine, -y_sine], axis=0).astype(jnp.float32)
    restored = einsum_high('by,xcbn->xcyn', y_table, depth_rows.astype(jnp.float32))
    return restored.reshape(width_x, channels, width_y, width_t, width_z)

def mix_modes(weight, coefficients):
    values = weight.astype(jnp.float32)
    weight_real = values[:, :, 0]
    weight_imag = values[:, :, 1]
    real_in = coefficients[:, 0]
    imag_in = coefficients[:, 1]
    real_out = einsum_high('ioam,iam->oam', weight_real, real_in) - einsum_high('ioam,iam->oam', weight_imag, imag_in)
    imag_out = einsum_high('ioam,iam->oam', weight_real, imag_in) + einsum_high('ioam,iam->oam', weight_imag, real_in)
    return jnp.stack([real_out, imag_out], axis=1)

def mix_adjoint(weight, coefficients):
    values = weight.astype(jnp.float32)
    weight_real = values[:, :, 0]
    weight_imag = values[:, :, 1]
    real_in = coefficients[:, 0]
    imag_in = coefficients[:, 1]
    real_out = einsum_high('ioam,oam->iam', weight_real, real_in) + einsum_high('ioam,oam->iam', weight_imag, imag_in)
    imag_out = einsum_high('ioam,oam->iam', weight_real, imag_in) - einsum_high('ioam,oam->iam', weight_imag, real_in)
    return jnp.stack([real_out, imag_out], axis=1)

def weight_gradient(grad_modes, modes):
    real_grad = grad_modes[:, 0]
    imag_grad = grad_modes[:, 1]
    real_mode = modes[:, 0]
    imag_mode = modes[:, 1]
    real_part = einsum_high('iam,oam->ioam', real_mode, real_grad) + einsum_high('iam,oam->ioam', imag_mode, imag_grad)
    imag_part = einsum_high('iam,oam->ioam', real_mode, imag_grad) - einsum_high('iam,oam->ioam', imag_mode, real_grad)
    return jnp.stack([real_part, imag_part], axis=2)

def gelu_slope(values):
    normal_cdf = 0.5 * (1.0 + jax.scipy.special.erf(values * (1.0 / math.sqrt(2.0))))
    normal_pdf = jnp.exp(-0.5 * values * values) * (1.0 / math.sqrt(2.0 * math.pi))
    return normal_cdf + values * normal_pdf

def reference(plume_state, out_cotangent, spectral_weight, pointwise_weight):
    width_x, channels, width_y, width_t, width_z = plume_state.shape
    basis = depth_basis(width_t, width_z, KZ)
    y_cosine, y_sine = wave_basis(jnp.arange(width_y, dtype=jnp.int32), width_y, KY)
    x_cosine, x_sine = wave_basis(jnp.arange(width_x, dtype=jnp.int32), width_x, KX)
    tables = (basis, y_cosine, y_sine, x_cosine, x_sine)
    modes = forward_modes(plume_state, *tables)
    mixed = mix_modes(spectral_weight, modes).astype(jnp.bfloat16)
    spectral = inverse_modes(mixed, *tables, plume_state.shape)
    weight_point = pointwise_weight.astype(jnp.float32)
    state_values = plume_state.astype(jnp.float32)
    pre = spectral + einsum_high('xiytz,io->xoytz', state_values, weight_point)
    grad_pre = (out_cotangent.astype(jnp.float32) * gelu_slope(pre)).astype(jnp.bfloat16)
    grad_modes = forward_modes(grad_pre, *tables)
    spectral_grad = weight_gradient(grad_modes, modes)
    back = mix_adjoint(spectral_weight, grad_modes).astype(jnp.bfloat16)
    grad_values = grad_pre.astype(jnp.float32)
    state_grad = inverse_modes(back, *tables, plume_state.shape) + einsum_high('xoytz,io->xiytz', grad_values, weight_point)
    pointwise_grad = einsum_high('xiytz,xoytz->io', state_values, grad_values) / math.sqrt(width_x * width_y * width_t * width_z)
    return (state_grad.astype(jnp.bfloat16), spectral_grad, pointwise_grad)
```

```python
import functools
import math

import jax
import jax.numpy as jnp
import ml_dtypes
import numpy as np
from jax import lax
from jax.experimental import pallas as pl
from jax.experimental.pallas import tpu as pltpu
from jax.sharding import PartitionSpec as P

KX = 24
KY = 24
KZ = 24
NT = 2
ROW_GROUP = 16
BF16 = jnp.bfloat16
F32 = jnp.float32
VMEM_LIMIT = 56 * 1024 * 1024


def rounded(table):
    return np.asarray(table, np.float64).astype(np.float32).astype(ml_dtypes.bfloat16)


def wave_tables(cells, kept):
    frequency = np.arange(kept) - kept // 2
    angle = 2.0 * np.pi / cells * (frequency[:, None] * np.arange(cells)[None, :] % cells)
    return np.cos(angle) / math.sqrt(cells), np.sin(angle) / math.sqrt(cells)


def depth_table(cells, kept):
    column = np.arange(kept)
    half = kept // 2
    frequency = np.where(column < half, column, column - half + 1)
    angle = 2.0 * np.pi / cells * (np.arange(cells)[:, None] * frequency[None, :] % cells)
    wave = np.where(column[None, :] < half, np.cos(angle), np.sin(angle))
    return wave * math.sqrt(2.0 / cells) * math.sqrt(0.5)


class Plan:
    def __init__(self, slab, channels, width_y, width_z, devices):
        self.slab = slab
        self.channels = channels
        self.width_y = width_y
        self.width_z = width_z
        self.devices = devices
        self.width_x = slab * devices
        self.pairs = KY * NT
        self.owned = self.pairs * KZ // devices
        self.kinds = 3
        self.owners = self.kinds * KZ // self.owned
        self.periods = self.pairs // self.kinds
        self.group = min(channels, 256 // self.owned)
        self.groups = -(-channels // self.group)
        self.lanes = 256 * self.groups
        self.rows_yt = width_y * NT
        sums = 2 * channels * -(-channels // (2 * slab))
        self.extra = 128 * -(-sums // 128)
        self.kind_rows = self.periods * 2
        self.links = [
            (kind, owner)
            for kind in range(self.kinds)
            for owner in range(self.owners)
            if kind * KZ < (owner + 1) * self.owned and owner * self.owned < (kind + 1) * KZ
        ]

    def group_size(self, group):
        return min(self.group, self.channels - group * self.group)

    def y_table(self):
        cosine, sine = wave_tables(self.width_y, KY)
        both = np.stack([cosine, -sine])
        table = np.zeros((self.kinds, self.periods, 2, self.width_y, NT))
        for kind in range(self.kinds):
            for period in range(self.periods):
                pair = self.kinds * period + kind
                for time in range(NT):
                    sign = -1.0 if (time % 2 and pair % 2) else 1.0
                    table[kind, period, :, :, time] = sign * both[:, pair // 2]
        return rounded(table.reshape(self.kinds * self.kind_rows, self.rows_yt))

    def depth_tables(self):
        values = depth_table(self.width_z, KZ)
        tables = np.zeros((len(self.links), self.group, self.width_z, 256))
        for index, (kind, owner) in enumerate(self.links):
            for mode in range(self.owned):
                column = owner * self.owned + mode - kind * KZ
                if 0 <= column < KZ:
                    for channel in range(self.group):
                        tables[index, channel, :, channel * self.owned + mode] = values[:, column]
        return rounded(tables.reshape(len(self.links), self.group * self.width_z, 256))

    def order(self):
        total = self.devices * self.slab * 2
        source = np.arange(total).reshape(self.owners, self.slab, self.periods, 2)
        source = source.transpose(2, 0, 1, 3).reshape(total)
        table = np.zeros((total, total))
        table[np.arange(total), source] = 1.0
        return rounded(table)

    def x_table(self):
        cosine, sine = wave_tables(self.width_x, KX)
        table = np.zeros((2, KX, self.width_x, 2))
        table[0, :, :, 0] = cosine
        table[0, :, :, 1] = sine
        table[1, :, :, 1] = cosine
        table[1, :, :, 0] = -sine
        return rounded(table.reshape(2 * KX, self.width_x * 2))


def dot(left, right):
    return jnp.dot(left, right, preferred_element_type=F32)


def project_depth(plan, proj_ref, depth_ref, order_ref, out_ref):
    for group in range(plan.groups):
        width = plan.group_size(group) * plan.width_z
        start = group * plan.group * plan.width_z
        blocks = []
        for owner in range(plan.owners):
            total = None
            for index, (kind, target) in enumerate(plan.links):
                if target != owner:
                    continue
                term = dot(proj_ref[kind, :, start : start + width], depth_ref[index, :width, :])
                total = term if total is None else total + term
            blocks.append(total.astype(BF16))
        joined = jnp.concatenate(blocks, axis=0)
        ordered = dot(order_ref[...], joined).astype(BF16)
        out_ref[:, group * 256 : (group + 1) * 256] = ordered


def restore_depth(plan, rows_ref, depth_t_ref, order_t_ref, iz_ref):
    block = plan.slab * plan.kind_rows
    for group in range(plan.groups):
        width = plan.group_size(group) * plan.width_z
        start = group * plan.group * plan.width_z
        rows = dot(order_t_ref[...], rows_ref[:, group * 256 : (group + 1) * 256]).astype(BF16)
        for kind in range(plan.kinds):
            total = None
            for index, (source, owner) in enumerate(plan.links):
                if source != kind:
                    continue
                part = rows[owner * block : (owner + 1) * block]
                term = dot(part, depth_t_ref[index, :, :width])
                total = term if total is None else total + term
            total = total.astype(BF16)
            for row in range(plan.slab):
                iz_ref[
                    row,
                    kind * plan.kind_rows : (kind + 1) * plan.kind_rows,
                    start : start + width,
                ] = total[row * plan.kind_rows : (row + 1) * plan.kind_rows]


def store_projection(plan, proj_ref, row, lane, values):
    for kind in range(plan.kinds):
        proj_ref[
            kind,
            pl.ds(pl.multiple_of(row * plan.kind_rows, plan.kind_rows), plan.kind_rows),
            pl.ds(lane, values.shape[1]),
        ] = values[kind * plan.kind_rows : (kind + 1) * plan.kind_rows]


def chunk_copy(source, target, sem, chunk, index):
    parts = source.shape[1] // chunk
    place = (index // parts, pl.ds(lax.rem(index, parts) * chunk, chunk))
    return pltpu.make_async_copy(source.at[place], target.at[place], sem.at[index])


def chunk_place(plan, chunk, index):
    parts = plan.channels // chunk
    return index // parts, lax.rem(index, parts) * chunk


def pair_lane(plan, channel):
    return pl.multiple_of(channel * plan.width_z, 2 * plan.width_z)


def forward_kernel(
    plan, chunk, u_hbm, y_ref, depth_ref, order_ref, out_ref, u_ref, proj_ref, u_sem
):
    steps = plan.slab * plan.channels // chunk
    for index in range(steps):
        chunk_copy(u_hbm, u_ref, u_sem, chunk, index).start()

    def step(index, carry):
        chunk_copy(u_hbm, u_ref, u_sem, chunk, index).wait()
        row, first = chunk_place(plan, chunk, index)
        for pair in range(chunk // 2):
            channel = first + 2 * pair
            values = jnp.concatenate([u_ref[row, channel], u_ref[row, channel + 1]], axis=1)
            projected = dot(y_ref[...], values).astype(BF16)
            store_projection(plan, proj_ref, row, pair_lane(plan, channel), projected)
        return carry

    lax.fori_loop(0, steps, step, 0)
    project_depth(plan, proj_ref, depth_ref, order_ref, out_ref)


def slope(values):
    cdf = 0.5 + 0.5 * lax.erf(values * math.sqrt(0.5))
    pdf = jnp.exp(-0.5 * values * values) * (1.0 / math.sqrt(2.0 * math.pi))
    return cdf + values * pdf


def middle_kernel(
    plan,
    chunk,
    rows_ref,
    point_hbm,
    cot_hbm,
    y_ref,
    y_t_ref,
    depth_ref,
    depth_t_ref,
    order_ref,
    order_t_ref,
    grad_hbm,
    out_ref,
    point_ref,
    cot_ref,
    grad_ref,
    iz_ref,
    proj_ref,
    point_sem,
    cot_sem,
    grad_sem,
):
    z = plan.width_z
    steps = plan.slab * plan.channels // chunk
    for index in range(steps):
        chunk_copy(point_hbm, point_ref, point_sem, chunk, index).start()
        chunk_copy(cot_hbm, cot_ref, cot_sem, chunk, index).start()
    restore_depth(plan, rows_ref, depth_t_ref, order_t_ref, iz_ref)

    def step(index, carry):
        chunk_copy(point_hbm, point_ref, point_sem, chunk, index).wait()
        chunk_copy(cot_hbm, cot_ref, cot_sem, chunk, index).wait()
        row, first = chunk_place(plan, chunk, index)
        for pair in range(chunk // 2):
            channel = first + 2 * pair
            lane = pair_lane(plan, channel)
            spectral = dot(y_t_ref[...], iz_ref[row, :, pl.ds(lane, 2 * z)])
            halves = []
            for half in range(2):
                pre = spectral[:, half * z : (half + 1) * z]
                pre = pre + point_ref[row, channel + half].astype(F32)
                grad = cot_ref[row, channel + half].astype(F32) * slope(pre)
                grad = grad.astype(BF16)
                grad_ref[row, channel + half] = grad
                halves.append(grad)
            values = jnp.concatenate(halves, axis=1)
            projected = dot(y_ref[...], values).astype(BF16)
            store_projection(plan, proj_ref, row, lane, projected)
        chunk_copy(grad_ref, grad_hbm, grad_sem, chunk, index).start()
        return carry

    lax.fori_loop(0, steps, step, 0)
    project_depth(plan, proj_ref, depth_ref, order_ref, out_ref)
    for index in range(steps):
        chunk_copy(grad_ref, grad_hbm, grad_sem, chunk, index).wait()


def final_kernel(
    plan,
    chunk,
    scale,
    rows_ref,
    point_hbm,
    y_t_ref,
    depth_t_ref,
    order_t_ref,
    out_hbm,
    sum_ref,
    point_ref,
    out_ref,
    iz_ref,
    point_sem,
    out_sem,
):
    z = plan.width_z
    steps = plan.slab * plan.channels // chunk
    for index in range(steps):
        chunk_copy(point_hbm, point_ref, point_sem, chunk, index).start()
    restore_depth(plan, rows_ref, depth_t_ref, order_t_ref, iz_ref)

    def step(index, carry):
        chunk_copy(point_hbm, point_ref, point_sem, chunk, index).wait()
        row, first = chunk_place(plan, chunk, index)
        for pair in range(chunk // 2):
            channel = first + 2 * pair
            spectral = dot(y_t_ref[...], iz_ref[row, :, pl.ds(pair_lane(plan, channel), 2 * z)])
            for half in range(2):
                total = spectral[:, half * z : (half + 1) * z]
                total = total + point_ref[row, channel + half].astype(F32)
                out_ref[row, channel + half] = total.astype(BF16)
        chunk_copy(out_ref, out_hbm, out_sem, chunk, index).start()
        return carry

    lax.fori_loop(0, steps, step, 0)
    sum_ref[...] = unpack_sums(plan, rows_ref) * scale
    for index in range(steps):
        chunk_copy(out_ref, out_hbm, out_sem, chunk, index).wait()


def pack_rows(plan):
    return 2 * plan.slab


def pack_sums(plan, sums):
    rows = pack_rows(plan)
    count = -(-plan.channels // rows)
    high = sums.astype(BF16)
    low = (sums - high.astype(F32)).astype(BF16)
    pieces = []
    for part in (high.astype(F32), low.astype(F32)):
        spare = count * rows - plan.channels
        if spare:
            part = jnp.concatenate([part, jnp.zeros((spare, plan.channels), F32)], axis=0)
        pieces += [part[index * rows : (index + 1) * rows] for index in range(count)]
    used = 2 * count * plan.channels
    pieces.append(jnp.zeros((rows, plan.extra - used), F32))
    block = jnp.concatenate(pieces, axis=1)
    return jnp.concatenate([block] * plan.devices, axis=0).astype(BF16)


def unpack_sums(plan, rows_ref):
    rows = pack_rows(plan)
    count = -(-plan.channels // rows)
    block = jnp.zeros((rows, plan.extra), F32)
    values = rows_ref[:, plan.lanes : plan.lanes + plan.extra].astype(F32)
    for device in range(plan.devices):
        block = block + values[device * rows : (device + 1) * rows]
    width = plan.channels
    parts = []
    for index in range(count):
        high = block[:, index * width : (index + 1) * width]
        low = block[:, (count + index) * width : (count + index + 1) * width]
        parts.append(high + low)
    return jnp.concatenate(parts, axis=0)[: plan.channels]


def row_copy(source, target, sem, tile, index):
    parts = source.shape[2] // tile
    place = (index // parts, slice(None), pl.ds(lax.rem(index, parts) * tile, tile))
    return pltpu.make_async_copy(source.at[place], target.at[place], sem.at[index])


def row_block(ref, row, start, count):
    channels, z = ref.shape[1], ref.shape[3]
    parts = [
        ref[row, :, pl.ds(start + index * ROW_GROUP, ROW_GROUP), :].reshape(
            channels * ROW_GROUP, z
        )
        for index in range(count)
    ]
    return jnp.concatenate(parts, axis=1)


def point_kernel(tile, weight_ref, u_hbm, out_hbm, u_ref, out_ref, u_sem, out_sem):
    channels, rows, z = u_hbm.shape[1:]
    parts = rows // tile
    steps = u_hbm.shape[0] * parts
    for index in range(steps):
        row_copy(u_hbm, u_ref, u_sem, tile, index).start()

    def step(index, carry):
        row_copy(u_hbm, u_ref, u_sem, tile, index).wait()
        row = index // parts
        base = pl.multiple_of(lax.rem(index, parts) * tile, tile)
        for start in range(0, tile, 2 * ROW_GROUP):
            mixed = dot(weight_ref[...], row_block(u_ref, row, base + start, 2)).astype(BF16)
            for half in range(2):
                out_ref[row, :, pl.ds(base + start + half * ROW_GROUP, ROW_GROUP), :] = mixed[
                    :, half * z : (half + 1) * z
                ].reshape(channels, ROW_GROUP, z)
        row_copy(out_ref, out_hbm, out_sem, tile, index).start()
        return carry

    lax.fori_loop(0, steps, step, 0)
    for index in range(steps):
        row_copy(out_ref, out_hbm, out_sem, tile, index).wait()


def point_sum_kernel(
    tile, u_hbm, g_hbm, same_ref, fold_ref, sum_ref, u_ref, g_ref, total_ref, u_sem, g_sem
):
    parts = u_hbm.shape[2] // tile
    steps = u_hbm.shape[0] * parts
    for index in range(steps):
        row_copy(u_hbm, u_ref, u_sem, tile, index).start()
        row_copy(g_hbm, g_ref, g_sem, tile, index).start()
    total_ref[...] = jnp.zeros_like(total_ref)

    def step(index, carry):
        row_copy(u_hbm, u_ref, u_sem, tile, index).wait()
        row_copy(g_hbm, g_ref, g_sem, tile, index).wait()
        row = index // parts
        base = pl.multiple_of(lax.rem(index, parts) * tile, tile)
        for start in range(0, tile, 8 * ROW_GROUP):
            total_ref[...] += lax.dot_general(
                row_block(u_ref, row, base + start, 8),
                row_block(g_ref, row, base + start, 8),
                (((1,), (1,)), ((), ())),
                preferred_element_type=F32,
            )
        return carry

    lax.fori_loop(0, steps, step, 0)
    kept = total_ref[...] * same_ref[...]
    folded = jnp.dot(
        fold_ref[...], kept, precision=lax.Precision.HIGHEST, preferred_element_type=F32
    )
    sum_ref[...] = lax.dot_general(
        folded,
        fold_ref[...],
        (((1,), (1,)), ((), ())),
        precision=lax.Precision.HIGHEST,
        preferred_element_type=F32,
    )


def channel_lanes(plan, channel):
    group = channel // plan.group
    return group * 256 + (channel - group * plan.group) * plan.owned


def weight_copy(plan, adjoint, step, source, target, sem, index):
    part = pl.ds(index * step, step)
    place = (part,) if adjoint else (slice(None), part)
    return pltpu.make_async_copy(source.at[place], target.at[place], sem.at[index])


def mix_kernel(plan, adjoint, step, rows_ref, weight_hbm, x_ref, x_t_ref, *rest):
    if adjoint:
        sums_ref, modes_ref, out_ref, weight_ref, mixed_ref, weight_sem = rest
    else:
        modes_ref, out_ref, weight_ref, mixed_ref, weight_sem = rest
    steps = plan.channels // step
    copy = functools.partial(weight_copy, plan, adjoint, step, weight_hbm, weight_ref, weight_sem)
    for index in range(steps):
        copy(index).start()
    modes = dot(x_ref[...], rows_ref[...])
    for channel in range(plan.channels):
        lane = channel_lanes(plan, channel)
        for part in range(2):
            modes_ref[channel, part] = modes[
                part * KX : (part + 1) * KX, lane : lane + plan.owned
            ]

    def mix_one(index, carry):
        @pl.when(lax.rem(index, step) == 0)
        def _():
            copy(index // step).wait()

        real = jnp.zeros((KX, plan.owned), F32)
        imag = jnp.zeros((KX, plan.owned), F32)
        for channel in range(plan.channels):
            place = (index, channel) if adjoint else (channel, index)
            weight_real = weight_ref[place + (0,)].astype(F32)
            weight_imag = weight_ref[place + (1,)].astype(F32)
            mode_real = modes_ref[channel, 0]
            mode_imag = modes_ref[channel, 1]
            if adjoint:
                real += weight_real * mode_real + weight_imag * mode_imag
                imag += weight_real * mode_imag - weight_imag * mode_real
            else:
                real += weight_real * mode_real - weight_imag * mode_imag
                imag += weight_real * mode_imag + weight_imag * mode_real
        mixed_ref[index, 0] = real
        mixed_ref[index, 1] = imag
        return carry

    lax.fori_loop(0, plan.channels, mix_one, 0)
    for group in range(plan.groups):
        size = plan.group_size(group)
        halves = []
        for part in range(2):
            pieces = [mixed_ref[group * plan.group + index, part] for index in range(size)]
            spare = 256 - size * plan.owned
            if spare:
                pieces.append(jnp.zeros((KX, spare), F32))
            halves.append(jnp.concatenate(pieces, axis=1))
        columns = jnp.concatenate(halves, axis=0).astype(BF16)
        out_ref[:, group * 256 : (group + 1) * 256] = dot(x_t_ref[...], columns).astype(BF16)
    if adjoint:
        out_ref[:, plan.lanes :] = pack_sums(plan, sums_ref[...])


def weight_grad_kernel(block, channels, modes_ref, grads_ref, out_ref):
    for index in range(block):
        mode_real = modes_ref[index, 0]
        mode_imag = modes_ref[index, 1]
        for channel in range(channels):
            grad_real = grads_ref[channel, 0]
            grad_imag = grads_ref[channel, 1]
            out_ref[index, channel, 0] = grad_real * mode_real + grad_imag * mode_imag
            out_ref[index, channel, 1] = grad_imag * mode_real - grad_real * mode_imag


def whole(shape):
    return pl.BlockSpec(shape, lambda *_: (0,) * len(shape))


def params():
    return pltpu.CompilerParams(vmem_limit_bytes=VMEM_LIMIT)


def cost(flops, moved, transcendentals=0):
    return pl.CostEstimate(
        flops=int(flops), bytes_accessed=int(moved), transcendentals=int(transcendentals)
    )


def shards(devices, plume_state, out_cotangent, spectral_weight, pointwise_weight):
    slab, channels, width_y, width_t, width_z = plume_state.shape
    plan = Plan(slab, channels, width_y, width_z, devices)
    rows = plan.rows_yt
    chunk = 10 if channels % 10 == 0 else channels
    steps = slab * (channels // chunk)
    flat = (slab, channels, rows, width_z)
    state = plume_state.reshape(flat)
    cotangent = out_cotangent.reshape(flat)
    field_bytes = 2 * math.prod(flat)
    exchanged = (devices * slab * 2, plan.lanes)
    exchanged_back = (devices * slab * 2, plan.lanes + plan.extra)

    y_table = jnp.asarray(plan.y_table())
    y_table_t = jnp.asarray(np.ascontiguousarray(plan.y_table().T))
    depth = jnp.asarray(plan.depth_tables())
    depth_t = jnp.asarray(np.ascontiguousarray(plan.depth_tables().transpose(0, 2, 1)))
    order = jnp.asarray(plan.order())
    order_t = jnp.asarray(np.ascontiguousarray(plan.order().T))
    x_table = jnp.asarray(plan.x_table())
    x_table_t = jnp.asarray(np.ascontiguousarray(plan.x_table().T))

    hbm = pl.BlockSpec(memory_space=pl.ANY)
    vmem = pl.BlockSpec(memory_space=pltpu.VMEM)
    field_shape = jax.ShapeDtypeStruct(flat, BF16)
    field = pltpu.VMEM(flat, BF16)
    proj_shape = pltpu.VMEM((plan.kinds, slab * plan.kind_rows, channels * width_z), BF16)
    iz_shape = pltpu.VMEM((slab, plan.kinds * plan.kind_rows, channels * width_z), BF16)
    transform_flops = 2 * math.prod(flat) * 96 * 2
    mode_shape = (channels, 2, KX, plan.owned)

    def sems(count):
        return pltpu.SemaphoreType.DMA((count,))

    def exchange(values):
        blocks = values.reshape(devices, slab * 2, values.shape[1])
        moved = lax.all_to_all(blocks, "gx", split_axis=0, concat_axis=0, tiled=True)
        return moved.reshape(values.shape)

    def mix(adjoint, moved, *sums):
        step = 5 if channels % 5 == 0 else channels
        sent = exchanged_back if adjoint else exchanged
        return pl.pallas_call(
            functools.partial(mix_kernel, plan, adjoint, step),
            in_specs=[vmem, hbm, vmem, vmem] + [vmem] * len(sums),
            out_specs=[vmem, vmem],
            out_shape=[
                jax.ShapeDtypeStruct(mode_shape, F32),
                jax.ShapeDtypeStruct(sent, BF16),
            ],
            scratch_shapes=[
                pltpu.VMEM(spectral_weight.shape, BF16),
                pltpu.VMEM(mode_shape, F32),
                sems(channels // step),
            ],
            compiler_params=params(),
            cost_estimate=cost(8 * 864 * 400, 5e6),
            name="mix_back" if adjoint else "mix_modes",
        )(moved, spectral_weight, x_table, x_table_t, *sums)

    sent = pl.pallas_call(
        functools.partial(forward_kernel, plan, chunk),
        in_specs=[hbm, vmem, vmem, vmem],
        out_specs=vmem,
        out_shape=jax.ShapeDtypeStruct(exchanged, BF16),
        scratch_shapes=[field, proj_shape, sems(steps)],
        compiler_params=params(),
        cost_estimate=cost(transform_flops, field_bytes),
        name="forward_rows",
    )(state, y_table, depth, order)
    moved = exchange(sent)

    eye = jnp.eye(ROW_GROUP, dtype=BF16)
    spread = channels * ROW_GROUP

    def spread_weight(weight):
        return (weight[:, None, :, None] * eye[None, :, None, :]).reshape(spread, spread)

    tile = min(256, rows)
    row_steps = slab * (rows // tile)
    mixing_flops = 2 * math.prod(flat) * spread

    def point(weight, values, name):
        return pl.pallas_call(
            functools.partial(point_kernel, tile),
            in_specs=[vmem, hbm],
            out_specs=hbm,
            out_shape=field_shape,
            scratch_shapes=[field, field, sems(row_steps), sems(row_steps)],
            compiler_params=params(),
            cost_estimate=cost(mixing_flops, 2 * field_bytes),
            name=name,
        )(spread_weight(weight), values)

    point_state = point(pointwise_weight.T, state, "point_mix")

    modes, mixed_rows = mix(False, moved)
    restored = exchange(mixed_rows)

    grad_pre, grad_rows = pl.pallas_call(
        functools.partial(middle_kernel, plan, chunk),
        in_specs=[vmem, hbm, hbm] + [vmem] * 6,
        out_specs=[hbm, vmem],
        out_shape=[field_shape, jax.ShapeDtypeStruct(exchanged, BF16)],
        scratch_shapes=[field, field, field, iz_shape, proj_shape] + [sems(steps)] * 3,
        compiler_params=params(),
        cost_estimate=cost(2 * transform_flops, 3 * field_bytes, 2 * math.prod(flat)),
        name="activation_grad",
    )(restored, point_state, cotangent, y_table, y_table_t, depth, depth_t, order, order_t)

    grad_moved = exchange(grad_rows)

    same = np.kron(np.ones((channels, channels)), np.eye(ROW_GROUP)).astype(np.float32)
    fold = np.kron(np.eye(channels), np.ones((1, ROW_GROUP))).astype(np.float32)
    sums = pl.pallas_call(
        functools.partial(point_sum_kernel, tile),
        in_specs=[hbm, hbm, vmem, vmem],
        out_specs=vmem,
        out_shape=jax.ShapeDtypeStruct((channels, channels), F32),
        scratch_shapes=[field, field, pltpu.VMEM((spread, spread), F32)] + [sems(row_steps)] * 2,
        compiler_params=params(),
        cost_estimate=cost(mixing_flops, 2 * field_bytes),
        name="point_sum",
    )(state, grad_pre, jnp.asarray(same), jnp.asarray(fold))

    grad_modes, back_rows = mix(True, grad_moved, sums)
    back_moved = exchange(back_rows)

    later_grad, grad_modes = lax.optimization_barrier((grad_pre, grad_modes))
    point_back = point(pointwise_weight, later_grad, "point_back")

    grad_shape = (channels, channels, 2, KX, plan.owned)
    block = 5 if channels % 5 == 0 else 1
    spectral_grad = pl.pallas_call(
        functools.partial(weight_grad_kernel, block, channels),
        grid=(channels // block,),
        in_specs=[
            pl.BlockSpec((block,) + mode_shape[1:], lambda i: (i, 0, 0, 0)),
            whole(mode_shape),
        ],
        out_specs=pl.BlockSpec((block,) + grad_shape[1:], lambda i: (i, 0, 0, 0, 0)),
        out_shape=jax.ShapeDtypeStruct(grad_shape, F32),
        compiler_params=params(),
        cost_estimate=cost(6 * 864 * 400, 1e7),
        name="weight_grad",
    )(modes, grad_modes)

    scale = 1.0 / math.sqrt(plan.width_x * width_y * width_t * width_z)
    state_grad, pointwise_grad = pl.pallas_call(
        functools.partial(final_kernel, plan, chunk, scale),
        in_specs=[vmem, hbm, vmem, vmem, vmem],
        out_specs=[hbm, vmem],
        out_shape=[field_shape, jax.ShapeDtypeStruct((channels, channels), F32)],
        scratch_shapes=[field, field, iz_shape] + [sems(steps)] * 2,
        compiler_params=params(),
        cost_estimate=cost(transform_flops, 2 * field_bytes),
        name="state_grad",
    )(back_moved, point_back, y_table_t, depth_t, order_t)
    return (state_grad.reshape(plume_state.shape), spectral_grad, pointwise_grad)


def solution(mesh):
    placed = (
        P(("groups", "gx"), None, None, None, None),
        P(("groups", "gx"), None, None, None, None),
        P(None, None, None, None, "gx"),
        P(),
    )
    return jax.shard_map(
        functools.partial(shards, mesh.shape["gx"]),
        mesh=mesh,
        in_specs=placed,
        out_specs=(
            P(("groups", "gx"), None, None, None, None),
            P("groups", None, None, None, "gx"),
            P("groups", None),
        ),
        check_vma=False,
    )
```

```python
import functools
import math

import jax
import jax.numpy as jnp
import ml_dtypes
import numpy as np
from jax import lax
from jax.experimental import pallas as pl
from jax.experimental.pallas import tpu as pltpu
from jax.sharding import PartitionSpec as P

KX = 24
KY = 24
KZ = 24
NT = 2
ROW_GROUP = 16
BF16 = jnp.bfloat16
F32 = jnp.float32
VMEM_LIMIT = 56 * 1024 * 1024


def rounded(table):
    return np.asarray(table, np.float64).astype(np.float32).astype(ml_dtypes.bfloat16)


def wave_tables(cells, kept):
    frequency = np.arange(kept) - kept // 2
    angle = 2.0 * np.pi / cells * (frequency[:, None] * np.arange(cells)[None, :] % cells)
    return np.cos(angle) / math.sqrt(cells), np.sin(angle) / math.sqrt(cells)


def depth_table(cells, kept):
    column = np.arange(kept)
    half = kept // 2
    frequency = np.where(column < half, column, column - half + 1)
    angle = 2.0 * np.pi / cells * (np.arange(cells)[:, None] * frequency[None, :] % cells)
    wave = np.where(column[None, :] < half, np.cos(angle), np.sin(angle))
    return wave * math.sqrt(2.0 / cells) * math.sqrt(0.5)


class Plan:
    def __init__(self, slab, channels, width_y, width_z, devices):
        self.slab = slab
        self.channels = channels
        self.width_y = width_y
        self.width_z = width_z
        self.devices = devices
        self.width_x = slab * devices
        self.pairs = KY * NT
        self.owned = self.pairs * KZ // devices
        self.kinds = 3
        self.owners = self.kinds * KZ // self.owned
        self.periods = self.pairs // self.kinds
        self.unit = math.gcd(self.owned, KZ)
        self.units = KZ // self.unit
        self.owned_units = self.owned // self.unit
        self.unit_lanes = 128 * -(-channels * self.unit // 128)
        self.lanes = self.unit_lanes * self.owned_units
        self.rows_yt = width_y * NT
        self.kind_rows = self.periods * 2
        sums = 2 * channels * -(-channels // (2 * slab))
        self.extra = 128 * -(-sums // 128)

    def y_table(self):
        cosine, sine = wave_tables(self.width_y, KY)
        both = np.stack([cosine, -sine])
        table = np.zeros((self.kinds, self.periods, 2, self.width_y, NT))
        for kind in range(self.kinds):
            for period in range(self.periods):
                pair = self.kinds * period + kind
                for time in range(NT):
                    sign = -1.0 if (time % 2 and pair % 2) else 1.0
                    table[kind, period, :, :, time] = sign * both[:, pair // 2]
        return rounded(table.reshape(self.kinds * self.kind_rows, self.rows_yt))

    def depth_table(self):
        values = depth_table(self.width_z, KZ)
        table = np.zeros((self.channels, self.width_z, self.units, self.unit_lanes))
        for channel in range(self.channels):
            start = channel * self.unit
            table[channel, :, :, start : start + self.unit] = values.reshape(
                self.width_z, self.units, self.unit
            )
        return rounded(
            table.reshape(self.channels * self.width_z, self.units * self.unit_lanes)
        )

    def order(self):
        total = self.devices * self.slab * 2
        source = np.arange(total).reshape(self.owners, self.slab, self.periods, 2)
        source = source.transpose(2, 0, 1, 3).reshape(total)
        table = np.zeros((total, total))
        table[np.arange(total), source] = 1.0
        return rounded(table)

    def x_table(self):
        cosine, sine = wave_tables(self.width_x, KX)
        table = np.zeros((2, KX, self.width_x, 2))
        table[0, :, :, 0] = cosine
        table[0, :, :, 1] = sine
        table[1, :, :, 1] = cosine
        table[1, :, :, 0] = -sine
        return rounded(table.reshape(2 * KX, self.width_x * 2))


def dot(left, right):
    return jnp.dot(left, right, preferred_element_type=F32)


def project_depth(plan, proj_ref, depth_ref, order_ref, out_ref):
    rows = plan.slab * plan.kind_rows
    lanes = plan.unit_lanes
    parts = [
        dot(proj_ref[kind], depth_ref[...]).astype(BF16) for kind in range(plan.kinds)
    ]
    owners = []
    for owner in range(plan.owners):
        pieces = []
        for index in range(plan.owned_units):
            kind, unit = divmod(owner * plan.owned_units + index, plan.units)
            pieces.append(parts[kind][:rows, unit * lanes : (unit + 1) * lanes])
        owners.append(jnp.concatenate(pieces, axis=1))
    joined = jnp.concatenate(owners, axis=0)
    out_ref[...] = dot(order_ref[...], joined).astype(BF16)


def restore_depth(plan, scale, rows_ref, depth_t_ref, order_t_ref, iz_ref):
    block = plan.slab * plan.kind_rows
    lanes = plan.unit_lanes
    rows = dot(order_t_ref[...], rows_ref[:, : plan.lanes]).astype(BF16)
    kinds = []
    for kind in range(plan.kinds):
        pieces = []
        for unit in range(plan.units):
            owner, index = divmod(kind * plan.units + unit, plan.owned_units)
            pieces.append(
                rows[owner * block : (owner + 1) * block, index * lanes : (index + 1) * lanes]
            )
        kinds.append(jnp.concatenate(pieces, axis=1))
    joined = jnp.concatenate(kinds, axis=0)
    total = depth_t_ref.shape[1]
    width = min(total, 512)
    for start in range(0, total, width):
        stop = min(total, start + width)
        values = dot(joined, depth_t_ref[:, start:stop])
        if scale != 1.0:
            values = values * scale
        values = values.astype(BF16)
        for kind in range(plan.kinds):
            for row in range(plan.slab):
                first = (kind * plan.slab + row) * plan.kind_rows
                iz_ref[
                    row, kind * plan.kind_rows : (kind + 1) * plan.kind_rows, start:stop
                ] = values[first : first + plan.kind_rows]


def store_projection(plan, proj_ref, row, lane, values):
    for kind in range(plan.kinds):
        proj_ref[
            kind,
            pl.ds(pl.multiple_of(row * plan.kind_rows, plan.kind_rows), plan.kind_rows),
            pl.ds(lane, values.shape[1]),
        ] = values[kind * plan.kind_rows : (kind + 1) * plan.kind_rows]


def chunk_copy(source, target, sem, chunk, index):
    parts = source.shape[1] // chunk
    place = (index // parts, pl.ds(lax.rem(index, parts) * chunk, chunk))
    return pltpu.make_async_copy(source.at[place], target.at[place], sem.at[index])


def chunk_place(plan, chunk, index):
    parts = plan.channels // chunk
    return index // parts, lax.rem(index, parts) * chunk


def pair_lane(plan, channel):
    return pl.multiple_of(channel * plan.width_z, 2 * plan.width_z)


def whole_copies(pairs, sem):
    return [
        pltpu.make_async_copy(source, target, sem.at[index])
        for index, (source, target) in enumerate(pairs)
    ]


def forward_kernel(
    plan,
    chunk,
    u_hbm,
    depth_hbm,
    y_ref,
    order_ref,
    out_ref,
    u_ref,
    depth_ref,
    proj_ref,
    u_sem,
    table_sem,
):
    steps = plan.slab * plan.channels // chunk
    for index in range(steps):
        chunk_copy(u_hbm, u_ref, u_sem, chunk, index).start()
    (table,) = whole_copies([(depth_hbm, depth_ref)], table_sem)
    table.start()

    def step(index, carry):
        chunk_copy(u_hbm, u_ref, u_sem, chunk, index).wait()
        row, first = chunk_place(plan, chunk, index)
        for pair in range(chunk // 2):
            channel = first + 2 * pair
            values = jnp.concatenate([u_ref[row, channel], u_ref[row, channel + 1]], axis=1)
            projected = dot(y_ref[...], values).astype(BF16)
            store_projection(plan, proj_ref, row, pair_lane(plan, channel), projected)
        return carry

    lax.fori_loop(0, steps, step, 0)
    table.wait()
    project_depth(plan, proj_ref, depth_ref, order_ref, out_ref)


def twice_slope(scaled):
    shift = math.log2(2.0 / math.sqrt(math.pi))
    density = jnp.exp2(scaled * (scaled * -math.log2(math.e)) + shift)
    return (lax.erf(scaled) + 1.0) + scaled * density


def middle_kernel(
    plan,
    chunk,
    tile,
    rows_ref,
    point_hbm,
    cot_hbm,
    depth_hbm,
    depth_t_hbm,
    y_ref,
    y_t_ref,
    order_ref,
    order_t_ref,
    grad_hbm,
    out_ref,
    point_ref,
    cot_ref,
    grad_ref,
    depth_ref,
    depth_t_ref,
    iz_ref,
    proj_ref,
    point_sem,
    cot_sem,
    grad_sem,
    table_sem,
):
    z = plan.width_z
    parts = plan.channels // chunk
    steps = plan.slab * parts
    depth_copy, depth_t_copy = whole_copies(
        [(depth_hbm, depth_ref), (depth_t_hbm, depth_t_ref)], table_sem
    )
    depth_t_copy.start()
    for index in range(steps):
        chunk_copy(point_hbm, point_ref, point_sem, chunk, index).start()
        chunk_copy(cot_hbm, cot_ref, cot_sem, chunk, index).start()
    depth_copy.start()
    depth_t_copy.wait()
    restore_depth(plan, math.sqrt(0.5), rows_ref, depth_t_ref, order_t_ref, iz_ref)
    tiles = plan.rows_yt // tile

    def step(row, carry):
        def project(channel, start, stop):
            values = jnp.concatenate(
                [grad_ref[row, channel, start:stop], grad_ref[row, channel + 1, start:stop]],
                axis=1,
            )
            return dot(y_ref[:, start:stop], values)

        def store(channel, values):
            store_projection(plan, proj_ref, row, channel * z, values.astype(BF16))

        half_rows = plan.rows_yt // 2
        for channel in range(0, plan.channels, 2):
            if channel % chunk == 0:
                index = row * parts + channel // chunk
                chunk_copy(point_hbm, point_ref, point_sem, chunk, index).wait()
                chunk_copy(cot_hbm, cot_ref, cot_sem, chunk, index).wait()
            coefficients = iz_ref[row, :, channel * z : (channel + 2) * z]
            projected = None
            for place in range(tiles):
                span = slice(place * tile, (place + 1) * tile)
                spectral = dot(y_t_ref[span], coefficients)
                for half in range(2):
                    scaled = spectral[:, half * z : (half + 1) * z]
                    scaled = scaled + point_ref[row, channel + half, span].astype(F32)
                    grad = cot_ref[row, channel + half, span].astype(F32) * twice_slope(scaled)
                    grad_ref[row, channel + half, span] = grad.astype(BF16)
                if channel and place == tiles // 2 - 1:
                    projected = project(channel - 2, 0, half_rows)
            if channel:
                projected = projected + project(channel - 2, half_rows, 2 * half_rows)
                store(channel - 2, projected)
            if (channel + 2) % chunk == 0:
                index = row * parts + channel // chunk
                chunk_copy(grad_ref, grad_hbm, grad_sem, chunk, index).start()
        store(plan.channels - 2, project(plan.channels - 2, 0, plan.rows_yt))
        return carry

    lax.fori_loop(0, plan.slab, step, 0)
    depth_copy.wait()
    project_depth(plan, proj_ref, depth_ref, order_ref, out_ref)
    for index in range(steps):
        chunk_copy(grad_ref, grad_hbm, grad_sem, chunk, index).wait()


def final_kernel(
    plan,
    chunk,
    tile,
    scale,
    rows_ref,
    point_hbm,
    depth_t_hbm,
    y_t_ref,
    order_t_ref,
    out_hbm,
    sum_ref,
    point_ref,
    out_ref,
    depth_t_ref,
    iz_ref,
    point_sem,
    out_sem,
    table_sem,
):
    z = plan.width_z
    steps = plan.slab * plan.channels // chunk
    (table,) = whole_copies([(depth_t_hbm, depth_t_ref)], table_sem)
    table.start()
    for index in range(steps):
        chunk_copy(point_hbm, point_ref, point_sem, chunk, index).start()
    sum_ref[...] = unpack_sums(plan, rows_ref) * scale
    table.wait()
    restore_depth(plan, 1.0, rows_ref, depth_t_ref, order_t_ref, iz_ref)

    def step(index, carry):
        chunk_copy(point_hbm, point_ref, point_sem, chunk, index).wait()
        row, first = chunk_place(plan, chunk, index)
        for pair in range(chunk // 2):
            channel = first + 2 * pair
            coefficients = iz_ref[row, :, pl.ds(pair_lane(plan, channel), 2 * z)]
            for start in range(0, plan.rows_yt, tile):
                span = slice(start, start + tile)
                spectral = dot(y_t_ref[span], coefficients)
                for half in range(2):
                    total = spectral[:, half * z : (half + 1) * z]
                    total = total + point_ref[row, channel + half, span].astype(F32)
                    out_ref[row, channel + half, span] = total.astype(BF16)
        chunk_copy(out_ref, out_hbm, out_sem, chunk, index).start()
        return carry

    lax.fori_loop(0, steps, step, 0)
    for index in range(steps):
        chunk_copy(out_ref, out_hbm, out_sem, chunk, index).wait()


def pack_rows(plan):
    return 2 * plan.slab


def pack_sums(plan, sums):
    rows = pack_rows(plan)
    count = -(-plan.channels // rows)
    high = sums.astype(BF16)
    low = (sums - high.astype(F32)).astype(BF16)
    pieces = []
    for part in (high.astype(F32), low.astype(F32)):
        spare = count * rows - plan.channels
        if spare:
            part = jnp.concatenate([part, jnp.zeros((spare, plan.channels), F32)], axis=0)
        pieces += [part[index * rows : (index + 1) * rows] for index in range(count)]
    used = 2 * count * plan.channels
    pieces.append(jnp.zeros((rows, plan.extra - used), F32))
    block = jnp.concatenate(pieces, axis=1)
    return jnp.concatenate([block] * plan.devices, axis=0).astype(BF16)


def unpack_sums(plan, rows_ref):
    rows = pack_rows(plan)
    count = -(-plan.channels // rows)
    block = jnp.zeros((rows, plan.extra), F32)
    values = rows_ref[:, plan.lanes : plan.lanes + plan.extra].astype(F32)
    for device in range(plan.devices):
        block = block + values[device * rows : (device + 1) * rows]
    width = plan.channels
    parts = []
    for index in range(count):
        high = block[:, index * width : (index + 1) * width]
        low = block[:, (count + index) * width : (count + index + 1) * width]
        parts.append(high + low)
    return jnp.concatenate(parts, axis=0)[: plan.channels]


def row_copy(source, target, sem, tile, index):
    parts = source.shape[2] // tile
    place = (index // parts, slice(None), pl.ds(lax.rem(index, parts) * tile, tile))
    return pltpu.make_async_copy(source.at[place], target.at[place], sem.at[index])


def row_block(ref, row, start, count):
    channels, z = ref.shape[1], ref.shape[3]
    parts = [
        ref[row, :, pl.ds(start + index * ROW_GROUP, ROW_GROUP), :].reshape(
            channels * ROW_GROUP, z
        )
        for index in range(count)
    ]
    return jnp.concatenate(parts, axis=1)


def point_kernel(
    tile,
    side,
    scale,
    weight_ref,
    same_ref,
    fold_ref,
    fold_t_ref,
    u_hbm,
    out_hbm,
    u_ref,
    out_ref,
    spread_ref,
    u_sem,
    out_sem,
):
    channels, rows, z = u_hbm.shape[1:]
    parts = rows // tile
    steps = u_hbm.shape[0] * parts
    for index in range(steps):
        row_copy(u_hbm, u_ref, u_sem, tile, index).start()
    tall = lax.dot_general(
        fold_t_ref[...],
        weight_ref[...],
        (((1,), (side,)), ((), ())),
        preferred_element_type=F32,
    ).astype(BF16)
    spread_ref[...] = (dot(tall, fold_ref[...]) * same_ref[...]).astype(BF16)

    def step(index, carry):
        row_copy(u_hbm, u_ref, u_sem, tile, index).wait()
        row = index // parts
        base = pl.multiple_of(lax.rem(index, parts) * tile, tile)
        for start in range(0, tile, 2 * ROW_GROUP):
            mixed = dot(spread_ref[...], row_block(u_ref, row, base + start, 2)) * scale
            mixed = mixed.astype(BF16)
            for half in range(2):
                out_ref[row, :, pl.ds(base + start + half * ROW_GROUP, ROW_GROUP), :] = mixed[
                    :, half * z : (half + 1) * z
                ].reshape(channels, ROW_GROUP, z)
        row_copy(out_ref, out_hbm, out_sem, tile, index).start()
        return carry

    lax.fori_loop(0, steps, step, 0)
    for index in range(steps):
        row_copy(out_ref, out_hbm, out_sem, tile, index).wait()


def point_sum_kernel(
    tile, u_hbm, g_hbm, same_ref, fold_ref, sum_ref, u_ref, g_ref, total_ref, u_sem, g_sem
):
    parts = u_hbm.shape[2] // tile
    steps = u_hbm.shape[0] * parts
    for index in range(steps):
        row_copy(u_hbm, u_ref, u_sem, tile, index).start()
        row_copy(g_hbm, g_ref, g_sem, tile, index).start()
    total_ref[...] = jnp.zeros_like(total_ref)

    def step(index, carry):
        row_copy(u_hbm, u_ref, u_sem, tile, index).wait()
        row_copy(g_hbm, g_ref, g_sem, tile, index).wait()
        row = index // parts
        base = pl.multiple_of(lax.rem(index, parts) * tile, tile)
        for start in range(0, tile, 8 * ROW_GROUP):
            total_ref[...] += lax.dot_general(
                row_block(u_ref, row, base + start, 8),
                row_block(g_ref, row, base + start, 8),
                (((1,), (1,)), ((), ())),
                preferred_element_type=F32,
            )
        return carry

    lax.fori_loop(0, steps, step, 0)
    kept = total_ref[...] * same_ref[...]
    folded = jnp.dot(
        fold_ref[...], kept, precision=lax.Precision.HIGHEST, preferred_element_type=F32
    )
    sum_ref[...] = lax.dot_general(
        folded,
        fold_ref[...],
        (((1,), (1,)), ((), ())),
        precision=lax.Precision.HIGHEST,
        preferred_element_type=F32,
    )


def weight_copy(plan, adjoint, step, source, target, sem, index):
    part = pl.ds(index * step, step)
    place = (part,) if adjoint else (slice(None), part)
    return pltpu.make_async_copy(source.at[place], target.at[place], sem.at[index])


def mix_kernel(plan, adjoint, step, rows_ref, weight_hbm, x_ref, x_t_ref, *rest):
    if adjoint:
        sums_ref, modes_ref, out_ref, weight_ref, mixed_ref, weight_sem = rest
    else:
        modes_ref, out_ref, weight_ref, mixed_ref, weight_sem = rest
    steps = plan.channels // step
    copy = functools.partial(weight_copy, plan, adjoint, step, weight_hbm, weight_ref, weight_sem)
    for index in range(steps):
        copy(index).start()
    modes = dot(x_ref[...], rows_ref[...])
    for channel in range(plan.channels):
        pieces = []
        for index in range(plan.owned_units):
            lane = index * plan.unit_lanes + channel * plan.unit
            pieces.append(modes[:, lane : lane + plan.unit])
        joined = jnp.concatenate(pieces, axis=1)
        for part in range(2):
            modes_ref[channel, part] = joined[part * KX : (part + 1) * KX]

    def mix_one(index, carry):
        @pl.when(lax.rem(index, step) == 0)
        def _():
            copy(index // step).wait()

        real = jnp.zeros((KX, plan.owned), F32)
        imag = jnp.zeros((KX, plan.owned), F32)
        for channel in range(plan.channels):
            place = (index, channel) if adjoint else (channel, index)
            weight_real = weight_ref[place + (0,)].astype(F32)
            weight_imag = weight_ref[place + (1,)].astype(F32)
            mode_real = modes_ref[channel, 0]
            mode_imag = modes_ref[channel, 1]
            if adjoint:
                real += weight_real * mode_real + weight_imag * mode_imag
                imag += weight_real * mode_imag - weight_imag * mode_real
            else:
                real += weight_real * mode_real - weight_imag * mode_imag
                imag += weight_real * mode_imag + weight_imag * mode_real
        mixed_ref[index, 0] = real
        mixed_ref[index, 1] = imag
        return carry

    lax.fori_loop(0, plan.channels, mix_one, 0)
    for index in range(plan.owned_units):
        span = slice(index * plan.unit, (index + 1) * plan.unit)
        halves = []
        for part in range(2):
            pieces = [mixed_ref[channel, part][:, span] for channel in range(plan.channels)]
            spare = plan.unit_lanes - plan.channels * plan.unit
            if spare:
                pieces.append(jnp.zeros((KX, spare), F32))
            halves.append(jnp.concatenate(pieces, axis=1))
        columns = jnp.concatenate(halves, axis=0).astype(BF16)
        lanes = slice(index * plan.unit_lanes, (index + 1) * plan.unit_lanes)
        out_ref[:, lanes] = dot(x_t_ref[...], columns).astype(BF16)
    if adjoint:
        out_ref[:, plan.lanes :] = pack_sums(plan, sums_ref[...])


def weight_grad_kernel(block, channels, modes_ref, grads_ref, out_ref):
    for index in range(block):
        mode_real = modes_ref[index, 0]
        mode_imag = modes_ref[index, 1]
        for channel in range(channels):
            grad_real = grads_ref[channel, 0]
            grad_imag = grads_ref[channel, 1]
            out_ref[index, channel, 0] = grad_real * mode_real + grad_imag * mode_imag
            out_ref[index, channel, 1] = grad_imag * mode_real - grad_real * mode_imag


def whole(shape):
    return pl.BlockSpec(shape, lambda *_: (0,) * len(shape))


def params():
    return pltpu.CompilerParams(vmem_limit_bytes=VMEM_LIMIT)


def cost(flops, moved, transcendentals=0):
    return pl.CostEstimate(
        flops=int(flops), bytes_accessed=int(moved), transcendentals=int(transcendentals)
    )


def shards(devices, plume_state, out_cotangent, spectral_weight, pointwise_weight):
    slab, channels, width_y, width_t, width_z = plume_state.shape
    plan = Plan(slab, channels, width_y, width_z, devices)
    rows = plan.rows_yt
    chunk = 10 if channels % 10 == 0 else channels
    steps = slab * (channels // chunk)
    flat = (slab, channels, rows, width_z)
    state = plume_state.reshape(flat)
    cotangent = out_cotangent.reshape(flat)
    field_bytes = 2 * math.prod(flat)
    exchanged = (devices * slab * 2, plan.lanes)
    exchanged_back = (devices * slab * 2, plan.lanes + plan.extra)

    y_table = jnp.asarray(plan.y_table())
    y_table_t = jnp.asarray(np.ascontiguousarray(plan.y_table().T))
    depth = jnp.asarray(plan.depth_table())
    depth_t = jnp.asarray(np.ascontiguousarray(plan.depth_table().T))
    order = jnp.asarray(plan.order())
    order_t = jnp.asarray(np.ascontiguousarray(plan.order().T))
    x_table = jnp.asarray(plan.x_table())
    x_table_half = jnp.asarray((plan.x_table().astype(np.float32) * 0.5).astype(ml_dtypes.bfloat16))
    x_table_t = jnp.asarray(np.ascontiguousarray(plan.x_table().T))

    hbm = pl.BlockSpec(memory_space=pl.ANY)
    vmem = pl.BlockSpec(memory_space=pltpu.VMEM)
    field_shape = jax.ShapeDtypeStruct(flat, BF16)
    field = pltpu.VMEM(flat, BF16)
    proj_shape = pltpu.VMEM((plan.kinds, slab * plan.kind_rows, channels * width_z), BF16)
    iz_shape = pltpu.VMEM((slab, plan.kinds * plan.kind_rows, channels * width_z), BF16)
    depth_shape = pltpu.VMEM(depth.shape, BF16)
    depth_t_shape = pltpu.VMEM(depth_t.shape, BF16)
    transform_flops = 2 * math.prod(flat) * 96 * 2
    mode_shape = (channels, 2, KX, plan.owned)

    def sems(count):
        return pltpu.SemaphoreType.DMA((count,))

    def exchange(values):
        blocks = values.reshape(devices, slab * 2, values.shape[1])
        moved = lax.all_to_all(blocks, "gx", split_axis=0, concat_axis=0, tiled=True)
        return moved.reshape(values.shape)

    def mix(adjoint, moved, *sums):
        step = 5 if channels % 5 == 0 else channels
        sent = exchanged_back if adjoint else exchanged
        return pl.pallas_call(
            functools.partial(mix_kernel, plan, adjoint, step),
            in_specs=[vmem, hbm, vmem, vmem] + [vmem] * len(sums),
            out_specs=[vmem, vmem],
            out_shape=[
                jax.ShapeDtypeStruct(mode_shape, F32),
                jax.ShapeDtypeStruct(sent, BF16),
            ],
            scratch_shapes=[
                pltpu.VMEM(spectral_weight.shape, BF16),
                pltpu.VMEM(mode_shape, F32),
                sems(channels // step),
            ],
            compiler_params=params(),
            cost_estimate=cost(8 * 864 * 400, 5e6),
            name="mix_back" if adjoint else "mix_modes",
        )(moved, spectral_weight, x_table_half if adjoint else x_table, x_table_t, *sums)

    sent = pl.pallas_call(
        functools.partial(forward_kernel, plan, chunk),
        in_specs=[hbm, hbm, vmem, vmem],
        out_specs=vmem,
        out_shape=jax.ShapeDtypeStruct(exchanged, BF16),
        scratch_shapes=[field, depth_shape, proj_shape, sems(steps), sems(1)],
        compiler_params=params(),
        cost_estimate=cost(transform_flops, field_bytes),
        name="forward_rows",
    )(state, depth, y_table, order)
    moved = exchange(sent)

    spread = channels * ROW_GROUP
    same = np.kron(np.ones((channels, channels)), np.eye(ROW_GROUP)).astype(np.float32)
    same = jnp.asarray(same)
    fold_rows = np.kron(np.eye(channels), np.ones((1, ROW_GROUP)))
    fold = jnp.asarray(fold_rows.astype(np.float32))
    fold_b = jnp.asarray(rounded(fold_rows))
    fold_b_t = jnp.asarray(rounded(np.ascontiguousarray(fold_rows.T)))
    tile = min(256, rows)
    row_steps = slab * (rows // tile)
    mixing_flops = 2 * math.prod(flat) * spread

    def point(side, scale, values, name):
        return pl.pallas_call(
            functools.partial(point_kernel, tile, side, scale),
            in_specs=[vmem] * 4 + [hbm],
            out_specs=hbm,
            out_shape=field_shape,
            scratch_shapes=[field, field, pltpu.VMEM((spread, spread), BF16)]
            + [sems(row_steps)] * 2,
            compiler_params=params(),
            cost_estimate=cost(mixing_flops, 2 * field_bytes),
            name=name,
        )(pointwise_weight, same, fold_b, fold_b_t, values)

    point_state = point(1, math.sqrt(0.5), state, "point_mix")

    modes, mixed_rows = mix(False, moved)
    restored = exchange(mixed_rows)

    slope_tile = min(128, rows)
    grad_pre, grad_rows = pl.pallas_call(
        functools.partial(middle_kernel, plan, chunk, slope_tile),
        in_specs=[vmem] + [hbm] * 4 + [vmem] * 4,
        out_specs=[hbm, vmem],
        out_shape=[field_shape, jax.ShapeDtypeStruct(exchanged, BF16)],
        scratch_shapes=[field, field, field, depth_shape, depth_t_shape, iz_shape, proj_shape]
        + [sems(steps)] * 3
        + [sems(2)],
        compiler_params=params(),
        cost_estimate=cost(2 * transform_flops, 3 * field_bytes, 2 * math.prod(flat)),
        name="activation_grad",
    )(restored, point_state, cotangent, depth, depth_t, y_table, y_table_t, order, order_t)

    grad_moved = exchange(grad_rows)

    sums = pl.pallas_call(
        functools.partial(point_sum_kernel, tile),
        in_specs=[hbm, hbm, vmem, vmem],
        out_specs=vmem,
        out_shape=jax.ShapeDtypeStruct((channels, channels), F32),
        scratch_shapes=[field, field, pltpu.VMEM((spread, spread), F32)] + [sems(row_steps)] * 2,
        compiler_params=params(),
        cost_estimate=cost(mixing_flops, 2 * field_bytes),
        name="point_sum",
    )(state, grad_pre, same, fold)

    grad_modes, back_rows = mix(True, grad_moved, sums)
    back_moved = exchange(back_rows)

    later_grad, grad_modes = lax.optimization_barrier((grad_pre, grad_modes))
    point_back = point(0, 0.5, later_grad, "point_back")

    grad_shape = (channels, channels, 2, KX, plan.owned)
    block = 5 if channels % 5 == 0 else 1
    spectral_grad = pl.pallas_call(
        functools.partial(weight_grad_kernel, block, channels),
        grid=(channels // block,),
        in_specs=[
            pl.BlockSpec((block,) + mode_shape[1:], lambda i: (i, 0, 0, 0)),
            whole(mode_shape),
        ],
        out_specs=pl.BlockSpec((block,) + grad_shape[1:], lambda i: (i, 0, 0, 0, 0)),
        out_shape=jax.ShapeDtypeStruct(grad_shape, F32),
        compiler_params=params(),
        cost_estimate=cost(6 * 864 * 400, 1e7),
        name="weight_grad",
    )(modes, grad_modes)

    scale = 0.5 / math.sqrt(plan.width_x * width_y * width_t * width_z)
    state_grad, pointwise_grad = pl.pallas_call(
        functools.partial(final_kernel, plan, chunk, slope_tile, scale),
        in_specs=[vmem, hbm, hbm, vmem, vmem],
        out_specs=[hbm, vmem],
        out_shape=[field_shape, jax.ShapeDtypeStruct((channels, channels), F32)],
        scratch_shapes=[field, field, depth_t_shape, iz_shape] + [sems(steps)] * 2 + [sems(1)],
        compiler_params=params(),
        cost_estimate=cost(transform_flops, 2 * field_bytes),
        name="state_grad",
    )(back_moved, point_back, depth_t, y_table_t, order_t)
    return (state_grad.reshape(plume_state.shape), spectral_grad, pointwise_grad)


def solution(mesh):
    placed = (
        P(("groups", "gx"), None, None, None, None),
        P(("groups", "gx"), None, None, None, None),
        P(None, None, None, None, "gx"),
        P(),
    )
    return jax.shard_map(
        functools.partial(shards, mesh.shape["gx"]),
        mesh=mesh,
        in_specs=placed,
        out_specs=(
            P(("groups", "gx"), None, None, None, None),
            P("groups", None, None, None, "gx"),
            P("groups", None),
        ),
        check_vma=False,
    )
```

```python
import functools
import math

import jax
import jax.numpy as jnp
import ml_dtypes
import numpy as np
from jax import lax
from jax.experimental import pallas as pl
from jax.experimental.pallas import tpu as pltpu
from jax.sharding import PartitionSpec as P

KX = 24
KY = 24
KZ = 24
NT = 2
ROW_GROUP = 8
TILE_ROWS = 16
BF16 = jnp.bfloat16
F32 = jnp.float32
FIELD_MIB = 51
ONE_STREAM = 6
TWO_STREAMS = 3
WEIGHT_STREAM = 8
MIB = 1024 * 1024


def rounded(table):
    return np.asarray(table, np.float64).astype(np.float32).astype(ml_dtypes.bfloat16)


def wave_tables(cells, kept):
    frequency = np.arange(kept) - kept // 2
    angle = 2.0 * np.pi / cells * (frequency[:, None] * np.arange(cells)[None, :] % cells)
    return np.cos(angle) / math.sqrt(cells), np.sin(angle) / math.sqrt(cells)


def depth_table(cells, kept):
    column = np.arange(kept)
    half = kept // 2
    frequency = np.where(column < half, column, column - half + 1)
    angle = 2.0 * np.pi / cells * (np.arange(cells)[:, None] * frequency[None, :] % cells)
    wave = np.where(column[None, :] < half, np.cos(angle), np.sin(angle))
    return wave * math.sqrt(2.0 / cells) * math.sqrt(0.5)


class Plan:
    def __init__(self, slab, channels, width_y, width_z, devices):
        self.slab = slab
        self.channels = channels
        self.width_y = width_y
        self.width_z = width_z
        self.devices = devices
        self.width_x = slab * devices
        self.pairs = KY * NT
        self.owned = self.pairs * KZ // devices
        self.kinds = 3
        self.owners = self.kinds * KZ // self.owned
        self.periods = self.pairs // self.kinds
        self.unit = math.gcd(self.owned, KZ)
        self.units = KZ // self.unit
        self.owned_units = self.owned // self.unit
        self.unit_lanes = 128 * -(-channels * self.unit // 128)
        self.lanes = self.unit_lanes * self.owned_units
        self.rows_yt = width_y * NT
        self.kind_rows = self.periods * 2
        sums = 2 * channels * -(-channels // (2 * slab))
        self.extra = 128 * -(-sums // 128)

    def y_table(self):
        cosine, sine = wave_tables(self.width_y, KY)
        both = np.stack([cosine, -sine])
        table = np.zeros((self.kinds, self.periods, 2, self.width_y, NT))
        for kind in range(self.kinds):
            for period in range(self.periods):
                pair = self.kinds * period + kind
                for time in range(NT):
                    sign = -1.0 if (time % 2 and pair % 2) else 1.0
                    table[kind, period, :, :, time] = sign * both[:, pair // 2]
        return rounded(table.reshape(self.kinds * self.kind_rows, self.rows_yt))

    def depth_base(self):
        values = depth_table(self.width_z, KZ).reshape(self.width_z, self.units, self.unit)
        table = np.zeros((self.width_z, self.units, self.unit_lanes))
        used = self.channels * self.unit
        table[:, :, :used] = np.tile(values, (1, 1, self.channels))
        return rounded(table.reshape(self.width_z, self.units * self.unit_lanes))

    def order(self):
        total = self.devices * self.slab * 2
        source = np.arange(total).reshape(self.owners, self.slab, self.periods, 2)
        source = source.transpose(2, 0, 1, 3).reshape(total)
        table = np.zeros((total, total))
        table[np.arange(total), source] = 1.0
        return rounded(table)

    def x_table(self):
        cosine, sine = wave_tables(self.width_x, KX)
        table = np.zeros((2, KX, self.width_x, 2))
        table[0, :, :, 0] = cosine
        table[0, :, :, 1] = sine
        table[1, :, :, 1] = cosine
        table[1, :, :, 0] = -sine
        return rounded(table.reshape(2 * KX, self.width_x * 2))


def dot(left, right):
    return jnp.dot(left, right, preferred_element_type=F32)


def channel_place(plan, axis):
    count = plan.units * plan.unit_lanes
    shape = (plan.width_z, count) if axis == 1 else (count, plan.width_z)
    return lax.rem(lax.broadcasted_iota(jnp.int32, shape, axis), plan.unit_lanes)


def spread_depth(plan, base_ref, depth_ref, axis):
    place = channel_place(plan, axis)
    base = base_ref[...].astype(F32)
    for channel in range(plan.channels):
        start = channel * plan.unit
        own = (place >= start) & (place < start + plan.unit)
        block = jnp.where(own, base, 0.0).astype(BF16)
        span = slice(channel * plan.width_z, (channel + 1) * plan.width_z)
        if axis == 1:
            depth_ref[span, :] = block
        else:
            depth_ref[:, span] = block


def project_depth(plan, proj_ref, depth_ref, order_ref, out_ref):
    rows = plan.slab * plan.kind_rows
    lanes = plan.unit_lanes
    flat = proj_ref[...].reshape(plan.kinds * rows, plan.channels * plan.width_z)
    parts = dot(flat, depth_ref[...]).astype(BF16)
    owners = []
    for owner in range(plan.owners):
        pieces = []
        for index in range(plan.owned_units):
            kind, unit = divmod(owner * plan.owned_units + index, plan.units)
            pieces.append(
                parts[kind * rows : (kind + 1) * rows, unit * lanes : (unit + 1) * lanes]
            )
        owners.append(jnp.concatenate(pieces, axis=1))
    joined = jnp.concatenate(owners, axis=0)
    out_ref[...] = dot(order_ref[...], joined).astype(BF16)


def restore_depth(plan, scale, rows_ref, depth_t_ref, order_t_ref, iz_ref):
    block = plan.slab * plan.kind_rows
    lanes = plan.unit_lanes
    rows = dot(order_t_ref[...], rows_ref[:, : plan.lanes]).astype(BF16)
    kinds = []
    for kind in range(plan.kinds):
        pieces = []
        for unit in range(plan.units):
            owner, index = divmod(kind * plan.units + unit, plan.owned_units)
            pieces.append(
                rows[owner * block : (owner + 1) * block, index * lanes : (index + 1) * lanes]
            )
        kinds.append(jnp.concatenate(pieces, axis=1))
    joined = jnp.concatenate(kinds, axis=0)
    total = depth_t_ref.shape[1]
    width = min(total, 512)
    for start in range(0, total, width):
        stop = min(total, start + width)
        values = dot(joined, depth_t_ref[:, start:stop])
        if scale != 1.0:
            values = values * scale
        values = values.astype(BF16)
        for kind in range(plan.kinds):
            for row in range(plan.slab):
                first = (kind * plan.slab + row) * plan.kind_rows
                iz_ref[
                    row, kind * plan.kind_rows : (kind + 1) * plan.kind_rows, start:stop
                ] = values[first : first + plan.kind_rows]


def store_projection(plan, proj_ref, row, lane, values):
    for kind in range(plan.kinds):
        proj_ref[
            kind,
            pl.ds(pl.multiple_of(row * plan.kind_rows, plan.kind_rows), plan.kind_rows),
            pl.ds(lane, values.shape[1]),
        ] = values[kind * plan.kind_rows : (kind + 1) * plan.kind_rows]


def chunk_copy(source, target, sem, chunk, index):
    parts = source.shape[1] // chunk
    place = (index // parts, pl.ds(lax.rem(index, parts) * chunk, chunk))
    return pltpu.make_async_copy(source.at[place], target.at[place], sem.at[index])


def run_ahead(copy, ahead, index, steps):
    @pl.when(index + ahead < steps)
    def _():
        copy(index + ahead).start()


def chunk_place(plan, chunk, index):
    parts = plan.channels // chunk
    return index // parts, lax.rem(index, parts) * chunk


def pair_lane(plan, channel):
    return pl.multiple_of(channel * plan.width_z, 2 * plan.width_z)


def forward_kernel(
    plan,
    chunk,
    u_hbm,
    base_ref,
    y_ref,
    order_ref,
    out_ref,
    u_ref,
    depth_ref,
    proj_ref,
    u_sem,
):
    steps = plan.slab * plan.channels // chunk
    copy = functools.partial(chunk_copy, u_hbm, u_ref, u_sem, chunk)
    for index in range(min(ONE_STREAM, steps)):
        copy(index).start()
    spread_depth(plan, base_ref, depth_ref, 1)

    def step(index, carry):
        copy(index).wait()
        run_ahead(copy, ONE_STREAM, index, steps)
        row, first = chunk_place(plan, chunk, index)
        for pair in range(chunk // 2):
            channel = first + 2 * pair
            values = jnp.concatenate([u_ref[row, channel], u_ref[row, channel + 1]], axis=1)
            projected = dot(y_ref[...], values).astype(BF16)
            store_projection(plan, proj_ref, row, pair_lane(plan, channel), projected)
        return carry

    lax.fori_loop(0, steps, step, 0)
    project_depth(plan, proj_ref, depth_ref, order_ref, out_ref)


def twice_slope(scaled):
    shift = math.log2(2.0 / math.sqrt(math.pi))
    density = jnp.exp2(scaled * (scaled * -math.log2(math.e)) + shift)
    return (lax.erf(scaled) + 1.0) + scaled * density


def middle_kernel(
    plan,
    chunk,
    tile,
    rows_ref,
    point_hbm,
    cot_hbm,
    base_ref,
    base_t_ref,
    y_ref,
    y_t_ref,
    order_ref,
    order_t_ref,
    grad_hbm,
    out_ref,
    point_ref,
    cot_ref,
    grad_ref,
    depth_ref,
    depth_t_ref,
    iz_ref,
    proj_ref,
    point_sem,
    cot_sem,
    grad_sem,
):
    z = plan.width_z
    parts = plan.channels // chunk
    steps = plan.slab * parts
    point_copy = functools.partial(chunk_copy, point_hbm, point_ref, point_sem, chunk)
    cot_copy = functools.partial(chunk_copy, cot_hbm, cot_ref, cot_sem, chunk)
    grad_copy = functools.partial(chunk_copy, grad_ref, grad_hbm, grad_sem, chunk)
    for index in range(min(TWO_STREAMS, steps)):
        point_copy(index).start()
        cot_copy(index).start()
    spread_depth(plan, base_t_ref, depth_t_ref, 0)
    spread_depth(plan, base_ref, depth_ref, 1)
    restore_depth(plan, math.sqrt(0.5), rows_ref, depth_t_ref, order_t_ref, iz_ref)
    tiles = plan.rows_yt // tile

    def step(row, carry):
        def project(channel, start, stop):
            values = jnp.concatenate(
                [grad_ref[row, channel, start:stop], grad_ref[row, channel + 1, start:stop]],
                axis=1,
            )
            return dot(y_ref[:, start:stop], values)

        def store(channel, values):
            store_projection(plan, proj_ref, row, channel * z, values.astype(BF16))

        half_rows = plan.rows_yt // 2
        for channel in range(0, plan.channels, 2):
            if channel % chunk == 0:
                index = row * parts + channel // chunk
                point_copy(index).wait()
                cot_copy(index).wait()
                run_ahead(point_copy, TWO_STREAMS, index, steps)
                run_ahead(cot_copy, TWO_STREAMS, index, steps)
            coefficients = iz_ref[row, :, channel * z : (channel + 2) * z]
            projected = None
            for place in range(tiles):
                span = slice(place * tile, (place + 1) * tile)
                spectral = dot(y_t_ref[span], coefficients)
                for half in range(2):
                    scaled = spectral[:, half * z : (half + 1) * z]
                    scaled = scaled + point_ref[row, channel + half, span].astype(F32)
                    grad = cot_ref[row, channel + half, span].astype(F32) * twice_slope(scaled)
                    grad_ref[row, channel + half, span] = grad.astype(BF16)
                if channel and place == tiles // 2 - 1:
                    projected = project(channel - 2, 0, half_rows)
            if channel:
                projected = projected + project(channel - 2, half_rows, 2 * half_rows)
                store(channel - 2, projected)
            if (channel + 2) % chunk == 0:
                grad_copy(row * parts + channel // chunk).start()
        store(plan.channels - 2, project(plan.channels - 2, 0, plan.rows_yt))
        return carry

    lax.fori_loop(0, plan.slab, step, 0)
    project_depth(plan, proj_ref, depth_ref, order_ref, out_ref)
    for index in range(steps):
        grad_copy(index).wait()


def final_kernel(
    plan,
    chunk,
    tile,
    scale,
    rows_ref,
    point_hbm,
    base_t_ref,
    y_t_ref,
    order_t_ref,
    out_hbm,
    sum_ref,
    point_ref,
    out_ref,
    depth_t_ref,
    iz_ref,
    point_sem,
    out_sem,
):
    z = plan.width_z
    steps = plan.slab * plan.channels // chunk
    copy = functools.partial(chunk_copy, point_hbm, point_ref, point_sem, chunk)
    for index in range(min(ONE_STREAM, steps)):
        copy(index).start()
    sum_ref[...] = unpack_sums(plan, rows_ref) * scale
    spread_depth(plan, base_t_ref, depth_t_ref, 0)
    restore_depth(plan, 1.0, rows_ref, depth_t_ref, order_t_ref, iz_ref)

    def step(index, carry):
        copy(index).wait()
        run_ahead(copy, ONE_STREAM, index, steps)
        row, first = chunk_place(plan, chunk, index)
        for pair in range(chunk // 2):
            channel = first + 2 * pair
            coefficients = iz_ref[row, :, pl.ds(pair_lane(plan, channel), 2 * z)]
            for start in range(0, plan.rows_yt, tile):
                span = slice(start, start + tile)
                spectral = dot(y_t_ref[span], coefficients)
                for half in range(2):
                    total = spectral[:, half * z : (half + 1) * z]
                    total = total + point_ref[row, channel + half, span].astype(F32)
                    out_ref[row, channel + half, span] = total.astype(BF16)
        chunk_copy(out_ref, out_hbm, out_sem, chunk, index).start()
        return carry

    lax.fori_loop(0, steps, step, 0)
    for index in range(steps):
        chunk_copy(out_ref, out_hbm, out_sem, chunk, index).wait()


def pack_rows(plan):
    return 2 * plan.slab


def pack_sums(plan, sums):
    rows = pack_rows(plan)
    count = -(-plan.channels // rows)
    high = sums.astype(BF16)
    low = (sums - high.astype(F32)).astype(BF16)
    pieces = []
    for part in (high.astype(F32), low.astype(F32)):
        spare = count * rows - plan.channels
        if spare:
            part = jnp.concatenate([part, jnp.zeros((spare, plan.channels), F32)], axis=0)
        pieces += [part[index * rows : (index + 1) * rows] for index in range(count)]
    used = 2 * count * plan.channels
    pieces.append(jnp.zeros((rows, plan.extra - used), F32))
    block = jnp.concatenate(pieces, axis=1)
    return jnp.concatenate([block] * plan.devices, axis=0).astype(BF16)


def unpack_sums(plan, rows_ref):
    rows = pack_rows(plan)
    count = -(-plan.channels // rows)
    block = jnp.zeros((rows, plan.extra), F32)
    values = rows_ref[:, plan.lanes : plan.lanes + plan.extra].astype(F32)
    for device in range(plan.devices):
        block = block + values[device * rows : (device + 1) * rows]
    width = plan.channels
    parts = []
    for index in range(count):
        high = block[:, index * width : (index + 1) * width]
        low = block[:, (count + index) * width : (count + index + 1) * width]
        parts.append(high + low)
    return jnp.concatenate(parts, axis=0)[: plan.channels]


def row_copy(source, target, sem, tile, index):
    parts = source.shape[2] // tile
    place = (index // parts, slice(None), pl.ds(lax.rem(index, parts) * tile, tile))
    return pltpu.make_async_copy(source.at[place], target.at[place], sem.at[index])


def row_block(ref, row, start, count):
    channels, z = ref.shape[1], ref.shape[3]
    parts = []
    for index in range(count):
        values = ref[row, :, pl.ds(start + index * TILE_ROWS, TILE_ROWS), :].astype(F32)
        for first in range(0, TILE_ROWS, ROW_GROUP):
            group = values[:, first : first + ROW_GROUP, :]
            parts.append(group.reshape(channels * ROW_GROUP, z).astype(BF16))
    return jnp.concatenate(parts, axis=1)


def spread_weight(side, weight_ref, same_ref, fold_ref, fold_t_ref, spread_ref):
    tall = lax.dot_general(
        fold_t_ref[...],
        weight_ref[...],
        (((1,), (side,)), ((), ())),
        preferred_element_type=F32,
    ).astype(BF16)
    spread_ref[...] = (dot(tall, fold_ref[...]) * same_ref[...]).astype(BF16)


def mix_rows(spread_ref, u_ref, out_ref, row, base, tile, scale):
    channels, z = u_ref.shape[1], u_ref.shape[3]
    for start in range(0, tile, TILE_ROWS):
        mixed = dot(spread_ref[...], row_block(u_ref, row, base + start, 1)) * scale
        groups = [
            mixed[:, first : first + z].reshape(channels, ROW_GROUP, z)
            for first in range(0, mixed.shape[1], z)
        ]
        values = jnp.concatenate(groups, axis=1).astype(BF16)
        out_ref[row, :, pl.ds(base + start, TILE_ROWS), :] = values


def point_kernel(
    tile, side, scale, head, weight_ref, same_ref, fold_ref, fold_t_ref, u_hbm, *rest
):
    out_hbm, u_ref, out_ref, spread_ref, u_sem, out_sem = rest[-6:]
    parts = u_hbm.shape[2] // tile
    steps = u_hbm.shape[0] * parts
    copy = functools.partial(row_copy, u_hbm, u_ref, u_sem, tile)
    for index in range(head, min(head + ONE_STREAM, steps)):
        copy(index).start()
    spread_weight(side, weight_ref, same_ref, fold_ref, fold_t_ref, spread_ref)

    def step(index, carry):
        copy(index).wait()
        run_ahead(copy, ONE_STREAM, index, steps)
        base = pl.multiple_of(lax.rem(index, parts) * tile, tile)
        mix_rows(spread_ref, u_ref, out_ref, index // parts, base, tile, scale)
        row_copy(out_ref, out_hbm, out_sem, tile, index).start()
        return carry

    lax.fori_loop(head, steps, step, 0)
    for index in range(head, steps):
        row_copy(out_ref, out_hbm, out_sem, tile, index).wait()


def point_sum_kernel(
    tile,
    head,
    mix_scale,
    u_hbm,
    g_hbm,
    weight_ref,
    same_ref,
    fold_ref,
    fold_b_ref,
    fold_b_t_ref,
    sum_ref,
    out_hbm,
    u_ref,
    g_ref,
    out_ref,
    spread_ref,
    total_ref,
    u_sem,
    g_sem,
    out_sem,
):
    parts = u_hbm.shape[2] // tile
    steps = u_hbm.shape[0] * parts
    u_copy = functools.partial(row_copy, u_hbm, u_ref, u_sem, tile)
    g_copy = functools.partial(row_copy, g_hbm, g_ref, g_sem, tile)
    out_copy = functools.partial(row_copy, out_ref, out_hbm, out_sem, tile)
    for index in range(min(TWO_STREAMS, steps)):
        u_copy(index).start()
        g_copy(index).start()
    spread_weight(0, weight_ref, same_ref, fold_b_ref, fold_b_t_ref, spread_ref)
    total_ref[...] = jnp.zeros_like(total_ref)

    def step(index, carry):
        u_copy(index).wait()
        g_copy(index).wait()
        run_ahead(u_copy, TWO_STREAMS, index, steps)
        run_ahead(g_copy, TWO_STREAMS, index, steps)
        row = index // parts
        base = pl.multiple_of(lax.rem(index, parts) * tile, tile)

        @pl.when(index < head)
        def _():
            mix_rows(spread_ref, g_ref, out_ref, row, base, tile, mix_scale)
            out_copy(index).start()

        for start in range(0, tile, 4 * TILE_ROWS):
            total_ref[...] += lax.dot_general(
                row_block(u_ref, row, base + start, 4),
                row_block(g_ref, row, base + start, 4),
                (((1,), (1,)), ((), ())),
                preferred_element_type=F32,
            )
        return carry

    lax.fori_loop(0, steps, step, 0)
    for index in range(head):
        out_copy(index).wait()
    kept = total_ref[...] * same_ref[...]
    folded = jnp.dot(
        fold_ref[...], kept, precision=lax.Precision.HIGHEST, preferred_element_type=F32
    )
    sum_ref[...] = lax.dot_general(
        folded,
        fold_ref[...],
        (((1,), (1,)), ((), ())),
        precision=lax.Precision.HIGHEST,
        preferred_element_type=F32,
    )


def mix_kernel(plan, adjoint, step, rows_ref, weight_in, x_ref, x_t_ref, *rest):
    if adjoint:
        sums_ref, modes_ref, out_ref, mixed_ref, weight_ref, weight_sem = rest
    else:
        modes_ref, out_ref, mixed_ref = rest
        weight_ref = weight_in
    steps = plan.channels // step

    def copy(index):
        part = pl.ds(index * step, step)
        return pltpu.make_async_copy(
            weight_in.at[part], weight_ref.at[part], weight_sem.at[index]
        )

    if adjoint:
        for index in range(min(WEIGHT_STREAM, steps)):
            copy(index).start()
    modes = dot(x_ref[...], rows_ref[...])
    for channel in range(plan.channels):
        pieces = []
        for index in range(plan.owned_units):
            lane = index * plan.unit_lanes + channel * plan.unit
            pieces.append(modes[:, lane : lane + plan.unit])
        joined = jnp.concatenate(pieces, axis=1)
        for part in range(2):
            modes_ref[channel, part] = joined[part * KX : (part + 1) * KX]

    def mix_one(index, carry):
        if adjoint:

            @pl.when(lax.rem(index, step) == 0)
            def _():
                copy(index // step).wait()
                run_ahead(copy, WEIGHT_STREAM, index // step, steps)

        real = jnp.zeros((KX, plan.owned), F32)
        imag = jnp.zeros((KX, plan.owned), F32)
        for channel in range(plan.channels):
            place = (index, channel) if adjoint else (channel, index)
            weight_real = weight_ref[place + (0,)].astype(F32)
            weight_imag = weight_ref[place + (1,)].astype(F32)
            mode_real = modes_ref[channel, 0]
            mode_imag = modes_ref[channel, 1]
            if adjoint:
                real += weight_real * mode_real + weight_imag * mode_imag
                imag += weight_real * mode_imag - weight_imag * mode_real
            else:
                real += weight_real * mode_real - weight_imag * mode_imag
                imag += weight_real * mode_imag + weight_imag * mode_real
        mixed_ref[index, 0] = real
        mixed_ref[index, 1] = imag
        return carry

    lax.fori_loop(0, plan.channels, mix_one, 0)
    for index in range(plan.owned_units):
        span = slice(index * plan.unit, (index + 1) * plan.unit)
        halves = []
        for part in range(2):
            pieces = [mixed_ref[channel, part][:, span] for channel in range(plan.channels)]
            spare = plan.unit_lanes - plan.channels * plan.unit
            if spare:
                pieces.append(jnp.zeros((KX, spare), F32))
            halves.append(jnp.concatenate(pieces, axis=1))
        columns = jnp.concatenate(halves, axis=0).astype(BF16)
        lanes = slice(index * plan.unit_lanes, (index + 1) * plan.unit_lanes)
        out_ref[:, lanes] = dot(x_t_ref[...], columns).astype(BF16)
    if adjoint:
        out_ref[:, plan.lanes :] = pack_sums(plan, sums_ref[...])


def weight_grad_kernel(block, channels, modes_ref, grads_ref, out_ref):
    for index in range(block):
        mode_real = modes_ref[index, 0]
        mode_imag = modes_ref[index, 1]
        for channel in range(channels):
            grad_real = grads_ref[channel, 0]
            grad_imag = grads_ref[channel, 1]
            out_ref[index, channel, 0] = grad_real * mode_real + grad_imag * mode_imag
            out_ref[index, channel, 1] = grad_imag * mode_real - grad_real * mode_imag


def whole(shape):
    return pl.BlockSpec(shape, lambda *_: (0,) * len(shape))


def params(mebibytes):
    return pltpu.CompilerParams(vmem_limit_bytes=mebibytes * MIB)


def cost(flops, moved, transcendentals=0):
    return pl.CostEstimate(
        flops=int(flops), bytes_accessed=int(moved), transcendentals=int(transcendentals)
    )


def shards(devices, plume_state, out_cotangent, spectral_weight, pointwise_weight):
    slab, channels, width_y, width_t, width_z = plume_state.shape
    plan = Plan(slab, channels, width_y, width_z, devices)
    rows = plan.rows_yt
    chunk = 4 if channels % 4 == 0 else channels
    steps = slab * (channels // chunk)
    wide = 10 if channels % 10 == 0 else channels
    wide_steps = slab * (channels // wide)
    flat = (slab, channels, rows, width_z)
    state = plume_state.reshape(flat)
    cotangent = out_cotangent.reshape(flat)
    field_bytes = 2 * math.prod(flat)
    exchanged = (devices * slab * 2, plan.lanes)
    exchanged_back = (devices * slab * 2, plan.lanes + plan.extra)

    y_table = jnp.asarray(plan.y_table())
    y_table_t = jnp.asarray(np.ascontiguousarray(plan.y_table().T))
    base = jnp.asarray(plan.depth_base())
    base_t = jnp.asarray(np.ascontiguousarray(plan.depth_base().T))
    order = jnp.asarray(plan.order())
    order_t = jnp.asarray(np.ascontiguousarray(plan.order().T))
    x_table = jnp.asarray(plan.x_table())
    x_table_half = jnp.asarray((plan.x_table().astype(np.float32) * 0.5).astype(ml_dtypes.bfloat16))
    x_table_t = jnp.asarray(np.ascontiguousarray(plan.x_table().T))

    hbm = pl.BlockSpec(memory_space=pl.ANY)
    vmem = pl.BlockSpec(memory_space=pltpu.VMEM)
    field_shape = jax.ShapeDtypeStruct(flat, BF16)
    field = pltpu.VMEM(flat, BF16)
    proj_shape = pltpu.VMEM((plan.kinds, slab * plan.kind_rows, channels * width_z), BF16)
    iz_shape = pltpu.VMEM((slab, plan.kinds * plan.kind_rows, channels * width_z), BF16)
    depth_shape = pltpu.VMEM((channels * width_z, base.shape[1]), BF16)
    depth_t_shape = pltpu.VMEM((base.shape[1], channels * width_z), BF16)
    transform_flops = 2 * math.prod(flat) * 96 * 2
    mode_shape = (channels, 2, KX, plan.owned)

    def sems(count):
        return pltpu.SemaphoreType.DMA((count,))

    def exchange(values):
        blocks = values.reshape(devices, slab * 2, values.shape[1])
        moved = lax.all_to_all(blocks, "gx", split_axis=0, concat_axis=0, tiled=True)
        return moved.reshape(values.shape)

    def mix(adjoint, moved, weight, *sums):
        sent = exchanged_back if adjoint else exchanged
        step = 2 if channels % 2 == 0 else channels
        scratch = [pltpu.VMEM(mode_shape, F32)]
        if adjoint:
            scratch += [pltpu.VMEM(weight.shape, BF16), sems(channels // step)]
        return pl.pallas_call(
            functools.partial(mix_kernel, plan, adjoint, step),
            in_specs=[vmem, hbm if adjoint else vmem] + [vmem] * (2 + len(sums)),
            out_specs=[vmem, vmem],
            out_shape=[
                jax.ShapeDtypeStruct(mode_shape, F32),
                jax.ShapeDtypeStruct(sent, BF16),
            ],
            scratch_shapes=scratch,
            compiler_params=params(58 if adjoint else 12),
            cost_estimate=cost(8 * 864 * 400, 5e6),
            name="mix_back" if adjoint else "mix_modes",
        )(moved, weight, x_table_half if adjoint else x_table, x_table_t, *sums)

    sent = pl.pallas_call(
        functools.partial(forward_kernel, plan, chunk),
        in_specs=[hbm, vmem, vmem, vmem],
        out_specs=vmem,
        out_shape=jax.ShapeDtypeStruct(exchanged, BF16),
        scratch_shapes=[field, depth_shape, proj_shape, sems(steps)],
        compiler_params=params(58),
        cost_estimate=cost(transform_flops, field_bytes),
        name="forward_rows",
    )(state, base, y_table, order)
    sent, later_weight = lax.optimization_barrier((sent, spectral_weight))
    moved = exchange(sent)

    spread = channels * ROW_GROUP
    same = np.kron(np.ones((channels, channels)), np.eye(ROW_GROUP)).astype(np.float32)
    same = jnp.asarray(same)
    fold_rows = np.kron(np.eye(channels), np.ones((1, ROW_GROUP)))
    fold = jnp.asarray(fold_rows.astype(np.float32))
    fold_b = jnp.asarray(rounded(fold_rows))
    fold_b_t = jnp.asarray(rounded(np.ascontiguousarray(fold_rows.T)))
    tile = min(128, rows)
    row_steps = slab * (rows // tile)
    mixing_flops = 2 * math.prod(flat) * spread

    modes, mixed_rows = mix(False, moved, later_weight)
    later_state, mixed_rows = lax.optimization_barrier((state, mixed_rows))
    spread_shape = pltpu.VMEM((spread, spread), BF16)

    def point(side, scale, head, name, values, *begun):
        return pl.pallas_call(
            functools.partial(point_kernel, tile, side, scale, head),
            in_specs=[vmem] * 4 + [hbm] * (1 + len(begun)),
            out_specs=hbm,
            out_shape=field_shape,
            scratch_shapes=[field, field, spread_shape, sems(row_steps), sems(row_steps)],
            input_output_aliases={5: 0} if begun else {},
            compiler_params=params(FIELD_MIB),
            cost_estimate=cost(mixing_flops, 2 * field_bytes),
            name=name,
        )(pointwise_weight, same, fold_b, fold_b_t, values, *begun)

    point_state = point(1, math.sqrt(0.5), 0, "point_mix", later_state)

    restored = exchange(mixed_rows)

    slope_tile = min(128, rows)
    grad_pre, grad_rows = pl.pallas_call(
        functools.partial(middle_kernel, plan, wide, slope_tile),
        in_specs=[vmem, hbm, hbm] + [vmem] * 6,
        out_specs=[hbm, vmem],
        out_shape=[field_shape, jax.ShapeDtypeStruct(exchanged, BF16)],
        scratch_shapes=[field, field, field, depth_shape, depth_t_shape, iz_shape, proj_shape]
        + [sems(wide_steps)] * 3,
        compiler_params=params(FIELD_MIB),
        cost_estimate=cost(2 * transform_flops, 3 * field_bytes, 2 * math.prod(flat)),
        name="activation_grad",
    )(restored, point_state, cotangent, base, base_t, y_table, y_table_t, order, order_t)

    grad_moved = exchange(grad_rows)

    head = max(1, 3 * row_steps // 8)
    sums, begun_back = pl.pallas_call(
        functools.partial(point_sum_kernel, tile, head, 0.5),
        in_specs=[hbm, hbm] + [vmem] * 5,
        out_specs=[vmem, hbm],
        out_shape=[jax.ShapeDtypeStruct((channels, channels), F32), field_shape],
        scratch_shapes=[field, field, field, spread_shape, pltpu.VMEM((spread, spread), F32)]
        + [sems(row_steps)] * 3,
        compiler_params=params(FIELD_MIB),
        cost_estimate=cost(mixing_flops, 2 * field_bytes),
        name="point_sum",
    )(state, grad_pre, pointwise_weight, same, fold, fold_b, fold_b_t)

    grad_modes, back_rows = mix(True, grad_moved, spectral_weight, sums)
    back_moved = exchange(back_rows)

    later_grad, grad_modes = lax.optimization_barrier((grad_pre, grad_modes))
    point_back = point(0, 0.5, head, "point_back", later_grad, begun_back)

    grad_shape = (channels, channels, 2, KX, plan.owned)
    block = 5 if channels % 5 == 0 else 1
    spectral_grad = pl.pallas_call(
        functools.partial(weight_grad_kernel, block, channels),
        grid=(channels // block,),
        in_specs=[
            pl.BlockSpec((block,) + mode_shape[1:], lambda i: (i, 0, 0, 0)),
            whole(mode_shape),
        ],
        out_specs=pl.BlockSpec((block,) + grad_shape[1:], lambda i: (i, 0, 0, 0, 0)),
        out_shape=jax.ShapeDtypeStruct(grad_shape, F32),
        compiler_params=params(14),
        cost_estimate=cost(6 * 864 * 400, 1e7),
        name="weight_grad",
    )(modes, grad_modes)

    scale = 0.5 / math.sqrt(plan.width_x * width_y * width_t * width_z)
    state_grad, pointwise_grad = pl.pallas_call(
        functools.partial(final_kernel, plan, chunk, slope_tile, scale),
        in_specs=[vmem, hbm, vmem, vmem, vmem],
        out_specs=[hbm, vmem],
        out_shape=[field_shape, jax.ShapeDtypeStruct((channels, channels), F32)],
        scratch_shapes=[field, field, depth_t_shape, iz_shape] + [sems(steps)] * 2,
        compiler_params=params(FIELD_MIB),
        cost_estimate=cost(transform_flops, 2 * field_bytes),
        name="state_grad",
    )(back_moved, point_back, base_t, y_table_t, order_t)
    return (state_grad.reshape(plume_state.shape), spectral_grad, pointwise_grad)


def solution(mesh):
    placed = (
        P(("groups", "gx"), None, None, None, None),
        P(("groups", "gx"), None, None, None, None),
        P(None, None, None, None, "gx"),
        P(),
    )
    return jax.shard_map(
        functools.partial(shards, mesh.shape["gx"]),
        mesh=mesh,
        in_specs=placed,
        out_specs=(
            P(("groups", "gx"), None, None, None, None),
            P("groups", None, None, None, "gx"),
            P("groups", None),
        ),
        check_vma=False,
    )
```

```python
import functools
import math

import jax
import jax.numpy as jnp
import ml_dtypes
import numpy as np
from jax import lax
from jax.experimental import pallas as pl
from jax.experimental.pallas import tpu as pltpu
from jax.sharding import PartitionSpec as P

KX = 24
KY = 24
KZ = 24
NT = 2
ROW_GROUP = 8
TILE_ROWS = 16
BF16 = jnp.bfloat16
F32 = jnp.float32
FIELD_MIB = 51
ONE_STREAM = 3
TWO_STREAMS = 3
WEIGHT_STREAM = 8
MIB = 1024 * 1024


def rounded(table):
    return np.asarray(table, np.float64).astype(np.float32).astype(ml_dtypes.bfloat16)


def wave_tables(cells, kept):
    frequency = np.arange(kept) - kept // 2
    angle = 2.0 * np.pi / cells * (frequency[:, None] * np.arange(cells)[None, :] % cells)
    return np.cos(angle) / math.sqrt(cells), np.sin(angle) / math.sqrt(cells)


def depth_table(cells, kept):
    column = np.arange(kept)
    half = kept // 2
    frequency = np.where(column < half, column, column - half + 1)
    angle = 2.0 * np.pi / cells * (np.arange(cells)[:, None] * frequency[None, :] % cells)
    wave = np.where(column[None, :] < half, np.cos(angle), np.sin(angle))
    return wave * math.sqrt(2.0 / cells) * math.sqrt(0.5)


class Plan:
    def __init__(self, slab, channels, width_y, width_z, devices):
        self.slab = slab
        self.channels = channels
        self.width_y = width_y
        self.width_z = width_z
        self.devices = devices
        self.width_x = slab * devices
        self.pairs = KY * NT
        self.owned = self.pairs * KZ // devices
        self.kinds = 3
        self.owners = self.kinds * KZ // self.owned
        self.periods = self.pairs // self.kinds
        self.unit = math.gcd(self.owned, KZ)
        self.units = KZ // self.unit
        self.owned_units = self.owned // self.unit
        self.unit_lanes = 128 * -(-channels * self.unit // 128)
        self.lanes = self.unit_lanes * self.owned_units
        self.rows_yt = width_y * NT
        self.kind_rows = self.periods * 2
        sums = 2 * channels * -(-channels // (2 * slab))
        self.extra = 128 * -(-sums // 128)

    def y_table(self):
        cosine, sine = wave_tables(self.width_y, KY)
        both = np.stack([cosine, -sine])
        table = np.zeros((self.kinds, self.periods, 2, self.width_y, NT))
        for kind in range(self.kinds):
            for period in range(self.periods):
                pair = self.kinds * period + kind
                for time in range(NT):
                    sign = -1.0 if (time % 2 and pair % 2) else 1.0
                    table[kind, period, :, :, time] = sign * both[:, pair // 2]
        return rounded(table.reshape(self.kinds * self.kind_rows, self.rows_yt))

    def depth_base(self):
        values = depth_table(self.width_z, KZ).reshape(self.width_z, self.units, self.unit)
        table = np.zeros((self.width_z, self.units, self.unit_lanes))
        used = self.channels * self.unit
        table[:, :, :used] = np.tile(values, (1, 1, self.channels))
        return rounded(table.reshape(self.width_z, self.units * self.unit_lanes))

    def order(self):
        total = self.devices * self.slab * 2
        source = np.arange(total).reshape(self.owners, self.slab, self.periods, 2)
        source = source.transpose(2, 0, 1, 3).reshape(total)
        table = np.zeros((total, total))
        table[np.arange(total), source] = 1.0
        return rounded(table)

    def x_table(self):
        cosine, sine = wave_tables(self.width_x, KX)
        table = np.zeros((2, KX, self.width_x, 2))
        table[0, :, :, 0] = cosine
        table[0, :, :, 1] = sine
        table[1, :, :, 1] = cosine
        table[1, :, :, 0] = -sine
        return rounded(table.reshape(2 * KX, self.width_x * 2))


def dot(left, right):
    return jnp.dot(left, right, preferred_element_type=F32)


def channel_place(plan, axis):
    count = plan.units * plan.unit_lanes
    shape = (plan.width_z, count) if axis == 1 else (count, plan.width_z)
    return lax.rem(lax.broadcasted_iota(jnp.int32, shape, axis), plan.unit_lanes)


def spread_depth(plan, base_ref, depth_ref, axis):
    place = channel_place(plan, axis)
    base = base_ref[...].astype(F32)
    for channel in range(plan.channels):
        start = channel * plan.unit
        own = (place >= start) & (place < start + plan.unit)
        block = jnp.where(own, base, 0.0).astype(BF16)
        span = slice(channel * plan.width_z, (channel + 1) * plan.width_z)
        if axis == 1:
            depth_ref[span, :] = block
        else:
            depth_ref[:, span] = block


def project_depth(plan, proj_ref, depth_ref, order_ref, out_ref):
    rows = plan.slab * plan.kind_rows
    lanes = plan.unit_lanes
    flat = proj_ref[...].reshape(plan.kinds * rows, plan.channels * plan.width_z)
    parts = dot(flat, depth_ref[...]).astype(BF16)
    owners = []
    for owner in range(plan.owners):
        pieces = []
        for index in range(plan.owned_units):
            kind, unit = divmod(owner * plan.owned_units + index, plan.units)
            pieces.append(
                parts[kind * rows : (kind + 1) * rows, unit * lanes : (unit + 1) * lanes]
            )
        owners.append(jnp.concatenate(pieces, axis=1))
    joined = jnp.concatenate(owners, axis=0)
    out_ref[...] = dot(order_ref[...], joined).astype(BF16)


def restore_depth(plan, scale, rows_ref, depth_t_ref, order_t_ref, iz_ref):
    block = plan.slab * plan.kind_rows
    lanes = plan.unit_lanes
    rows = dot(order_t_ref[...], rows_ref[:, : plan.lanes]).astype(BF16)
    kinds = []
    for kind in range(plan.kinds):
        pieces = []
        for unit in range(plan.units):
            owner, index = divmod(kind * plan.units + unit, plan.owned_units)
            pieces.append(
                rows[owner * block : (owner + 1) * block, index * lanes : (index + 1) * lanes]
            )
        kinds.append(jnp.concatenate(pieces, axis=1))
    joined = jnp.concatenate(kinds, axis=0)
    total = depth_t_ref.shape[1]
    width = min(total, 512)
    for start in range(0, total, width):
        stop = min(total, start + width)
        values = dot(joined, depth_t_ref[:, start:stop])
        if scale != 1.0:
            values = values * scale
        values = values.astype(BF16)
        for kind in range(plan.kinds):
            for row in range(plan.slab):
                first = (kind * plan.slab + row) * plan.kind_rows
                iz_ref[
                    row, kind * plan.kind_rows : (kind + 1) * plan.kind_rows, start:stop
                ] = values[first : first + plan.kind_rows]


def store_projection(plan, proj_ref, row, lane, values):
    for kind in range(plan.kinds):
        proj_ref[
            kind,
            pl.ds(pl.multiple_of(row * plan.kind_rows, plan.kind_rows), plan.kind_rows),
            pl.ds(lane, values.shape[1]),
        ] = values[kind * plan.kind_rows : (kind + 1) * plan.kind_rows]


def chunk_copy(source, target, sem, chunk, index):
    parts = source.shape[1] // chunk
    place = (index // parts, pl.ds(lax.rem(index, parts) * chunk, chunk))
    return pltpu.make_async_copy(source.at[place], target.at[place], sem.at[index])


def run_ahead(copy, ahead, index, steps):
    @pl.when(index + ahead < steps)
    def _():
        copy(index + ahead).start()


def chunk_place(plan, chunk, index):
    parts = plan.channels // chunk
    return index // parts, lax.rem(index, parts) * chunk


def pair_lane(plan, channel):
    return pl.multiple_of(channel * plan.width_z, 2 * plan.width_z)


def forward_kernel(
    plan,
    chunk,
    u_hbm,
    base_hbm,
    y_hbm,
    order_hbm,
    out_ref,
    base_ref,
    y_ref,
    order_ref,
    u_ref,
    depth_ref,
    proj_ref,
    table_sem,
    u_sem,
):
    steps = plan.slab * plan.channels // chunk
    copy = functools.partial(chunk_copy, u_hbm, u_ref, u_sem, chunk)
    y_copy, base_copy, order_copy = [
        pltpu.make_async_copy(source, target, table_sem.at[index])
        for index, (source, target) in enumerate(
            ((y_hbm, y_ref), (base_hbm, base_ref), (order_hbm, order_ref))
        )
    ]
    y_copy.start()
    for index in range(min(ONE_STREAM, steps)):
        copy(index).start()
    base_copy.start()
    order_copy.start()
    y_copy.wait()

    def step(index, carry):
        copy(index).wait()
        run_ahead(copy, ONE_STREAM, index, steps)

        @pl.when(index == steps // 2)
        def _():
            base_copy.wait()
            spread_depth(plan, base_ref, depth_ref, 1)

        row, first = chunk_place(plan, chunk, index)
        for pair in range(chunk // 2):
            channel = first + 2 * pair
            values = jnp.concatenate([u_ref[row, channel], u_ref[row, channel + 1]], axis=1)
            projected = dot(y_ref[...], values).astype(BF16)
            store_projection(plan, proj_ref, row, pair_lane(plan, channel), projected)
        return carry

    lax.fori_loop(0, steps, step, 0)
    order_copy.wait()
    project_depth(plan, proj_ref, depth_ref, order_ref, out_ref)


def twice_slope(scaled):
    shift = math.log2(2.0 / math.sqrt(math.pi))
    density = jnp.exp2(scaled * (scaled * -math.log2(math.e)) + shift)
    return (lax.erf(scaled) + 1.0) + scaled * density


def middle_kernel(
    plan,
    chunk,
    tile,
    rows_ref,
    point_hbm,
    cot_hbm,
    base_ref,
    base_t_ref,
    y_ref,
    y_t_ref,
    order_ref,
    order_t_ref,
    grad_hbm,
    out_ref,
    point_ref,
    cot_ref,
    grad_ref,
    depth_ref,
    depth_t_ref,
    iz_ref,
    proj_ref,
    point_sem,
    cot_sem,
    grad_sem,
):
    z = plan.width_z
    parts = plan.channels // chunk
    steps = plan.slab * parts
    point_copy = functools.partial(chunk_copy, point_hbm, point_ref, point_sem, chunk)
    cot_copy = functools.partial(chunk_copy, cot_hbm, cot_ref, cot_sem, chunk)
    grad_copy = functools.partial(chunk_copy, grad_ref, grad_hbm, grad_sem, chunk)
    for index in range(min(TWO_STREAMS, steps)):
        point_copy(index).start()
        cot_copy(index).start()
    spread_depth(plan, base_t_ref, depth_t_ref, 0)
    spread_depth(plan, base_ref, depth_ref, 1)
    restore_depth(plan, math.sqrt(0.5), rows_ref, depth_t_ref, order_t_ref, iz_ref)
    tiles = plan.rows_yt // tile

    def step(row, carry):
        def project(channel, start, stop):
            values = jnp.concatenate(
                [grad_ref[row, channel, start:stop], grad_ref[row, channel + 1, start:stop]],
                axis=1,
            )
            return dot(y_ref[:, start:stop], values)

        def store(channel, values):
            store_projection(plan, proj_ref, row, channel * z, values.astype(BF16))

        half_rows = plan.rows_yt // 2
        for channel in range(0, plan.channels, 2):
            if channel % chunk == 0:
                index = row * parts + channel // chunk
                point_copy(index).wait()
                cot_copy(index).wait()
                run_ahead(point_copy, TWO_STREAMS, index, steps)
                run_ahead(cot_copy, TWO_STREAMS, index, steps)
            coefficients = iz_ref[row, :, channel * z : (channel + 2) * z]
            projected = None
            for place in range(tiles):
                span = slice(place * tile, (place + 1) * tile)
                spectral = dot(y_t_ref[span], coefficients)
                for half in range(2):
                    scaled = spectral[:, half * z : (half + 1) * z]
                    scaled = scaled + point_ref[row, channel + half, span].astype(F32)
                    grad = cot_ref[row, channel + half, span].astype(F32) * twice_slope(scaled)
                    grad_ref[row, channel + half, span] = grad.astype(BF16)
                if channel and place == tiles // 2 - 1:
                    projected = project(channel - 2, 0, half_rows)
            if channel:
                projected = projected + project(channel - 2, half_rows, 2 * half_rows)
                store(channel - 2, projected)
            if (channel + 2) % chunk == 0:
                grad_copy(row * parts + channel // chunk).start()
        store(plan.channels - 2, project(plan.channels - 2, 0, plan.rows_yt))
        return carry

    lax.fori_loop(0, plan.slab, step, 0)
    project_depth(plan, proj_ref, depth_ref, order_ref, out_ref)
    for index in range(steps):
        grad_copy(index).wait()


def final_kernel(
    plan,
    chunk,
    tile,
    scale,
    rows_ref,
    point_hbm,
    base_t_ref,
    y_t_ref,
    order_t_ref,
    out_hbm,
    sum_ref,
    point_ref,
    out_ref,
    depth_t_ref,
    iz_ref,
    point_sem,
    out_sem,
):
    z = plan.width_z
    steps = plan.slab * plan.channels // chunk
    copy = functools.partial(chunk_copy, point_hbm, point_ref, point_sem, chunk)
    for index in range(min(ONE_STREAM, steps)):
        copy(index).start()
    sum_ref[...] = unpack_sums(plan, rows_ref) * scale
    spread_depth(plan, base_t_ref, depth_t_ref, 0)
    restore_depth(plan, 1.0, rows_ref, depth_t_ref, order_t_ref, iz_ref)

    def step(index, carry):
        copy(index).wait()
        run_ahead(copy, ONE_STREAM, index, steps)
        row, first = chunk_place(plan, chunk, index)
        for pair in range(chunk // 2):
            channel = first + 2 * pair
            coefficients = iz_ref[row, :, pl.ds(pair_lane(plan, channel), 2 * z)]
            for start in range(0, plan.rows_yt, tile):
                span = slice(start, start + tile)
                spectral = dot(y_t_ref[span], coefficients)
                for half in range(2):
                    total = spectral[:, half * z : (half + 1) * z]
                    total = total + point_ref[row, channel + half, span].astype(F32)
                    out_ref[row, channel + half, span] = total.astype(BF16)
        chunk_copy(out_ref, out_hbm, out_sem, chunk, index).start()
        return carry

    lax.fori_loop(0, steps, step, 0)
    for index in range(steps):
        chunk_copy(out_ref, out_hbm, out_sem, chunk, index).wait()


def pack_rows(plan):
    return 2 * plan.slab


def pack_sums(plan, sums):
    rows = pack_rows(plan)
    count = -(-plan.channels // rows)
    high = sums.astype(BF16)
    low = (sums - high.astype(F32)).astype(BF16)
    pieces = []
    for part in (high.astype(F32), low.astype(F32)):
        spare = count * rows - plan.channels
        if spare:
            part = jnp.concatenate([part, jnp.zeros((spare, plan.channels), F32)], axis=0)
        pieces += [part[index * rows : (index + 1) * rows] for index in range(count)]
    used = 2 * count * plan.channels
    pieces.append(jnp.zeros((rows, plan.extra - used), F32))
    block = jnp.concatenate(pieces, axis=1)
    return jnp.concatenate([block] * plan.devices, axis=0).astype(BF16)


def unpack_sums(plan, rows_ref):
    rows = pack_rows(plan)
    count = -(-plan.channels // rows)
    block = jnp.zeros((rows, plan.extra), F32)
    values = rows_ref[:, plan.lanes : plan.lanes + plan.extra].astype(F32)
    for device in range(plan.devices):
        block = block + values[device * rows : (device + 1) * rows]
    width = plan.channels
    parts = []
    for index in range(count):
        high = block[:, index * width : (index + 1) * width]
        low = block[:, (count + index) * width : (count + index + 1) * width]
        parts.append(high + low)
    return jnp.concatenate(parts, axis=0)[: plan.channels]


def row_copy(source, target, sem, tile, index):
    parts = source.shape[2] // tile
    place = (index // parts, slice(None), pl.ds(lax.rem(index, parts) * tile, tile))
    return pltpu.make_async_copy(source.at[place], target.at[place], sem.at[index])


def row_block(ref, row, start, count):
    channels, z = ref.shape[1], ref.shape[3]
    parts = []
    for index in range(count):
        values = ref[row, :, pl.ds(start + index * TILE_ROWS, TILE_ROWS), :].astype(F32)
        for first in range(0, TILE_ROWS, ROW_GROUP):
            group = values[:, first : first + ROW_GROUP, :]
            parts.append(group.reshape(channels * ROW_GROUP, z).astype(BF16))
    return jnp.concatenate(parts, axis=1)


def spread_weight(side, weight_ref, same_ref, fold_ref, fold_t_ref, spread_ref):
    tall = lax.dot_general(
        fold_t_ref[...],
        weight_ref[...],
        (((1,), (side,)), ((), ())),
        preferred_element_type=F32,
    ).astype(BF16)
    spread_ref[...] = (dot(tall, fold_ref[...]) * same_ref[...]).astype(BF16)


def mix_rows(spread_ref, u_ref, out_ref, row, base, tile, scale):
    channels, z = u_ref.shape[1], u_ref.shape[3]
    for start in range(0, tile, TILE_ROWS):
        mixed = dot(spread_ref[...], row_block(u_ref, row, base + start, 1)) * scale
        groups = [
            mixed[:, first : first + z].reshape(channels, ROW_GROUP, z)
            for first in range(0, mixed.shape[1], z)
        ]
        values = jnp.concatenate(groups, axis=1).astype(BF16)
        out_ref[row, :, pl.ds(base + start, TILE_ROWS), :] = values


def point_kernel(
    tile, side, scale, head, weight_ref, same_ref, fold_ref, fold_t_ref, u_hbm, *rest
):
    out_hbm, u_ref, out_ref, spread_ref, u_sem, out_sem = rest[-6:]
    parts = u_hbm.shape[2] // tile
    steps = u_hbm.shape[0] * parts
    copy = functools.partial(row_copy, u_hbm, u_ref, u_sem, tile)
    for index in range(head, min(head + ONE_STREAM, steps)):
        copy(index).start()
    spread_weight(side, weight_ref, same_ref, fold_ref, fold_t_ref, spread_ref)

    def step(index, carry):
        copy(index).wait()
        run_ahead(copy, ONE_STREAM, index, steps)
        base = pl.multiple_of(lax.rem(index, parts) * tile, tile)
        mix_rows(spread_ref, u_ref, out_ref, index // parts, base, tile, scale)
        row_copy(out_ref, out_hbm, out_sem, tile, index).start()
        return carry

    lax.fori_loop(head, steps, step, 0)
    for index in range(head, steps):
        row_copy(out_ref, out_hbm, out_sem, tile, index).wait()


def point_sum_kernel(
    tile,
    head,
    mix_scale,
    u_hbm,
    g_hbm,
    weight_ref,
    same_ref,
    fold_ref,
    fold_b_ref,
    fold_b_t_ref,
    sum_ref,
    out_hbm,
    u_ref,
    g_ref,
    out_ref,
    spread_ref,
    total_ref,
    u_sem,
    g_sem,
    out_sem,
):
    parts = u_hbm.shape[2] // tile
    steps = u_hbm.shape[0] * parts
    u_copy = functools.partial(row_copy, u_hbm, u_ref, u_sem, tile)
    g_copy = functools.partial(row_copy, g_hbm, g_ref, g_sem, tile)
    out_copy = functools.partial(row_copy, out_ref, out_hbm, out_sem, tile)
    for index in range(min(TWO_STREAMS, steps)):
        u_copy(index).start()
        g_copy(index).start()
    spread_weight(0, weight_ref, same_ref, fold_b_ref, fold_b_t_ref, spread_ref)
    total_ref[...] = jnp.zeros_like(total_ref)

    def step(index, carry):
        u_copy(index).wait()
        g_copy(index).wait()
        run_ahead(u_copy, TWO_STREAMS, index, steps)
        run_ahead(g_copy, TWO_STREAMS, index, steps)
        row = index // parts
        base = pl.multiple_of(lax.rem(index, parts) * tile, tile)

        @pl.when(index < head)
        def _():
            mix_rows(spread_ref, g_ref, out_ref, row, base, tile, mix_scale)
            out_copy(index).start()

        for start in range(0, tile, 4 * TILE_ROWS):
            total_ref[...] += lax.dot_general(
                row_block(u_ref, row, base + start, 4),
                row_block(g_ref, row, base + start, 4),
                (((1,), (1,)), ((), ())),
                preferred_element_type=F32,
            )
        return carry

    lax.fori_loop(0, steps, step, 0)
    for index in range(head):
        out_copy(index).wait()
    kept = total_ref[...] * same_ref[...]
    folded = jnp.dot(
        fold_ref[...], kept, precision=lax.Precision.HIGHEST, preferred_element_type=F32
    )
    sum_ref[...] = lax.dot_general(
        folded,
        fold_ref[...],
        (((1,), (1,)), ((), ())),
        precision=lax.Precision.HIGHEST,
        preferred_element_type=F32,
    )


def mix_kernel(plan, adjoint, step, rows_ref, weight_in, x_ref, x_t_ref, *rest):
    if adjoint:
        sums_ref, modes_ref, out_ref, mixed_ref, weight_ref, weight_sem = rest
    else:
        modes_ref, out_ref, mixed_ref = rest
        weight_ref = weight_in
    steps = plan.channels // step

    def copy(index):
        part = pl.ds(index * step, step)
        return pltpu.make_async_copy(
            weight_in.at[part], weight_ref.at[part], weight_sem.at[index]
        )

    if adjoint:
        for index in range(min(WEIGHT_STREAM, steps)):
            copy(index).start()
    modes = dot(x_ref[...], rows_ref[...])
    for channel in range(plan.channels):
        pieces = []
        for index in range(plan.owned_units):
            lane = index * plan.unit_lanes + channel * plan.unit
            pieces.append(modes[:, lane : lane + plan.unit])
        joined = jnp.concatenate(pieces, axis=1)
        for part in range(2):
            modes_ref[channel, part] = joined[part * KX : (part + 1) * KX]

    def mix_one(index, carry):
        if adjoint:

            @pl.when(lax.rem(index, step) == 0)
            def _():
                copy(index // step).wait()
                run_ahead(copy, WEIGHT_STREAM, index // step, steps)

        real = jnp.zeros((KX, plan.owned), F32)
        imag = jnp.zeros((KX, plan.owned), F32)
        for channel in range(plan.channels):
            place = (index, channel) if adjoint else (channel, index)
            weight_real = weight_ref[place + (0,)].astype(F32)
            weight_imag = weight_ref[place + (1,)].astype(F32)
            mode_real = modes_ref[channel, 0]
            mode_imag = modes_ref[channel, 1]
            if adjoint:
                real += weight_real * mode_real + weight_imag * mode_imag
                imag += weight_real * mode_imag - weight_imag * mode_real
            else:
                real += weight_real * mode_real - weight_imag * mode_imag
                imag += weight_real * mode_imag + weight_imag * mode_real
        mixed_ref[index, 0] = real
        mixed_ref[index, 1] = imag
        return carry

    lax.fori_loop(0, plan.channels, mix_one, 0)
    for index in range(plan.owned_units):
        span = slice(index * plan.unit, (index + 1) * plan.unit)
        halves = []
        for part in range(2):
            pieces = [mixed_ref[channel, part][:, span] for channel in range(plan.channels)]
            spare = plan.unit_lanes - plan.channels * plan.unit
            if spare:
                pieces.append(jnp.zeros((KX, spare), F32))
            halves.append(jnp.concatenate(pieces, axis=1))
        columns = jnp.concatenate(halves, axis=0).astype(BF16)
        lanes = slice(index * plan.unit_lanes, (index + 1) * plan.unit_lanes)
        out_ref[:, lanes] = dot(x_t_ref[...], columns).astype(BF16)
    if adjoint:
        out_ref[:, plan.lanes :] = pack_sums(plan, sums_ref[...])


def weight_grad_kernel(block, channels, modes_ref, grads_ref, out_ref):
    for index in range(block):
        mode_real = modes_ref[index, 0]
        mode_imag = modes_ref[index, 1]
        for channel in range(channels):
            grad_real = grads_ref[channel, 0]
            grad_imag = grads_ref[channel, 1]
            out_ref[index, channel, 0] = grad_real * mode_real + grad_imag * mode_imag
            out_ref[index, channel, 1] = grad_imag * mode_real - grad_real * mode_imag


def whole(shape):
    return pl.BlockSpec(shape, lambda *_: (0,) * len(shape))


def params(mebibytes):
    return pltpu.CompilerParams(vmem_limit_bytes=mebibytes * MIB)


def cost(flops, moved, transcendentals=0):
    return pl.CostEstimate(
        flops=int(flops), bytes_accessed=int(moved), transcendentals=int(transcendentals)
    )


def shards(devices, plume_state, out_cotangent, spectral_weight, pointwise_weight):
    slab, channels, width_y, width_t, width_z = plume_state.shape
    plan = Plan(slab, channels, width_y, width_z, devices)
    rows = plan.rows_yt
    chunk = 10 if channels % 10 == 0 else channels
    steps = slab * (channels // chunk)
    flat = (slab, channels, rows, width_z)
    state = plume_state.reshape(flat)
    cotangent = out_cotangent.reshape(flat)
    field_bytes = 2 * math.prod(flat)
    exchanged = (devices * slab * 2, plan.lanes)
    exchanged_back = (devices * slab * 2, plan.lanes + plan.extra)

    y_table = jnp.asarray(plan.y_table())
    y_table_t = jnp.asarray(np.ascontiguousarray(plan.y_table().T))
    base = jnp.asarray(plan.depth_base())
    base_t = jnp.asarray(np.ascontiguousarray(plan.depth_base().T))
    order = jnp.asarray(plan.order())
    order_t = jnp.asarray(np.ascontiguousarray(plan.order().T))
    x_table = jnp.asarray(plan.x_table())
    x_table_half = jnp.asarray((plan.x_table().astype(np.float32) * 0.5).astype(ml_dtypes.bfloat16))
    x_table_t = jnp.asarray(np.ascontiguousarray(plan.x_table().T))

    hbm = pl.BlockSpec(memory_space=pl.ANY)
    vmem = pl.BlockSpec(memory_space=pltpu.VMEM)
    field_shape = jax.ShapeDtypeStruct(flat, BF16)
    field = pltpu.VMEM(flat, BF16)
    proj_shape = pltpu.VMEM((plan.kinds, slab * plan.kind_rows, channels * width_z), BF16)
    iz_shape = pltpu.VMEM((slab, plan.kinds * plan.kind_rows, channels * width_z), BF16)
    depth_shape = pltpu.VMEM((channels * width_z, base.shape[1]), BF16)
    depth_t_shape = pltpu.VMEM((base.shape[1], channels * width_z), BF16)
    transform_flops = 2 * math.prod(flat) * 96 * 2
    mode_shape = (channels, 2, KX, plan.owned)

    def sems(count):
        return pltpu.SemaphoreType.DMA((count,))

    def exchange(values):
        blocks = values.reshape(devices, slab * 2, values.shape[1])
        moved = lax.all_to_all(blocks, "gx", split_axis=0, concat_axis=0, tiled=True)
        return moved.reshape(values.shape)

    def mix(adjoint, moved, weight, *sums):
        sent = exchanged_back if adjoint else exchanged
        step = 2 if channels % 2 == 0 else channels
        scratch = [pltpu.VMEM(mode_shape, F32)]
        if adjoint:
            scratch += [pltpu.VMEM(weight.shape, BF16), sems(channels // step)]
        return pl.pallas_call(
            functools.partial(mix_kernel, plan, adjoint, step),
            in_specs=[vmem, hbm if adjoint else vmem] + [vmem] * (2 + len(sums)),
            out_specs=[vmem, vmem],
            out_shape=[
                jax.ShapeDtypeStruct(mode_shape, F32),
                jax.ShapeDtypeStruct(sent, BF16),
            ],
            scratch_shapes=scratch,
            compiler_params=params(53 if adjoint else 12),
            cost_estimate=cost(8 * 864 * 400, 5e6),
            name="mix_back" if adjoint else "mix_modes",
        )(moved, weight, x_table_half if adjoint else x_table, x_table_t, *sums)

    sent = pl.pallas_call(
        functools.partial(forward_kernel, plan, chunk),
        in_specs=[hbm, hbm, hbm, hbm],
        out_specs=vmem,
        out_shape=jax.ShapeDtypeStruct(exchanged, BF16),
        scratch_shapes=[
            pltpu.VMEM(base.shape, BF16),
            pltpu.VMEM(y_table.shape, BF16),
            pltpu.VMEM(order.shape, BF16),
            field,
            depth_shape,
            proj_shape,
            sems(3),
            sems(steps),
        ],
        compiler_params=params(58),
        cost_estimate=cost(transform_flops, field_bytes),
        name="forward_rows",
    )(state, base, y_table, order)
    sent, later_weight = lax.optimization_barrier((sent, spectral_weight))
    moved = exchange(sent)

    spread = channels * ROW_GROUP
    same = np.kron(np.ones((channels, channels)), np.eye(ROW_GROUP)).astype(np.float32)
    same = jnp.asarray(same)
    fold_rows = np.kron(np.eye(channels), np.ones((1, ROW_GROUP)))
    fold = jnp.asarray(fold_rows.astype(np.float32))
    fold_b = jnp.asarray(rounded(fold_rows))
    fold_b_t = jnp.asarray(rounded(np.ascontiguousarray(fold_rows.T)))
    tile = min(256, rows)
    row_steps = slab * (rows // tile)
    mixing_flops = 2 * math.prod(flat) * spread

    modes, mixed_rows = mix(False, moved, later_weight)
    later_state, mixed_rows = lax.optimization_barrier((state, mixed_rows))
    spread_shape = pltpu.VMEM((spread, spread), BF16)

    def point(side, scale, head, name, values, *begun):
        return pl.pallas_call(
            functools.partial(point_kernel, tile, side, scale, head),
            in_specs=[vmem] * 4 + [hbm] * (1 + len(begun)),
            out_specs=hbm,
            out_shape=field_shape,
            scratch_shapes=[field, field, spread_shape, sems(row_steps), sems(row_steps)],
            input_output_aliases={5: 0} if begun else {},
            compiler_params=params(FIELD_MIB),
            cost_estimate=cost(mixing_flops, 2 * field_bytes),
            name=name,
        )(pointwise_weight, same, fold_b, fold_b_t, values, *begun)

    point_state = point(1, math.sqrt(0.5), 0, "point_mix", later_state)

    restored = exchange(mixed_rows)

    slope_tile = min(128, rows)
    grad_pre, grad_rows = pl.pallas_call(
        functools.partial(middle_kernel, plan, chunk, slope_tile),
        in_specs=[vmem, hbm, hbm] + [vmem] * 6,
        out_specs=[hbm, vmem],
        out_shape=[field_shape, jax.ShapeDtypeStruct(exchanged, BF16)],
        scratch_shapes=[field, field, field, depth_shape, depth_t_shape, iz_shape, proj_shape]
        + [sems(steps)] * 3,
        compiler_params=params(FIELD_MIB),
        cost_estimate=cost(2 * transform_flops, 3 * field_bytes, 2 * math.prod(flat)),
        name="activation_grad",
    )(restored, point_state, cotangent, base, base_t, y_table, y_table_t, order, order_t)

    grad_moved = exchange(grad_rows)

    head = max(1, row_steps // 4)
    sums, begun_back = pl.pallas_call(
        functools.partial(point_sum_kernel, tile, head, 0.5),
        in_specs=[hbm, hbm] + [vmem] * 5,
        out_specs=[vmem, hbm],
        out_shape=[jax.ShapeDtypeStruct((channels, channels), F32), field_shape],
        scratch_shapes=[field, field, field, spread_shape, pltpu.VMEM((spread, spread), F32)]
        + [sems(row_steps)] * 3,
        compiler_params=params(FIELD_MIB),
        cost_estimate=cost(mixing_flops, 2 * field_bytes),
        name="point_sum",
    )(state, grad_pre, pointwise_weight, same, fold, fold_b, fold_b_t)

    grad_modes, back_rows = mix(True, grad_moved, spectral_weight, sums)
    back_moved = exchange(back_rows)

    later_grad, grad_modes = lax.optimization_barrier((grad_pre, grad_modes))
    point_back = point(0, 0.5, head, "point_back", later_grad, begun_back)

    grad_shape = (channels, channels, 2, KX, plan.owned)
    block = 5 if channels % 5 == 0 else 1
    spectral_grad = pl.pallas_call(
        functools.partial(weight_grad_kernel, block, channels),
        grid=(channels // block,),
        in_specs=[
            pl.BlockSpec((block,) + mode_shape[1:], lambda i: (i, 0, 0, 0)),
            whole(mode_shape),
        ],
        out_specs=pl.BlockSpec((block,) + grad_shape[1:], lambda i: (i, 0, 0, 0, 0)),
        out_shape=jax.ShapeDtypeStruct(grad_shape, F32),
        compiler_params=params(14),
        cost_estimate=cost(6 * 864 * 400, 1e7),
        name="weight_grad",
    )(modes, grad_modes)

    scale = 0.5 / math.sqrt(plan.width_x * width_y * width_t * width_z)
    state_grad, pointwise_grad = pl.pallas_call(
        functools.partial(final_kernel, plan, chunk, slope_tile, scale),
        in_specs=[vmem, hbm, vmem, vmem, vmem],
        out_specs=[hbm, vmem],
        out_shape=[field_shape, jax.ShapeDtypeStruct((channels, channels), F32)],
        scratch_shapes=[field, field, depth_t_shape, iz_shape] + [sems(steps)] * 2,
        compiler_params=params(FIELD_MIB),
        cost_estimate=cost(transform_flops, 2 * field_bytes),
        name="state_grad",
    )(back_moved, point_back, base_t, y_table_t, order_t)
    return (state_grad.reshape(plume_state.shape), spectral_grad, pointwise_grad)


def solution(mesh):
    placed = (
        P(("groups", "gx"), None, None, None, None),
        P(("groups", "gx"), None, None, None, None),
        P(None, None, None, None, "gx"),
        P(),
    )
    return jax.shard_map(
        functools.partial(shards, mesh.shape["gx"]),
        mesh=mesh,
        in_specs=placed,
        out_specs=(
            P(("groups", "gx"), None, None, None, None),
            P("groups", None, None, None, "gx"),
            P("groups", None),
        ),
        check_vma=False,
    )
```

```python
import functools
import math

import jax
import jax.numpy as jnp
import ml_dtypes
import numpy as np
from jax import lax
from jax.experimental import pallas as pl
from jax.experimental.pallas import tpu as pltpu
from jax.sharding import PartitionSpec as P

KX = 24
KY = 24
KZ = 24
NT = 2
ROW_GROUP = 8
TILE_ROWS = 16
BF16 = jnp.bfloat16
F32 = jnp.float32
FIELD_MIB = 51
ONE_STREAM = 3
TWO_STREAMS = 3
WEIGHT_STREAM = 8
MIB = 1024 * 1024


def rounded(table):
    return np.asarray(table, np.float64).astype(np.float32).astype(ml_dtypes.bfloat16)


def wave_tables(cells, kept):
    frequency = np.arange(kept) - kept // 2
    angle = 2.0 * np.pi / cells * (frequency[:, None] * np.arange(cells)[None, :] % cells)
    return np.cos(angle) / math.sqrt(cells), np.sin(angle) / math.sqrt(cells)


def depth_table(cells, kept):
    column = np.arange(kept)
    half = kept // 2
    frequency = np.where(column < half, column, column - half + 1)
    angle = 2.0 * np.pi / cells * (np.arange(cells)[:, None] * frequency[None, :] % cells)
    wave = np.where(column[None, :] < half, np.cos(angle), np.sin(angle))
    return wave * math.sqrt(2.0 / cells) * math.sqrt(0.5)


class Plan:
    def __init__(self, slab, channels, width_y, width_z, devices):
        self.slab = slab
        self.channels = channels
        self.width_y = width_y
        self.width_z = width_z
        self.devices = devices
        self.width_x = slab * devices
        self.pairs = KY * NT
        self.owned = self.pairs * KZ // devices
        self.kinds = 3
        self.owners = self.kinds * KZ // self.owned
        self.periods = self.pairs // self.kinds
        self.unit = math.gcd(self.owned, KZ)
        self.units = KZ // self.unit
        self.owned_units = self.owned // self.unit
        self.unit_lanes = 128 * -(-channels * self.unit // 128)
        self.lanes = self.unit_lanes * self.owned_units
        self.rows_yt = width_y * NT
        self.kind_rows = self.periods * 2
        sums = 2 * channels * -(-channels // (2 * slab))
        self.extra = 128 * -(-sums // 128)

    def y_table(self):
        cosine, sine = wave_tables(self.width_y, KY)
        both = np.stack([cosine, -sine])
        table = np.zeros((self.kinds, self.periods, 2, self.width_y, NT))
        for kind in range(self.kinds):
            for period in range(self.periods):
                pair = self.kinds * period + kind
                for time in range(NT):
                    sign = -1.0 if (time % 2 and pair % 2) else 1.0
                    table[kind, period, :, :, time] = sign * both[:, pair // 2]
        return rounded(table.reshape(self.kinds * self.kind_rows, self.rows_yt))

    def depth_base(self):
        values = depth_table(self.width_z, KZ).reshape(self.width_z, self.units, self.unit)
        table = np.zeros((self.width_z, self.units, self.unit_lanes))
        used = self.channels * self.unit
        table[:, :, :used] = np.tile(values, (1, 1, self.channels))
        return rounded(table.reshape(self.width_z, self.units * self.unit_lanes))

    def order(self):
        total = self.devices * self.slab * 2
        source = np.arange(total).reshape(self.owners, self.slab, self.periods, 2)
        source = source.transpose(2, 0, 1, 3).reshape(total)
        table = np.zeros((total, total))
        table[np.arange(total), source] = 1.0
        return rounded(table)

    def x_table(self):
        cosine, sine = wave_tables(self.width_x, KX)
        table = np.zeros((2, KX, self.width_x, 2))
        table[0, :, :, 0] = cosine
        table[0, :, :, 1] = sine
        table[1, :, :, 1] = cosine
        table[1, :, :, 0] = -sine
        return rounded(table.reshape(2 * KX, self.width_x * 2))


def dot(left, right):
    return jnp.dot(left, right, preferred_element_type=F32)


def channel_place(plan, axis):
    count = plan.units * plan.unit_lanes
    shape = (plan.width_z, count) if axis == 1 else (count, plan.width_z)
    return lax.rem(lax.broadcasted_iota(jnp.int32, shape, axis), plan.unit_lanes)


def spread_depth(plan, base_ref, depth_ref, axis):
    place = channel_place(plan, axis)
    base = base_ref[...].astype(F32)
    for channel in range(plan.channels):
        start = channel * plan.unit
        own = (place >= start) & (place < start + plan.unit)
        block = jnp.where(own, base, 0.0).astype(BF16)
        span = slice(channel * plan.width_z, (channel + 1) * plan.width_z)
        if axis == 1:
            depth_ref[span, :] = block
        else:
            depth_ref[:, span] = block


def project_depth(plan, proj_ref, depth_ref, order_ref, out_ref):
    rows = plan.slab * plan.kind_rows
    lanes = plan.unit_lanes
    flat = proj_ref[...].reshape(plan.kinds * rows, plan.channels * plan.width_z)
    parts = dot(flat, depth_ref[...]).astype(BF16)
    owners = []
    for owner in range(plan.owners):
        pieces = []
        for index in range(plan.owned_units):
            kind, unit = divmod(owner * plan.owned_units + index, plan.units)
            pieces.append(
                parts[kind * rows : (kind + 1) * rows, unit * lanes : (unit + 1) * lanes]
            )
        owners.append(jnp.concatenate(pieces, axis=1))
    joined = jnp.concatenate(owners, axis=0)
    out_ref[...] = dot(order_ref[...], joined).astype(BF16)


def restore_depth(plan, scale, rows_ref, depth_t_ref, order_t_ref, iz_ref):
    block = plan.slab * plan.kind_rows
    lanes = plan.unit_lanes
    rows = dot(order_t_ref[...], rows_ref[:, : plan.lanes]).astype(BF16)
    kinds = []
    for kind in range(plan.kinds):
        pieces = []
        for unit in range(plan.units):
            owner, index = divmod(kind * plan.units + unit, plan.owned_units)
            pieces.append(
                rows[owner * block : (owner + 1) * block, index * lanes : (index + 1) * lanes]
            )
        kinds.append(jnp.concatenate(pieces, axis=1))
    joined = jnp.concatenate(kinds, axis=0)
    total = depth_t_ref.shape[1]
    width = min(total, 512)
    for start in range(0, total, width):
        stop = min(total, start + width)
        values = dot(joined, depth_t_ref[:, start:stop])
        if scale != 1.0:
            values = values * scale
        values = values.astype(BF16)
        for kind in range(plan.kinds):
            for row in range(plan.slab):
                first = (kind * plan.slab + row) * plan.kind_rows
                iz_ref[
                    row, kind * plan.kind_rows : (kind + 1) * plan.kind_rows, start:stop
                ] = values[first : first + plan.kind_rows]


def store_projection(plan, proj_ref, row, lane, values):
    for kind in range(plan.kinds):
        proj_ref[
            kind,
            pl.ds(pl.multiple_of(row * plan.kind_rows, plan.kind_rows), plan.kind_rows),
            pl.ds(lane, values.shape[1]),
        ] = values[kind * plan.kind_rows : (kind + 1) * plan.kind_rows]


def chunk_copy(source, target, sem, chunk, index):
    parts = source.shape[1] // chunk
    place = (index // parts, pl.ds(lax.rem(index, parts) * chunk, chunk))
    return pltpu.make_async_copy(source.at[place], target.at[place], sem.at[index])


def run_ahead(copy, ahead, index, steps):
    @pl.when(index + ahead < steps)
    def _():
        copy(index + ahead).start()


def chunk_place(plan, chunk, index):
    parts = plan.channels // chunk
    return index // parts, lax.rem(index, parts) * chunk


def pair_lane(plan, channel):
    return pl.multiple_of(channel * plan.width_z, 2 * plan.width_z)


def forward_kernel(
    plan,
    chunk,
    u_hbm,
    base_hbm,
    y_hbm,
    order_hbm,
    out_ref,
    base_ref,
    y_ref,
    order_ref,
    u_ref,
    depth_ref,
    proj_ref,
    table_sem,
    u_sem,
):
    steps = plan.slab * plan.channels // chunk
    copy = functools.partial(chunk_copy, u_hbm, u_ref, u_sem, chunk)
    y_copy, base_copy, order_copy = [
        pltpu.make_async_copy(source, target, table_sem.at[index])
        for index, (source, target) in enumerate(
            ((y_hbm, y_ref), (base_hbm, base_ref), (order_hbm, order_ref))
        )
    ]
    y_copy.start()
    for index in range(min(ONE_STREAM, steps)):
        copy(index).start()
    base_copy.start()
    order_copy.start()
    y_copy.wait()

    def step(index, carry):
        copy(index).wait()
        run_ahead(copy, ONE_STREAM, index, steps)

        @pl.when(index == steps // 2)
        def _():
            base_copy.wait()
            spread_depth(plan, base_ref, depth_ref, 1)

        row, first = chunk_place(plan, chunk, index)
        for pair in range(chunk // 2):
            channel = first + 2 * pair
            values = jnp.concatenate([u_ref[row, channel], u_ref[row, channel + 1]], axis=1)
            projected = dot(y_ref[...], values).astype(BF16)
            store_projection(plan, proj_ref, row, pair_lane(plan, channel), projected)
        return carry

    lax.fori_loop(0, steps, step, 0)
    order_copy.wait()
    project_depth(plan, proj_ref, depth_ref, order_ref, out_ref)


def twice_slope(scaled):
    shift = math.log2(2.0 / math.sqrt(math.pi))
    density = jnp.exp2(scaled * (scaled * -math.log2(math.e)) + shift)
    return (lax.erf(scaled) + 1.0) + scaled * density


def middle_kernel(
    plan,
    chunk,
    tile,
    rows_ref,
    point_hbm,
    cot_hbm,
    base_ref,
    base_t_ref,
    y_ref,
    y_t_ref,
    order_ref,
    order_t_ref,
    grad_hbm,
    out_ref,
    point_ref,
    cot_ref,
    grad_ref,
    depth_ref,
    depth_t_ref,
    iz_ref,
    proj_ref,
    point_sem,
    cot_sem,
    grad_sem,
):
    z = plan.width_z
    parts = plan.channels // chunk
    steps = plan.slab * parts
    point_copy = functools.partial(chunk_copy, point_hbm, point_ref, point_sem, chunk)
    cot_copy = functools.partial(chunk_copy, cot_hbm, cot_ref, cot_sem, chunk)
    grad_copy = functools.partial(chunk_copy, grad_ref, grad_hbm, grad_sem, chunk)
    for index in range(min(TWO_STREAMS, steps)):
        point_copy(index).start()
        cot_copy(index).start()
    spread_depth(plan, base_t_ref, depth_t_ref, 0)
    spread_depth(plan, base_ref, depth_ref, 1)
    restore_depth(plan, math.sqrt(0.5), rows_ref, depth_t_ref, order_t_ref, iz_ref)
    tiles = plan.rows_yt // tile

    def step(row, carry):
        def project(channel, start, stop):
            values = jnp.concatenate(
                [grad_ref[row, channel, start:stop], grad_ref[row, channel + 1, start:stop]],
                axis=1,
            )
            return dot(y_ref[:, start:stop], values)

        def store(channel, values):
            store_projection(plan, proj_ref, row, channel * z, values.astype(BF16))

        half_rows = plan.rows_yt // 2
        for channel in range(0, plan.channels, 2):
            if channel % chunk == 0:
                index = row * parts + channel // chunk
                point_copy(index).wait()
                cot_copy(index).wait()
                run_ahead(point_copy, TWO_STREAMS, index, steps)
                run_ahead(cot_copy, TWO_STREAMS, index, steps)
            coefficients = iz_ref[row, :, channel * z : (channel + 2) * z]
            projected = None
            for place in range(tiles):
                span = slice(place * tile, (place + 1) * tile)
                spectral = dot(y_t_ref[span], coefficients)
                for half in range(2):
                    scaled = spectral[:, half * z : (half + 1) * z]
                    scaled = scaled + point_ref[row, channel + half, span].astype(F32)
                    grad = cot_ref[row, channel + half, span].astype(F32) * twice_slope(scaled)
                    grad_ref[row, channel + half, span] = grad.astype(BF16)
                if channel and place == tiles // 2 - 1:
                    projected = project(channel - 2, 0, half_rows)
            if channel:
                projected = projected + project(channel - 2, half_rows, 2 * half_rows)
                store(channel - 2, projected)
            if (channel + 2) % chunk == 0:
                grad_copy(row * parts + channel // chunk).start()
        store(plan.channels - 2, project(plan.channels - 2, 0, plan.rows_yt))
        return carry

    lax.fori_loop(0, plan.slab, step, 0)
    project_depth(plan, proj_ref, depth_ref, order_ref, out_ref)
    for index in range(steps):
        grad_copy(index).wait()


def final_kernel(
    plan,
    chunk,
    tile,
    scale,
    rows_ref,
    point_hbm,
    base_t_ref,
    y_t_ref,
    order_t_ref,
    out_hbm,
    sum_ref,
    point_ref,
    out_ref,
    depth_t_ref,
    iz_ref,
    point_sem,
    out_sem,
):
    z = plan.width_z
    steps = plan.slab * plan.channels // chunk
    copy = functools.partial(chunk_copy, point_hbm, point_ref, point_sem, chunk)
    for index in range(min(ONE_STREAM, steps)):
        copy(index).start()
    sum_ref[...] = unpack_sums(plan, rows_ref) * scale
    spread_depth(plan, base_t_ref, depth_t_ref, 0)
    restore_depth(plan, 1.0, rows_ref, depth_t_ref, order_t_ref, iz_ref)

    def step(index, carry):
        copy(index).wait()
        run_ahead(copy, ONE_STREAM, index, steps)
        row, first = chunk_place(plan, chunk, index)
        for pair in range(chunk // 2):
            channel = first + 2 * pair
            coefficients = iz_ref[row, :, pl.ds(pair_lane(plan, channel), 2 * z)]
            for start in range(0, plan.rows_yt, tile):
                span = slice(start, start + tile)
                spectral = dot(y_t_ref[span], coefficients)
                for half in range(2):
                    total = spectral[:, half * z : (half + 1) * z]
                    total = total + point_ref[row, channel + half, span].astype(F32)
                    out_ref[row, channel + half, span] = total.astype(BF16)
        chunk_copy(out_ref, out_hbm, out_sem, chunk, index).start()
        return carry

    lax.fori_loop(0, steps, step, 0)
    for index in range(steps):
        chunk_copy(out_ref, out_hbm, out_sem, chunk, index).wait()


def pack_rows(plan):
    return 2 * plan.slab


def pack_sums(plan, sums):
    rows = pack_rows(plan)
    count = -(-plan.channels // rows)
    high = sums.astype(BF16)
    low = (sums - high.astype(F32)).astype(BF16)
    pieces = []
    for part in (high.astype(F32), low.astype(F32)):
        spare = count * rows - plan.channels
        if spare:
            part = jnp.concatenate([part, jnp.zeros((spare, plan.channels), F32)], axis=0)
        pieces += [part[index * rows : (index + 1) * rows] for index in range(count)]
    used = 2 * count * plan.channels
    pieces.append(jnp.zeros((rows, plan.extra - used), F32))
    block = jnp.concatenate(pieces, axis=1)
    return jnp.concatenate([block] * plan.devices, axis=0).astype(BF16)


def unpack_sums(plan, rows_ref):
    rows = pack_rows(plan)
    count = -(-plan.channels // rows)
    block = jnp.zeros((rows, plan.extra), F32)
    values = rows_ref[:, plan.lanes : plan.lanes + plan.extra].astype(F32)
    for device in range(plan.devices):
        block = block + values[device * rows : (device + 1) * rows]
    width = plan.channels
    parts = []
    for index in range(count):
        high = block[:, index * width : (index + 1) * width]
        low = block[:, (count + index) * width : (count + index + 1) * width]
        parts.append(high + low)
    return jnp.concatenate(parts, axis=0)[: plan.channels]


def row_copy(source, target, sem, tile, index):
    parts = source.shape[2] // tile
    place = (index // parts, slice(None), pl.ds(lax.rem(index, parts) * tile, tile))
    return pltpu.make_async_copy(source.at[place], target.at[place], sem.at[index])


def row_block(ref, row, start, count):
    channels, z = ref.shape[1], ref.shape[3]
    parts = []
    for index in range(count):
        values = ref[row, :, pl.ds(start + index * TILE_ROWS, TILE_ROWS), :].astype(F32)
        for first in range(0, TILE_ROWS, ROW_GROUP):
            group = values[:, first : first + ROW_GROUP, :]
            parts.append(group.reshape(channels * ROW_GROUP, z).astype(BF16))
    return jnp.concatenate(parts, axis=1)


def spread_weight(side, weight_ref, same_ref, fold_ref, fold_t_ref, spread_ref):
    tall = lax.dot_general(
        fold_t_ref[...],
        weight_ref[...],
        (((1,), (side,)), ((), ())),
        preferred_element_type=F32,
    ).astype(BF16)
    spread_ref[...] = (dot(tall, fold_ref[...]) * same_ref[...]).astype(BF16)


def mix_rows(spread_ref, u_ref, out_ref, row, base, tile, scale):
    channels, z = u_ref.shape[1], u_ref.shape[3]
    for start in range(0, tile, TILE_ROWS):
        mixed = dot(spread_ref[...], row_block(u_ref, row, base + start, 1)) * scale
        groups = [
            mixed[:, first : first + z].reshape(channels, ROW_GROUP, z)
            for first in range(0, mixed.shape[1], z)
        ]
        values = jnp.concatenate(groups, axis=1).astype(BF16)
        out_ref[row, :, pl.ds(base + start, TILE_ROWS), :] = values


def point_kernel(
    tile, side, scale, head, weight_ref, same_ref, fold_ref, fold_t_ref, u_hbm, *rest
):
    out_hbm, u_ref, out_ref, spread_ref, u_sem, out_sem = rest[-6:]
    parts = u_hbm.shape[2] // tile
    steps = u_hbm.shape[0] * parts
    copy = functools.partial(row_copy, u_hbm, u_ref, u_sem, tile)
    for index in range(head, min(head + ONE_STREAM, steps)):
        copy(index).start()
    spread_weight(side, weight_ref, same_ref, fold_ref, fold_t_ref, spread_ref)

    def step(index, carry):
        copy(index).wait()
        run_ahead(copy, ONE_STREAM, index, steps)
        base = pl.multiple_of(lax.rem(index, parts) * tile, tile)
        mix_rows(spread_ref, u_ref, out_ref, index // parts, base, tile, scale)
        row_copy(out_ref, out_hbm, out_sem, tile, index).start()
        return carry

    lax.fori_loop(head, steps, step, 0)
    for index in range(head, steps):
        row_copy(out_ref, out_hbm, out_sem, tile, index).wait()


def point_sum_kernel(
    tile,
    head,
    mix_scale,
    u_hbm,
    g_hbm,
    weight_ref,
    same_ref,
    fold_ref,
    fold_b_ref,
    fold_b_t_ref,
    sum_ref,
    out_hbm,
    u_ref,
    g_ref,
    out_ref,
    spread_ref,
    total_ref,
    u_sem,
    g_sem,
    out_sem,
):
    parts = u_hbm.shape[2] // tile
    steps = u_hbm.shape[0] * parts
    u_copy = functools.partial(row_copy, u_hbm, u_ref, u_sem, tile)
    g_copy = functools.partial(row_copy, g_hbm, g_ref, g_sem, tile)
    out_copy = functools.partial(row_copy, out_ref, out_hbm, out_sem, tile)
    for index in range(min(TWO_STREAMS, steps)):
        u_copy(index).start()
        g_copy(index).start()
    spread_weight(0, weight_ref, same_ref, fold_b_ref, fold_b_t_ref, spread_ref)
    total_ref[...] = jnp.zeros_like(total_ref)

    def step(index, carry):
        u_copy(index).wait()
        g_copy(index).wait()
        run_ahead(u_copy, TWO_STREAMS, index, steps)
        run_ahead(g_copy, TWO_STREAMS, index, steps)
        row = index // parts
        base = pl.multiple_of(lax.rem(index, parts) * tile, tile)

        @pl.when(index < head)
        def _():
            mix_rows(spread_ref, g_ref, out_ref, row, base, tile, mix_scale)
            out_copy(index).start()

        for start in range(0, tile, 4 * TILE_ROWS):
            total_ref[...] += lax.dot_general(
                row_block(u_ref, row, base + start, 4),
                row_block(g_ref, row, base + start, 4),
                (((1,), (1,)), ((), ())),
                preferred_element_type=F32,
            )
        return carry

    lax.fori_loop(0, steps, step, 0)
    for index in range(head):
        out_copy(index).wait()
    kept = total_ref[...] * same_ref[...]
    folded = jnp.dot(
        fold_ref[...], kept, precision=lax.Precision.HIGHEST, preferred_element_type=F32
    )
    sum_ref[...] = lax.dot_general(
        folded,
        fold_ref[...],
        (((1,), (1,)), ((), ())),
        precision=lax.Precision.HIGHEST,
        preferred_element_type=F32,
    )


def mix_kernel(plan, adjoint, step, rows_ref, weight_in, x_ref, x_t_ref, *rest):
    if adjoint:
        sums_ref, *rest = rest
    modes_ref, out_ref, mixed_ref, weight_ref, weight_sem = rest
    steps = plan.channels // step

    def copy(index):
        part = pl.ds(index * step, step)
        place = (part,) if adjoint else (slice(None), part)
        return pltpu.make_async_copy(
            weight_in.at[place], weight_ref.at[place], weight_sem.at[index]
        )

    for index in range(min(WEIGHT_STREAM, steps)):
        copy(index).start()
    modes = dot(x_ref[...], rows_ref[...])
    for channel in range(plan.channels):
        pieces = []
        for index in range(plan.owned_units):
            lane = index * plan.unit_lanes + channel * plan.unit
            pieces.append(modes[:, lane : lane + plan.unit])
        joined = jnp.concatenate(pieces, axis=1)
        for part in range(2):
            modes_ref[channel, part] = joined[part * KX : (part + 1) * KX]

    def mix_one(index):
        real = jnp.zeros((KX, plan.owned), F32)
        imag = jnp.zeros((KX, plan.owned), F32)
        for channel in range(plan.channels):
            place = (index, channel) if adjoint else (channel, index)
            weight_real = weight_ref[place + (0,)].astype(F32)
            weight_imag = weight_ref[place + (1,)].astype(F32)
            mode_real = modes_ref[channel, 0]
            mode_imag = modes_ref[channel, 1]
            if adjoint:
                real += weight_real * mode_real + weight_imag * mode_imag
                imag += weight_real * mode_imag - weight_imag * mode_real
            else:
                real += weight_real * mode_real - weight_imag * mode_imag
                imag += weight_real * mode_imag + weight_imag * mode_real
        mixed_ref[index, 0] = real
        mixed_ref[index, 1] = imag

    def mix_step(index, carry):
        copy(index).wait()
        run_ahead(copy, WEIGHT_STREAM, index, steps)
        for part in range(step):
            mix_one(index * step + part)
        return carry

    lax.fori_loop(0, steps, mix_step, 0)
    for index in range(plan.owned_units):
        span = slice(index * plan.unit, (index + 1) * plan.unit)
        halves = []
        for part in range(2):
            pieces = [mixed_ref[channel, part][:, span] for channel in range(plan.channels)]
            spare = plan.unit_lanes - plan.channels * plan.unit
            if spare:
                pieces.append(jnp.zeros((KX, spare), F32))
            halves.append(jnp.concatenate(pieces, axis=1))
        columns = jnp.concatenate(halves, axis=0).astype(BF16)
        lanes = slice(index * plan.unit_lanes, (index + 1) * plan.unit_lanes)
        out_ref[:, lanes] = dot(x_t_ref[...], columns).astype(BF16)
    if adjoint:
        out_ref[:, plan.lanes :] = pack_sums(plan, sums_ref[...])


def weight_grad_kernel(block, channels, modes_ref, grads_ref, out_ref):
    for index in range(block):
        mode_real = modes_ref[index, 0]
        mode_imag = modes_ref[index, 1]
        for channel in range(channels):
            grad_real = grads_ref[channel, 0]
            grad_imag = grads_ref[channel, 1]
            out_ref[index, channel, 0] = grad_real * mode_real + grad_imag * mode_imag
            out_ref[index, channel, 1] = grad_imag * mode_real - grad_real * mode_imag


def whole(shape):
    return pl.BlockSpec(shape, lambda *_: (0,) * len(shape))


def params(mebibytes):
    return pltpu.CompilerParams(vmem_limit_bytes=mebibytes * MIB)


def cost(flops, moved, transcendentals=0):
    return pl.CostEstimate(
        flops=int(flops), bytes_accessed=int(moved), transcendentals=int(transcendentals)
    )


def shards(devices, plume_state, out_cotangent, spectral_weight, pointwise_weight):
    slab, channels, width_y, width_t, width_z = plume_state.shape
    plan = Plan(slab, channels, width_y, width_z, devices)
    rows = plan.rows_yt
    chunk = 10 if channels % 10 == 0 else channels
    steps = slab * (channels // chunk)
    flat = (slab, channels, rows, width_z)
    state = plume_state.reshape(flat)
    cotangent = out_cotangent.reshape(flat)
    field_bytes = 2 * math.prod(flat)
    exchanged = (devices * slab * 2, plan.lanes)
    exchanged_back = (devices * slab * 2, plan.lanes + plan.extra)

    y_table = jnp.asarray(plan.y_table())
    y_table_t = jnp.asarray(np.ascontiguousarray(plan.y_table().T))
    base = jnp.asarray(plan.depth_base())
    base_t = jnp.asarray(np.ascontiguousarray(plan.depth_base().T))
    order = jnp.asarray(plan.order())
    order_t = jnp.asarray(np.ascontiguousarray(plan.order().T))
    x_table = jnp.asarray(plan.x_table())
    x_table_half = jnp.asarray((plan.x_table().astype(np.float32) * 0.5).astype(ml_dtypes.bfloat16))
    x_table_t = jnp.asarray(np.ascontiguousarray(plan.x_table().T))

    hbm = pl.BlockSpec(memory_space=pl.ANY)
    vmem = pl.BlockSpec(memory_space=pltpu.VMEM)
    field_shape = jax.ShapeDtypeStruct(flat, BF16)
    field = pltpu.VMEM(flat, BF16)
    proj_shape = pltpu.VMEM((plan.kinds, slab * plan.kind_rows, channels * width_z), BF16)
    iz_shape = pltpu.VMEM((slab, plan.kinds * plan.kind_rows, channels * width_z), BF16)
    depth_shape = pltpu.VMEM((channels * width_z, base.shape[1]), BF16)
    depth_t_shape = pltpu.VMEM((base.shape[1], channels * width_z), BF16)
    transform_flops = 2 * math.prod(flat) * 96 * 2
    mode_shape = (channels, 2, KX, plan.owned)

    def sems(count):
        return pltpu.SemaphoreType.DMA((count,))

    def exchange(values):
        blocks = values.reshape(devices, slab * 2, values.shape[1])
        moved = lax.all_to_all(blocks, "gx", split_axis=0, concat_axis=0, tiled=True)
        return moved.reshape(values.shape)

    def mix(adjoint, moved, weight, *sums):
        sent = exchanged_back if adjoint else exchanged
        step = 2 if channels % 2 == 0 else channels
        scratch = [
            pltpu.VMEM(mode_shape, F32),
            pltpu.VMEM(weight.shape, BF16),
            sems(channels // step),
        ]
        return pl.pallas_call(
            functools.partial(mix_kernel, plan, adjoint, step),
            in_specs=[vmem, hbm] + [vmem] * (2 + len(sums)),
            out_specs=[vmem, vmem],
            out_shape=[
                jax.ShapeDtypeStruct(mode_shape, F32),
                jax.ShapeDtypeStruct(sent, BF16),
            ],
            scratch_shapes=scratch,
            compiler_params=params(53),
            cost_estimate=cost(8 * 864 * 400, 5e6),
            name="mix_back" if adjoint else "mix_modes",
        )(moved, weight, x_table_half if adjoint else x_table, x_table_t, *sums)

    sent = pl.pallas_call(
        functools.partial(forward_kernel, plan, chunk),
        in_specs=[hbm, hbm, hbm, hbm],
        out_specs=vmem,
        out_shape=jax.ShapeDtypeStruct(exchanged, BF16),
        scratch_shapes=[
            pltpu.VMEM(base.shape, BF16),
            pltpu.VMEM(y_table.shape, BF16),
            pltpu.VMEM(order.shape, BF16),
            field,
            depth_shape,
            proj_shape,
            sems(3),
            sems(steps),
        ],
        compiler_params=params(58),
        cost_estimate=cost(transform_flops, field_bytes),
        name="forward_rows",
    )(state, base, y_table, order)
    moved = exchange(sent)

    spread = channels * ROW_GROUP
    same = np.kron(np.ones((channels, channels)), np.eye(ROW_GROUP)).astype(np.float32)
    same = jnp.asarray(same)
    fold_rows = np.kron(np.eye(channels), np.ones((1, ROW_GROUP)))
    fold = jnp.asarray(fold_rows.astype(np.float32))
    fold_b = jnp.asarray(rounded(fold_rows))
    fold_b_t = jnp.asarray(rounded(np.ascontiguousarray(fold_rows.T)))
    tile = min(256, rows)
    row_steps = slab * (rows // tile)
    mixing_flops = 2 * math.prod(flat) * spread

    modes, mixed_rows = mix(False, moved, spectral_weight)
    later_state, mixed_rows = lax.optimization_barrier((state, mixed_rows))
    spread_shape = pltpu.VMEM((spread, spread), BF16)

    def point(side, scale, head, name, values, *begun):
        return pl.pallas_call(
            functools.partial(point_kernel, tile, side, scale, head),
            in_specs=[vmem] * 4 + [hbm] * (1 + len(begun)),
            out_specs=hbm,
            out_shape=field_shape,
            scratch_shapes=[field, field, spread_shape, sems(row_steps), sems(row_steps)],
            input_output_aliases={5: 0} if begun else {},
            compiler_params=params(FIELD_MIB),
            cost_estimate=cost(mixing_flops, 2 * field_bytes),
            name=name,
        )(pointwise_weight, same, fold_b, fold_b_t, values, *begun)

    point_state = point(1, math.sqrt(0.5), 0, "point_mix", later_state)

    restored = exchange(mixed_rows)

    slope_tile = min(128, rows)
    grad_pre, grad_rows = pl.pallas_call(
        functools.partial(middle_kernel, plan, chunk, slope_tile),
        in_specs=[vmem, hbm, hbm] + [vmem] * 6,
        out_specs=[hbm, vmem],
        out_shape=[field_shape, jax.ShapeDtypeStruct(exchanged, BF16)],
        scratch_shapes=[field, field, field, depth_shape, depth_t_shape, iz_shape, proj_shape]
        + [sems(steps)] * 3,
        compiler_params=params(FIELD_MIB),
        cost_estimate=cost(2 * transform_flops, 3 * field_bytes, 2 * math.prod(flat)),
        name="activation_grad",
    )(restored, point_state, cotangent, base, base_t, y_table, y_table_t, order, order_t)

    grad_moved = exchange(grad_rows)

    head = max(1, row_steps // 4)
    sums, begun_back = pl.pallas_call(
        functools.partial(point_sum_kernel, tile, head, 0.5),
        in_specs=[hbm, hbm] + [vmem] * 5,
        out_specs=[vmem, hbm],
        out_shape=[jax.ShapeDtypeStruct((channels, channels), F32), field_shape],
        scratch_shapes=[field, field, field, spread_shape, pltpu.VMEM((spread, spread), F32)]
        + [sems(row_steps)] * 3,
        compiler_params=params(FIELD_MIB),
        cost_estimate=cost(mixing_flops, 2 * field_bytes),
        name="point_sum",
    )(state, grad_pre, pointwise_weight, same, fold, fold_b, fold_b_t)

    grad_modes, back_rows = mix(True, grad_moved, spectral_weight, sums)
    back_moved = exchange(back_rows)

    later_grad, grad_modes = lax.optimization_barrier((grad_pre, grad_modes))
    point_back = point(0, 0.5, head, "point_back", later_grad, begun_back)

    grad_shape = (channels, channels, 2, KX, plan.owned)
    block = 5 if channels % 5 == 0 else 1
    spectral_grad = pl.pallas_call(
        functools.partial(weight_grad_kernel, block, channels),
        grid=(channels // block,),
        in_specs=[
            pl.BlockSpec((block,) + mode_shape[1:], lambda i: (i, 0, 0, 0)),
            whole(mode_shape),
        ],
        out_specs=pl.BlockSpec((block,) + grad_shape[1:], lambda i: (i, 0, 0, 0, 0)),
        out_shape=jax.ShapeDtypeStruct(grad_shape, F32),
        compiler_params=params(14),
        cost_estimate=cost(6 * 864 * 400, 1e7),
        name="weight_grad",
    )(modes, grad_modes)

    scale = 0.5 / math.sqrt(plan.width_x * width_y * width_t * width_z)
    state_grad, pointwise_grad = pl.pallas_call(
        functools.partial(final_kernel, plan, chunk, slope_tile, scale),
        in_specs=[vmem, hbm, vmem, vmem, vmem],
        out_specs=[hbm, vmem],
        out_shape=[field_shape, jax.ShapeDtypeStruct((channels, channels), F32)],
        scratch_shapes=[field, field, depth_t_shape, iz_shape] + [sems(steps)] * 2,
        compiler_params=params(FIELD_MIB),
        cost_estimate=cost(transform_flops, 2 * field_bytes),
        name="state_grad",
    )(back_moved, point_back, base_t, y_table_t, order_t)
    return (state_grad.reshape(plume_state.shape), spectral_grad, pointwise_grad)


def solution(mesh):
    placed = (
        P(("groups", "gx"), None, None, None, None),
        P(("groups", "gx"), None, None, None, None),
        P(None, None, None, None, "gx"),
        P(),
    )
    return jax.shard_map(
        functools.partial(shards, mesh.shape["gx"]),
        mesh=mesh,
        in_specs=placed,
        out_specs=(
            P(("groups", "gx"), None, None, None, None),
            P("groups", None, None, None, "gx"),
            P("groups", None),
        ),
        check_vma=False,
    )
```

```python
import functools
import math

import jax
import jax.numpy as jnp
import ml_dtypes
import numpy as np
from jax import lax
from jax.experimental import pallas as pl
from jax.experimental.pallas import tpu as pltpu
from jax.sharding import PartitionSpec as P

KX = 24
KY = 24
KZ = 24
NT = 2
ROW_GROUP = 8
TILE_ROWS = 16
BF16 = jnp.bfloat16
F32 = jnp.float32
FIELD_MIB = 51
ONE_STREAM = 3
TWO_STREAMS = 3
WEIGHT_STREAM = 8
MIB = 1024 * 1024


def rounded(table):
    return np.asarray(table, np.float64).astype(np.float32).astype(ml_dtypes.bfloat16)


def wave_tables(cells, kept):
    frequency = np.arange(kept) - kept // 2
    angle = 2.0 * np.pi / cells * (frequency[:, None] * np.arange(cells)[None, :] % cells)
    return np.cos(angle) / math.sqrt(cells), np.sin(angle) / math.sqrt(cells)


def depth_table(cells, kept):
    column = np.arange(kept)
    half = kept // 2
    frequency = np.where(column < half, column, column - half + 1)
    angle = 2.0 * np.pi / cells * (np.arange(cells)[:, None] * frequency[None, :] % cells)
    wave = np.where(column[None, :] < half, np.cos(angle), np.sin(angle))
    return wave * math.sqrt(2.0 / cells) * math.sqrt(0.5)


class Plan:
    def __init__(self, slab, channels, width_y, width_z, devices):
        self.slab = slab
        self.channels = channels
        self.width_y = width_y
        self.width_z = width_z
        self.devices = devices
        self.width_x = slab * devices
        self.pairs = KY * NT
        self.owned = self.pairs * KZ // devices
        self.kinds = 3
        self.owners = self.kinds * KZ // self.owned
        self.periods = self.pairs // self.kinds
        self.unit = math.gcd(self.owned, KZ)
        self.units = KZ // self.unit
        self.owned_units = self.owned // self.unit
        self.unit_lanes = 128 * -(-channels * self.unit // 128)
        self.lanes = self.unit_lanes * self.owned_units
        self.rows_yt = width_y * NT
        self.kind_rows = self.periods * 2
        sums = 2 * channels * -(-channels // (2 * slab))
        self.extra = 128 * -(-sums // 128)

    def y_table(self):
        cosine, sine = wave_tables(self.width_y, KY)
        both = np.stack([cosine, -sine])
        table = np.zeros((self.kinds, self.periods, 2, self.width_y, NT))
        for kind in range(self.kinds):
            for period in range(self.periods):
                pair = self.kinds * period + kind
                for time in range(NT):
                    sign = -1.0 if (time % 2 and pair % 2) else 1.0
                    table[kind, period, :, :, time] = sign * both[:, pair // 2]
        return rounded(table.reshape(self.kinds * self.kind_rows, self.rows_yt))

    def depth_base(self):
        values = depth_table(self.width_z, KZ).reshape(self.width_z, self.units, self.unit)
        table = np.zeros((self.width_z, self.units, self.unit_lanes))
        used = self.channels * self.unit
        table[:, :, :used] = np.tile(values, (1, 1, self.channels))
        return rounded(table.reshape(self.width_z, self.units * self.unit_lanes))

    def order(self):
        total = self.devices * self.slab * 2
        source = np.arange(total).reshape(self.owners, self.slab, self.periods, 2)
        source = source.transpose(2, 0, 1, 3).reshape(total)
        table = np.zeros((total, total))
        table[np.arange(total), source] = 1.0
        return rounded(table)

    def x_table(self):
        cosine, sine = wave_tables(self.width_x, KX)
        table = np.zeros((2, KX, self.width_x, 2))
        table[0, :, :, 0] = cosine
        table[0, :, :, 1] = sine
        table[1, :, :, 1] = cosine
        table[1, :, :, 0] = -sine
        return rounded(table.reshape(2 * KX, self.width_x * 2))


def dot(left, right):
    return jnp.dot(left, right, preferred_element_type=F32)


def channel_place(plan, axis):
    count = plan.units * plan.unit_lanes
    shape = (plan.width_z, count) if axis == 1 else (count, plan.width_z)
    return lax.rem(lax.broadcasted_iota(jnp.int32, shape, axis), plan.unit_lanes)


def spread_depth(plan, base_ref, depth_ref, axis):
    place = channel_place(plan, axis)
    base = base_ref[...].astype(F32)
    for channel in range(plan.channels):
        start = channel * plan.unit
        own = (place >= start) & (place < start + plan.unit)
        block = jnp.where(own, base, 0.0).astype(BF16)
        span = slice(channel * plan.width_z, (channel + 1) * plan.width_z)
        if axis == 1:
            depth_ref[span, :] = block
        else:
            depth_ref[:, span] = block


def project_depth(plan, proj_ref, depth_ref, order_ref, out_ref):
    rows = plan.slab * plan.kind_rows
    lanes = plan.unit_lanes
    flat = proj_ref[...].reshape(plan.kinds * rows, plan.channels * plan.width_z)
    parts = dot(flat, depth_ref[...]).astype(BF16)
    owners = []
    for owner in range(plan.owners):
        pieces = []
        for index in range(plan.owned_units):
            kind, unit = divmod(owner * plan.owned_units + index, plan.units)
            pieces.append(
                parts[kind * rows : (kind + 1) * rows, unit * lanes : (unit + 1) * lanes]
            )
        owners.append(jnp.concatenate(pieces, axis=1))
    joined = jnp.concatenate(owners, axis=0)
    out_ref[...] = dot(order_ref[...], joined).astype(BF16)


def restore_depth(plan, scale, rows_ref, depth_t_ref, order_t_ref, iz_ref):
    block = plan.slab * plan.kind_rows
    lanes = plan.unit_lanes
    rows = dot(order_t_ref[...], rows_ref[:, : plan.lanes]).astype(BF16)
    kinds = []
    for kind in range(plan.kinds):
        pieces = []
        for unit in range(plan.units):
            owner, index = divmod(kind * plan.units + unit, plan.owned_units)
            pieces.append(
                rows[owner * block : (owner + 1) * block, index * lanes : (index + 1) * lanes]
            )
        kinds.append(jnp.concatenate(pieces, axis=1))
    joined = jnp.concatenate(kinds, axis=0)
    total = depth_t_ref.shape[1]
    width = min(total, 512)
    for start in range(0, total, width):
        stop = min(total, start + width)
        values = dot(joined, depth_t_ref[:, start:stop])
        if scale != 1.0:
            values = values * scale
        values = values.astype(BF16)
        for kind in range(plan.kinds):
            for row in range(plan.slab):
                first = (kind * plan.slab + row) * plan.kind_rows
                iz_ref[
                    row, kind * plan.kind_rows : (kind + 1) * plan.kind_rows, start:stop
                ] = values[first : first + plan.kind_rows]


def store_projection(plan, proj_ref, row, lane, values):
    for kind in range(plan.kinds):
        proj_ref[
            kind,
            pl.ds(pl.multiple_of(row * plan.kind_rows, plan.kind_rows), plan.kind_rows),
            pl.ds(lane, values.shape[1]),
        ] = values[kind * plan.kind_rows : (kind + 1) * plan.kind_rows]


def chunk_copy(source, target, sem, chunk, index):
    parts = source.shape[1] // chunk
    place = (index // parts, pl.ds(lax.rem(index, parts) * chunk, chunk))
    return pltpu.make_async_copy(source.at[place], target.at[place], sem.at[index])


def run_ahead(copy, ahead, index, steps):
    @pl.when(index + ahead < steps)
    def _():
        copy(index + ahead).start()


def chunk_place(plan, chunk, index):
    parts = plan.channels // chunk
    return index // parts, lax.rem(index, parts) * chunk


def pair_lane(plan, channel):
    return pl.multiple_of(channel * plan.width_z, 2 * plan.width_z)


def forward_kernel(
    plan,
    chunk,
    u_hbm,
    base_hbm,
    y_hbm,
    order_hbm,
    out_ref,
    base_ref,
    y_ref,
    order_ref,
    u_ref,
    depth_ref,
    proj_ref,
    table_sem,
    u_sem,
):
    steps = plan.slab * plan.channels // chunk
    copy = functools.partial(chunk_copy, u_hbm, u_ref, u_sem, chunk)
    y_copy, base_copy, order_copy = [
        pltpu.make_async_copy(source, target, table_sem.at[index])
        for index, (source, target) in enumerate(
            ((y_hbm, y_ref), (base_hbm, base_ref), (order_hbm, order_ref))
        )
    ]
    y_copy.start()
    for index in range(min(ONE_STREAM, steps)):
        copy(index).start()
    base_copy.start()
    order_copy.start()
    y_copy.wait()

    def step(index, carry):
        copy(index).wait()
        run_ahead(copy, ONE_STREAM, index, steps)

        @pl.when(index == steps // 2)
        def _():
            base_copy.wait()
            spread_depth(plan, base_ref, depth_ref, 1)

        row, first = chunk_place(plan, chunk, index)
        for pair in range(chunk // 2):
            channel = first + 2 * pair
            values = jnp.concatenate([u_ref[row, channel], u_ref[row, channel + 1]], axis=1)
            projected = dot(y_ref[...], values).astype(BF16)
            store_projection(plan, proj_ref, row, pair_lane(plan, channel), projected)
        return carry

    lax.fori_loop(0, steps, step, 0)
    order_copy.wait()
    project_depth(plan, proj_ref, depth_ref, order_ref, out_ref)


def twice_slope(scaled):
    shift = math.log2(2.0 / math.sqrt(math.pi))
    density = jnp.exp2(scaled * (scaled * -math.log2(math.e)) + shift)
    return (lax.erf(scaled) + 1.0) + scaled * density


def middle_kernel(
    plan,
    chunk,
    tile,
    rows_ref,
    point_hbm,
    cot_hbm,
    base_ref,
    base_t_ref,
    y_ref,
    y_t_ref,
    order_ref,
    order_t_ref,
    grad_hbm,
    out_ref,
    point_ref,
    cot_ref,
    grad_ref,
    depth_ref,
    depth_t_ref,
    iz_ref,
    proj_ref,
    point_sem,
    cot_sem,
    grad_sem,
):
    z = plan.width_z
    parts = plan.channels // chunk
    steps = plan.slab * parts
    point_copy = functools.partial(chunk_copy, point_hbm, point_ref, point_sem, chunk)
    cot_copy = functools.partial(chunk_copy, cot_hbm, cot_ref, cot_sem, chunk)
    grad_copy = functools.partial(chunk_copy, grad_ref, grad_hbm, grad_sem, chunk)
    for index in range(min(TWO_STREAMS, steps)):
        point_copy(index).start()
        cot_copy(index).start()
    spread_depth(plan, base_t_ref, depth_t_ref, 0)
    spread_depth(plan, base_ref, depth_ref, 1)
    restore_depth(plan, math.sqrt(0.5), rows_ref, depth_t_ref, order_t_ref, iz_ref)
    tiles = plan.rows_yt // tile

    def step(row, carry):
        def project(channel, start, stop):
            values = jnp.concatenate(
                [grad_ref[row, channel, start:stop], grad_ref[row, channel + 1, start:stop]],
                axis=1,
            )
            return dot(y_ref[:, start:stop], values)

        def store(channel, values):
            store_projection(plan, proj_ref, row, channel * z, values.astype(BF16))

        half_rows = plan.rows_yt // 2
        for channel in range(0, plan.channels, 2):
            if channel % chunk == 0:
                index = row * parts + channel // chunk
                point_copy(index).wait()
                cot_copy(index).wait()
                run_ahead(point_copy, TWO_STREAMS, index, steps)
                run_ahead(cot_copy, TWO_STREAMS, index, steps)
            coefficients = iz_ref[row, :, channel * z : (channel + 2) * z]
            projected = None
            for place in range(tiles):
                span = slice(place * tile, (place + 1) * tile)
                spectral = dot(y_t_ref[span], coefficients)
                for half in range(2):
                    scaled = spectral[:, half * z : (half + 1) * z]
                    scaled = scaled + point_ref[row, channel + half, span].astype(F32)
                    grad = cot_ref[row, channel + half, span].astype(F32) * twice_slope(scaled)
                    grad_ref[row, channel + half, span] = grad.astype(BF16)
                if channel and place == tiles // 2 - 1:
                    projected = project(channel - 2, 0, half_rows)
            if channel:
                projected = projected + project(channel - 2, half_rows, 2 * half_rows)
                store(channel - 2, projected)
            if (channel + 2) % chunk == 0:
                grad_copy(row * parts + channel // chunk).start()
        store(plan.channels - 2, project(plan.channels - 2, 0, plan.rows_yt))
        return carry

    lax.fori_loop(0, plan.slab, step, 0)
    project_depth(plan, proj_ref, depth_ref, order_ref, out_ref)
    for index in range(steps):
        grad_copy(index).wait()


def final_kernel(
    plan,
    chunk,
    tile,
    scale,
    rows_ref,
    point_hbm,
    base_t_ref,
    y_t_ref,
    order_t_ref,
    out_hbm,
    sum_ref,
    point_ref,
    out_ref,
    depth_t_ref,
    iz_ref,
    point_sem,
    out_sem,
):
    z = plan.width_z
    steps = plan.slab * plan.channels // chunk
    copy = functools.partial(chunk_copy, point_hbm, point_ref, point_sem, chunk)
    for index in range(min(ONE_STREAM, steps)):
        copy(index).start()
    sum_ref[...] = unpack_sums(plan, rows_ref) * scale
    spread_depth(plan, base_t_ref, depth_t_ref, 0)
    restore_depth(plan, 1.0, rows_ref, depth_t_ref, order_t_ref, iz_ref)

    def step(index, carry):
        copy(index).wait()
        run_ahead(copy, ONE_STREAM, index, steps)
        row, first = chunk_place(plan, chunk, index)
        for pair in range(chunk // 2):
            channel = first + 2 * pair
            coefficients = iz_ref[row, :, pl.ds(pair_lane(plan, channel), 2 * z)]
            for start in range(0, plan.rows_yt, tile):
                span = slice(start, start + tile)
                spectral = dot(y_t_ref[span], coefficients)
                for half in range(2):
                    total = spectral[:, half * z : (half + 1) * z]
                    total = total + point_ref[row, channel + half, span].astype(F32)
                    out_ref[row, channel + half, span] = total.astype(BF16)
        chunk_copy(out_ref, out_hbm, out_sem, chunk, index).start()
        return carry

    lax.fori_loop(0, steps, step, 0)
    for index in range(steps):
        chunk_copy(out_ref, out_hbm, out_sem, chunk, index).wait()


def pack_rows(plan):
    return 2 * plan.slab


def pack_sums(plan, sums):
    rows = pack_rows(plan)
    count = -(-plan.channels // rows)
    high = sums.astype(BF16)
    low = (sums - high.astype(F32)).astype(BF16)
    pieces = []
    for part in (high.astype(F32), low.astype(F32)):
        spare = count * rows - plan.channels
        if spare:
            part = jnp.concatenate([part, jnp.zeros((spare, plan.channels), F32)], axis=0)
        pieces += [part[index * rows : (index + 1) * rows] for index in range(count)]
    used = 2 * count * plan.channels
    pieces.append(jnp.zeros((rows, plan.extra - used), F32))
    block = jnp.concatenate(pieces, axis=1)
    return jnp.concatenate([block] * plan.devices, axis=0).astype(BF16)


def unpack_sums(plan, rows_ref):
    rows = pack_rows(plan)
    count = -(-plan.channels // rows)
    block = jnp.zeros((rows, plan.extra), F32)
    values = rows_ref[:, plan.lanes : plan.lanes + plan.extra].astype(F32)
    for device in range(plan.devices):
        block = block + values[device * rows : (device + 1) * rows]
    width = plan.channels
    parts = []
    for index in range(count):
        high = block[:, index * width : (index + 1) * width]
        low = block[:, (count + index) * width : (count + index + 1) * width]
        parts.append(high + low)
    return jnp.concatenate(parts, axis=0)[: plan.channels]


def row_copy(source, target, sem, tile, index):
    parts = source.shape[2] // tile
    place = (index // parts, slice(None), pl.ds(lax.rem(index, parts) * tile, tile))
    return pltpu.make_async_copy(source.at[place], target.at[place], sem.at[index])


def row_block(ref, row, start, count):
    channels, z = ref.shape[1], ref.shape[3]
    parts = []
    for index in range(count):
        values = ref[row, :, pl.ds(start + index * TILE_ROWS, TILE_ROWS), :].astype(F32)
        for first in range(0, TILE_ROWS, ROW_GROUP):
            group = values[:, first : first + ROW_GROUP, :]
            parts.append(group.reshape(channels * ROW_GROUP, z).astype(BF16))
    return jnp.concatenate(parts, axis=1)


def spread_weight(side, weight_ref, same_ref, fold_ref, fold_t_ref, spread_ref):
    tall = lax.dot_general(
        fold_t_ref[...],
        weight_ref[...],
        (((1,), (side,)), ((), ())),
        preferred_element_type=F32,
    ).astype(BF16)
    spread_ref[...] = (dot(tall, fold_ref[...]) * same_ref[...]).astype(BF16)


def mix_rows(spread_ref, u_ref, out_ref, row, base, tile, scale):
    channels, z = u_ref.shape[1], u_ref.shape[3]
    for start in range(0, tile, TILE_ROWS):
        mixed = dot(spread_ref[...], row_block(u_ref, row, base + start, 1)) * scale
        groups = [
            mixed[:, first : first + z].reshape(channels, ROW_GROUP, z)
            for first in range(0, mixed.shape[1], z)
        ]
        values = jnp.concatenate(groups, axis=1).astype(BF16)
        out_ref[row, :, pl.ds(base + start, TILE_ROWS), :] = values


def point_kernel(
    tile, side, scale, head, weight_ref, same_ref, fold_ref, fold_t_ref, u_hbm, *rest
):
    out_hbm, u_ref, out_ref, spread_ref, u_sem, out_sem = rest[-6:]
    parts = u_hbm.shape[2] // tile
    steps = u_hbm.shape[0] * parts
    copy = functools.partial(row_copy, u_hbm, u_ref, u_sem, tile)
    for index in range(head, min(head + ONE_STREAM, steps)):
        copy(index).start()
    spread_weight(side, weight_ref, same_ref, fold_ref, fold_t_ref, spread_ref)

    def step(index, carry):
        copy(index).wait()
        run_ahead(copy, ONE_STREAM, index, steps)
        base = pl.multiple_of(lax.rem(index, parts) * tile, tile)
        mix_rows(spread_ref, u_ref, out_ref, index // parts, base, tile, scale)
        row_copy(out_ref, out_hbm, out_sem, tile, index).start()
        return carry

    lax.fori_loop(head, steps, step, 0)
    for index in range(head, steps):
        row_copy(out_ref, out_hbm, out_sem, tile, index).wait()


def point_sum_kernel(
    tile,
    head,
    mix_scale,
    u_hbm,
    g_hbm,
    weight_ref,
    same_ref,
    fold_ref,
    fold_b_ref,
    fold_b_t_ref,
    sum_ref,
    out_hbm,
    u_ref,
    g_ref,
    out_ref,
    spread_ref,
    total_ref,
    u_sem,
    g_sem,
    out_sem,
):
    parts = u_hbm.shape[2] // tile
    steps = u_hbm.shape[0] * parts
    u_copy = functools.partial(row_copy, u_hbm, u_ref, u_sem, tile)
    g_copy = functools.partial(row_copy, g_hbm, g_ref, g_sem, tile)
    out_copy = functools.partial(row_copy, out_ref, out_hbm, out_sem, tile)
    for index in range(min(TWO_STREAMS, steps)):
        u_copy(index).start()
        g_copy(index).start()
    spread_weight(0, weight_ref, same_ref, fold_b_ref, fold_b_t_ref, spread_ref)
    total_ref[...] = jnp.zeros_like(total_ref)

    def step(index, carry):
        u_copy(index).wait()
        g_copy(index).wait()
        run_ahead(u_copy, TWO_STREAMS, index, steps)
        run_ahead(g_copy, TWO_STREAMS, index, steps)
        row = index // parts
        base = pl.multiple_of(lax.rem(index, parts) * tile, tile)

        @pl.when(index < head)
        def _():
            mix_rows(spread_ref, g_ref, out_ref, row, base, tile, mix_scale)
            out_copy(index).start()

        for start in range(0, tile, 4 * TILE_ROWS):
            total_ref[...] += lax.dot_general(
                row_block(u_ref, row, base + start, 4),
                row_block(g_ref, row, base + start, 4),
                (((1,), (1,)), ((), ())),
                preferred_element_type=F32,
            )
        return carry

    lax.fori_loop(0, steps, step, 0)
    for index in range(head):
        out_copy(index).wait()
    kept = total_ref[...] * same_ref[...]
    folded = jnp.dot(
        fold_ref[...], kept, precision=lax.Precision.HIGHEST, preferred_element_type=F32
    )
    sum_ref[...] = lax.dot_general(
        folded,
        fold_ref[...],
        (((1,), (1,)), ((), ())),
        precision=lax.Precision.HIGHEST,
        preferred_element_type=F32,
    )


def mix_kernel(plan, adjoint, step, rows_ref, weight_in, x_ref, x_t_ref, *rest):
    if adjoint:
        sums_ref, *rest = rest
    modes_ref, out_ref, mixed_ref, weight_ref, weight_sem = rest
    steps = plan.channels // step

    def copy(index):
        part = pl.ds(index * step, step)
        place = (part,) if adjoint else (slice(None), part)
        return pltpu.make_async_copy(
            weight_in.at[place], weight_ref.at[place], weight_sem.at[index]
        )

    for index in range(min(WEIGHT_STREAM, steps)):
        copy(index).start()
    modes = dot(x_ref[...], rows_ref[...])
    for channel in range(plan.channels):
        pieces = []
        for index in range(plan.owned_units):
            lane = index * plan.unit_lanes + channel * plan.unit
            pieces.append(modes[:, lane : lane + plan.unit])
        joined = jnp.concatenate(pieces, axis=1)
        for part in range(2):
            modes_ref[channel, part] = joined[part * KX : (part + 1) * KX]

    def mix_one(index):
        real = jnp.zeros((KX, plan.owned), F32)
        imag = jnp.zeros((KX, plan.owned), F32)
        for channel in range(plan.channels):
            place = (index, channel) if adjoint else (channel, index)
            weight_real = weight_ref[place + (0,)].astype(F32)
            weight_imag = weight_ref[place + (1,)].astype(F32)
            mode_real = modes_ref[channel, 0]
            mode_imag = modes_ref[channel, 1]
            if adjoint:
                real += weight_real * mode_real + weight_imag * mode_imag
                imag += weight_real * mode_imag - weight_imag * mode_real
            else:
                real += weight_real * mode_real - weight_imag * mode_imag
                imag += weight_real * mode_imag + weight_imag * mode_real
        mixed_ref[index, 0] = real
        mixed_ref[index, 1] = imag

    def mix_step(index, carry):
        copy(index).wait()
        run_ahead(copy, WEIGHT_STREAM, index, steps)
        for part in range(step):
            mix_one(index * step + part)
        return carry

    lax.fori_loop(0, steps, mix_step, 0)
    for index in range(plan.owned_units):
        span = slice(index * plan.unit, (index + 1) * plan.unit)
        halves = []
        for part in range(2):
            pieces = [mixed_ref[channel, part][:, span] for channel in range(plan.channels)]
            spare = plan.unit_lanes - plan.channels * plan.unit
            if spare:
                pieces.append(jnp.zeros((KX, spare), F32))
            halves.append(jnp.concatenate(pieces, axis=1))
        columns = jnp.concatenate(halves, axis=0).astype(BF16)
        lanes = slice(index * plan.unit_lanes, (index + 1) * plan.unit_lanes)
        out_ref[:, lanes] = dot(x_t_ref[...], columns).astype(BF16)
    if adjoint:
        out_ref[:, plan.lanes :] = pack_sums(plan, sums_ref[...])


def weight_grad_kernel(block, channels, modes_ref, grads_ref, out_ref):
    for index in range(block):
        mode_real = modes_ref[index, 0]
        mode_imag = modes_ref[index, 1]
        for channel in range(channels):
            grad_real = grads_ref[channel, 0]
            grad_imag = grads_ref[channel, 1]
            out_ref[index, channel, 0] = grad_real * mode_real + grad_imag * mode_imag
            out_ref[index, channel, 1] = grad_imag * mode_real - grad_real * mode_imag


def whole(shape):
    return pl.BlockSpec(shape, lambda *_: (0,) * len(shape))


def params(mebibytes):
    return pltpu.CompilerParams(vmem_limit_bytes=mebibytes * MIB)


def cost(flops, moved, transcendentals=0):
    return pl.CostEstimate(
        flops=int(flops), bytes_accessed=int(moved), transcendentals=int(transcendentals)
    )


def shards(devices, plume_state, out_cotangent, spectral_weight, pointwise_weight):
    slab, channels, width_y, width_t, width_z = plume_state.shape
    plan = Plan(slab, channels, width_y, width_z, devices)
    rows = plan.rows_yt
    chunk = 10 if channels % 10 == 0 else channels
    steps = slab * (channels // chunk)
    flat = (slab, channels, rows, width_z)
    state = plume_state.reshape(flat)
    cotangent = out_cotangent.reshape(flat)
    field_bytes = 2 * math.prod(flat)
    exchanged = (devices * slab * 2, plan.lanes)
    exchanged_back = (devices * slab * 2, plan.lanes + plan.extra)

    y_table = jnp.asarray(plan.y_table())
    y_table_t = jnp.asarray(np.ascontiguousarray(plan.y_table().T))
    base = jnp.asarray(plan.depth_base())
    base_t = jnp.asarray(np.ascontiguousarray(plan.depth_base().T))
    order = jnp.asarray(plan.order())
    order_t = jnp.asarray(np.ascontiguousarray(plan.order().T))
    x_table = jnp.asarray(plan.x_table())
    x_table_half = jnp.asarray((plan.x_table().astype(np.float32) * 0.5).astype(ml_dtypes.bfloat16))
    x_table_t = jnp.asarray(np.ascontiguousarray(plan.x_table().T))

    hbm = pl.BlockSpec(memory_space=pl.ANY)
    vmem = pl.BlockSpec(memory_space=pltpu.VMEM)
    field_shape = jax.ShapeDtypeStruct(flat, BF16)
    field = pltpu.VMEM(flat, BF16)
    proj_shape = pltpu.VMEM((plan.kinds, slab * plan.kind_rows, channels * width_z), BF16)
    iz_shape = pltpu.VMEM((slab, plan.kinds * plan.kind_rows, channels * width_z), BF16)
    depth_shape = pltpu.VMEM((channels * width_z, base.shape[1]), BF16)
    depth_t_shape = pltpu.VMEM((base.shape[1], channels * width_z), BF16)
    transform_flops = 2 * math.prod(flat) * 96 * 2
    mode_shape = (channels, 2, KX, plan.owned)

    def sems(count):
        return pltpu.SemaphoreType.DMA((count,))

    def exchange(values):
        blocks = values.reshape(devices, slab * 2, values.shape[1])
        moved = lax.all_to_all(blocks, "gx", split_axis=0, concat_axis=0, tiled=True)
        return moved.reshape(values.shape)

    def mix(adjoint, moved, weight, *sums):
        sent = exchanged_back if adjoint else exchanged
        step = 4 if channels % 4 == 0 else channels
        scratch = [
            pltpu.VMEM(mode_shape, F32),
            pltpu.VMEM(weight.shape, BF16),
            sems(channels // step),
        ]
        return pl.pallas_call(
            functools.partial(mix_kernel, plan, adjoint, step),
            in_specs=[vmem, hbm] + [vmem] * (2 + len(sums)),
            out_specs=[vmem, vmem],
            out_shape=[
                jax.ShapeDtypeStruct(mode_shape, F32),
                jax.ShapeDtypeStruct(sent, BF16),
            ],
            scratch_shapes=scratch,
            compiler_params=params(53),
            cost_estimate=cost(8 * 864 * 400, 5e6),
            name="mix_back" if adjoint else "mix_modes",
        )(moved, weight, x_table_half if adjoint else x_table, x_table_t, *sums)

    sent = pl.pallas_call(
        functools.partial(forward_kernel, plan, chunk),
        in_specs=[hbm, hbm, hbm, hbm],
        out_specs=vmem,
        out_shape=jax.ShapeDtypeStruct(exchanged, BF16),
        scratch_shapes=[
            pltpu.VMEM(base.shape, BF16),
            pltpu.VMEM(y_table.shape, BF16),
            pltpu.VMEM(order.shape, BF16),
            field,
            depth_shape,
            proj_shape,
            sems(3),
            sems(steps),
        ],
        compiler_params=params(58),
        cost_estimate=cost(transform_flops, field_bytes),
        name="forward_rows",
    )(state, base, y_table, order)
    moved = exchange(sent)

    spread = channels * ROW_GROUP
    same = np.kron(np.ones((channels, channels)), np.eye(ROW_GROUP)).astype(np.float32)
    same = jnp.asarray(same)
    fold_rows = np.kron(np.eye(channels), np.ones((1, ROW_GROUP)))
    fold = jnp.asarray(fold_rows.astype(np.float32))
    fold_b = jnp.asarray(rounded(fold_rows))
    fold_b_t = jnp.asarray(rounded(np.ascontiguousarray(fold_rows.T)))
    tile = min(256, rows)
    row_steps = slab * (rows // tile)
    mixing_flops = 2 * math.prod(flat) * spread

    modes, mixed_rows = mix(False, moved, spectral_weight)
    later_state, mixed_rows = lax.optimization_barrier((state, mixed_rows))
    spread_shape = pltpu.VMEM((spread, spread), BF16)

    def point(side, scale, head, name, values, *begun):
        return pl.pallas_call(
            functools.partial(point_kernel, tile, side, scale, head),
            in_specs=[vmem] * 4 + [hbm] * (1 + len(begun)),
            out_specs=hbm,
            out_shape=field_shape,
            scratch_shapes=[field, field, spread_shape, sems(row_steps), sems(row_steps)],
            input_output_aliases={5: 0} if begun else {},
            compiler_params=params(FIELD_MIB),
            cost_estimate=cost(mixing_flops, 2 * field_bytes),
            name=name,
        )(pointwise_weight, same, fold_b, fold_b_t, values, *begun)

    point_state = point(1, math.sqrt(0.5), 0, "point_mix", later_state)

    restored = exchange(mixed_rows)

    slope_tile = min(128, rows)
    grad_pre, grad_rows = pl.pallas_call(
        functools.partial(middle_kernel, plan, chunk, slope_tile),
        in_specs=[vmem, hbm, hbm] + [vmem] * 6,
        out_specs=[hbm, vmem],
        out_shape=[field_shape, jax.ShapeDtypeStruct(exchanged, BF16)],
        scratch_shapes=[field, field, field, depth_shape, depth_t_shape, iz_shape, proj_shape]
        + [sems(steps)] * 3,
        compiler_params=params(FIELD_MIB),
        cost_estimate=cost(2 * transform_flops, 3 * field_bytes, 2 * math.prod(flat)),
        name="activation_grad",
    )(restored, point_state, cotangent, base, base_t, y_table, y_table_t, order, order_t)

    grad_moved = exchange(grad_rows)

    head = max(1, row_steps // 4)
    sums, begun_back = pl.pallas_call(
        functools.partial(point_sum_kernel, tile, head, 0.5),
        in_specs=[hbm, hbm] + [vmem] * 5,
        out_specs=[vmem, hbm],
        out_shape=[jax.ShapeDtypeStruct((channels, channels), F32), field_shape],
        scratch_shapes=[field, field, field, spread_shape, pltpu.VMEM((spread, spread), F32)]
        + [sems(row_steps)] * 3,
        compiler_params=params(FIELD_MIB),
        cost_estimate=cost(mixing_flops, 2 * field_bytes),
        name="point_sum",
    )(state, grad_pre, pointwise_weight, same, fold, fold_b, fold_b_t)

    grad_modes, back_rows = mix(True, grad_moved, spectral_weight, sums)
    back_moved = exchange(back_rows)

    later_grad, grad_modes = lax.optimization_barrier((grad_pre, grad_modes))
    point_back = point(0, 0.5, head, "point_back", later_grad, begun_back)
    point_back, grad_modes = lax.optimization_barrier((point_back, grad_modes))

    grad_shape = (channels, channels, 2, KX, plan.owned)
    block = 5 if channels % 5 == 0 else 1
    spectral_grad = pl.pallas_call(
        functools.partial(weight_grad_kernel, block, channels),
        grid=(channels // block,),
        in_specs=[
            pl.BlockSpec((block,) + mode_shape[1:], lambda i: (i, 0, 0, 0)),
            whole(mode_shape),
        ],
        out_specs=pl.BlockSpec((block,) + grad_shape[1:], lambda i: (i, 0, 0, 0, 0)),
        out_shape=jax.ShapeDtypeStruct(grad_shape, F32),
        compiler_params=params(14),
        cost_estimate=cost(6 * 864 * 400, 1e7),
        name="weight_grad",
    )(modes, grad_modes)

    scale = 0.5 / math.sqrt(plan.width_x * width_y * width_t * width_z)
    state_grad, pointwise_grad = pl.pallas_call(
        functools.partial(final_kernel, plan, chunk, slope_tile, scale),
        in_specs=[vmem, hbm, vmem, vmem, vmem],
        out_specs=[hbm, vmem],
        out_shape=[field_shape, jax.ShapeDtypeStruct((channels, channels), F32)],
        scratch_shapes=[field, field, depth_t_shape, iz_shape] + [sems(steps)] * 2,
        compiler_params=params(FIELD_MIB),
        cost_estimate=cost(transform_flops, 2 * field_bytes),
        name="state_grad",
    )(back_moved, point_back, base_t, y_table_t, order_t)
    return (state_grad.reshape(plume_state.shape), spectral_grad, pointwise_grad)


def solution(mesh):
    placed = (
        P(("groups", "gx"), None, None, None, None),
        P(("groups", "gx"), None, None, None, None),
        P(None, None, None, None, "gx"),
        P(),
    )
    return jax.shard_map(
        functools.partial(shards, mesh.shape["gx"]),
        mesh=mesh,
        in_specs=placed,
        out_specs=(
            P(("groups", "gx"), None, None, None, None),
            P("groups", None, None, None, "gx"),
            P("groups", None),
        ),
        check_vma=False,
    )
```

```python
import functools
import math

import jax
import jax.numpy as jnp
import ml_dtypes
import numpy as np
from jax import lax
from jax.experimental import pallas as pl
from jax.experimental.pallas import tpu as pltpu
from jax.sharding import PartitionSpec as P

KX = 24
KY = 24
KZ = 24
NT = 2
ROW_GROUP = 8
TILE_ROWS = 16
BF16 = jnp.bfloat16
F32 = jnp.float32
FIELD_MIB = 51
ONE_STREAM = 3
TWO_STREAMS = 3
WEIGHT_STREAM = 8
MIB = 1024 * 1024


def rounded(table):
    return np.asarray(table, np.float64).astype(np.float32).astype(ml_dtypes.bfloat16)


def wave_tables(cells, kept):
    frequency = np.arange(kept) - kept // 2
    angle = 2.0 * np.pi / cells * (frequency[:, None] * np.arange(cells)[None, :] % cells)
    return np.cos(angle) / math.sqrt(cells), np.sin(angle) / math.sqrt(cells)


def depth_table(cells, kept):
    column = np.arange(kept)
    half = kept // 2
    frequency = np.where(column < half, column, column - half + 1)
    angle = 2.0 * np.pi / cells * (np.arange(cells)[:, None] * frequency[None, :] % cells)
    wave = np.where(column[None, :] < half, np.cos(angle), np.sin(angle))
    return wave * math.sqrt(2.0 / cells) * math.sqrt(0.5)


class Plan:
    def __init__(self, slab, channels, width_y, width_z, devices):
        self.slab = slab
        self.channels = channels
        self.width_y = width_y
        self.width_z = width_z
        self.devices = devices
        self.width_x = slab * devices
        self.pairs = KY * NT
        self.owned = self.pairs * KZ // devices
        self.kinds = 3
        self.owners = self.kinds * KZ // self.owned
        self.periods = self.pairs // self.kinds
        self.unit = math.gcd(self.owned, KZ)
        self.units = KZ // self.unit
        self.owned_units = self.owned // self.unit
        self.unit_lanes = 128 * -(-channels * self.unit // 128)
        self.lanes = self.unit_lanes * self.owned_units
        self.rows_yt = width_y * NT
        self.kind_rows = self.periods * 2
        sums = 2 * channels * -(-channels // (2 * slab))
        self.extra = 128 * -(-sums // 128)

    def y_table(self):
        cosine, sine = wave_tables(self.width_y, KY)
        both = np.stack([cosine, -sine])
        table = np.zeros((self.kinds, self.periods, 2, self.width_y, NT))
        for kind in range(self.kinds):
            for period in range(self.periods):
                pair = self.kinds * period + kind
                for time in range(NT):
                    sign = -1.0 if (time % 2 and pair % 2) else 1.0
                    table[kind, period, :, :, time] = sign * both[:, pair // 2]
        return rounded(table.reshape(self.kinds * self.kind_rows, self.rows_yt))

    def depth_base(self):
        values = depth_table(self.width_z, KZ).reshape(self.width_z, self.units, self.unit)
        table = np.zeros((self.width_z, self.units, self.unit_lanes))
        used = self.channels * self.unit
        table[:, :, :used] = np.tile(values, (1, 1, self.channels))
        return rounded(table.reshape(self.width_z, self.units * self.unit_lanes))

    def order(self):
        total = self.devices * self.slab * 2
        source = np.arange(total).reshape(self.owners, self.slab, self.periods, 2)
        source = source.transpose(2, 0, 1, 3).reshape(total)
        table = np.zeros((total, total))
        table[np.arange(total), source] = 1.0
        return rounded(table)

    def x_table(self):
        cosine, sine = wave_tables(self.width_x, KX)
        table = np.zeros((2, KX, self.width_x, 2))
        table[0, :, :, 0] = cosine
        table[0, :, :, 1] = sine
        table[1, :, :, 1] = cosine
        table[1, :, :, 0] = -sine
        return rounded(table.reshape(2 * KX, self.width_x * 2))


def dot(left, right):
    return jnp.dot(left, right, preferred_element_type=F32)


def channel_place(plan, axis):
    count = plan.units * plan.unit_lanes
    shape = (plan.width_z, count) if axis == 1 else (count, plan.width_z)
    return lax.rem(lax.broadcasted_iota(jnp.int32, shape, axis), plan.unit_lanes)


def spread_depth(plan, base_ref, depth_ref, axis):
    place = channel_place(plan, axis)
    base = base_ref[...].astype(F32)
    for channel in range(plan.channels):
        start = channel * plan.unit
        own = (place >= start) & (place < start + plan.unit)
        block = jnp.where(own, base, 0.0).astype(BF16)
        span = slice(channel * plan.width_z, (channel + 1) * plan.width_z)
        if axis == 1:
            depth_ref[span, :] = block
        else:
            depth_ref[:, span] = block


def project_depth(plan, proj_ref, depth_ref, order_ref, out_ref):
    rows = plan.slab * plan.kind_rows
    lanes = plan.unit_lanes
    flat = proj_ref[...].reshape(plan.kinds * rows, plan.channels * plan.width_z)
    parts = dot(flat, depth_ref[...]).astype(BF16)
    owners = []
    for owner in range(plan.owners):
        pieces = []
        for index in range(plan.owned_units):
            kind, unit = divmod(owner * plan.owned_units + index, plan.units)
            pieces.append(
                parts[kind * rows : (kind + 1) * rows, unit * lanes : (unit + 1) * lanes]
            )
        owners.append(jnp.concatenate(pieces, axis=1))
    joined = jnp.concatenate(owners, axis=0)
    out_ref[...] = dot(order_ref[...], joined).astype(BF16)


def restore_depth(plan, scale, rows_ref, depth_t_ref, order_t_ref, iz_ref):
    block = plan.slab * plan.kind_rows
    lanes = plan.unit_lanes
    rows = dot(order_t_ref[...], rows_ref[:, : plan.lanes]).astype(BF16)
    kinds = []
    for kind in range(plan.kinds):
        pieces = []
        for unit in range(plan.units):
            owner, index = divmod(kind * plan.units + unit, plan.owned_units)
            pieces.append(
                rows[owner * block : (owner + 1) * block, index * lanes : (index + 1) * lanes]
            )
        kinds.append(jnp.concatenate(pieces, axis=1))
    joined = jnp.concatenate(kinds, axis=0)
    total = depth_t_ref.shape[1]
    width = min(total, 512)
    for start in range(0, total, width):
        stop = min(total, start + width)
        values = dot(joined, depth_t_ref[:, start:stop])
        if scale != 1.0:
            values = values * scale
        values = values.astype(BF16)
        for kind in range(plan.kinds):
            for row in range(plan.slab):
                first = (kind * plan.slab + row) * plan.kind_rows
                iz_ref[
                    row, kind * plan.kind_rows : (kind + 1) * plan.kind_rows, start:stop
                ] = values[first : first + plan.kind_rows]


def store_projection(plan, proj_ref, row, lane, values):
    for kind in range(plan.kinds):
        proj_ref[
            kind,
            pl.ds(pl.multiple_of(row * plan.kind_rows, plan.kind_rows), plan.kind_rows),
            pl.ds(lane, values.shape[1]),
        ] = values[kind * plan.kind_rows : (kind + 1) * plan.kind_rows]


def chunk_copy(source, target, sem, chunk, index):
    parts = source.shape[1] // chunk
    place = (index // parts, pl.ds(lax.rem(index, parts) * chunk, chunk))
    return pltpu.make_async_copy(source.at[place], target.at[place], sem.at[index])


def run_ahead(copy, ahead, index, steps):
    @pl.when(index + ahead < steps)
    def _():
        copy(index + ahead).start()


def chunk_place(plan, chunk, index):
    parts = plan.channels // chunk
    return index // parts, lax.rem(index, parts) * chunk


def pair_lane(plan, channel):
    return pl.multiple_of(channel * plan.width_z, 2 * plan.width_z)


def forward_kernel(
    plan,
    chunk,
    u_hbm,
    base_hbm,
    y_hbm,
    order_hbm,
    out_ref,
    base_ref,
    y_ref,
    order_ref,
    u_ref,
    depth_ref,
    proj_ref,
    table_sem,
    u_sem,
):
    steps = plan.slab * plan.channels // chunk
    copy = functools.partial(chunk_copy, u_hbm, u_ref, u_sem, chunk)
    y_copy, base_copy, order_copy = [
        pltpu.make_async_copy(source, target, table_sem.at[index])
        for index, (source, target) in enumerate(
            ((y_hbm, y_ref), (base_hbm, base_ref), (order_hbm, order_ref))
        )
    ]
    y_copy.start()
    for index in range(min(ONE_STREAM, steps)):
        copy(index).start()
    base_copy.start()
    order_copy.start()
    y_copy.wait()

    def step(index, carry):
        copy(index).wait()
        run_ahead(copy, ONE_STREAM, index, steps)

        @pl.when(index == steps // 2)
        def _():
            base_copy.wait()
            spread_depth(plan, base_ref, depth_ref, 1)

        row, first = chunk_place(plan, chunk, index)
        for pair in range(chunk // 2):
            channel = first + 2 * pair
            values = jnp.concatenate([u_ref[row, channel], u_ref[row, channel + 1]], axis=1)
            projected = dot(y_ref[...], values).astype(BF16)
            store_projection(plan, proj_ref, row, pair_lane(plan, channel), projected)
        return carry

    lax.fori_loop(0, steps, step, 0)
    order_copy.wait()
    project_depth(plan, proj_ref, depth_ref, order_ref, out_ref)


def twice_slope(scaled):
    shift = math.log2(2.0 / math.sqrt(math.pi))
    density = jnp.exp2(scaled * (scaled * -math.log2(math.e)) + shift)
    return (lax.erf(scaled) + 1.0) + scaled * density


def middle_kernel(
    plan,
    chunk,
    tile,
    rows_ref,
    point_hbm,
    cot_hbm,
    base_ref,
    base_t_ref,
    y_ref,
    y_t_ref,
    order_ref,
    order_t_ref,
    grad_hbm,
    out_ref,
    point_ref,
    cot_ref,
    grad_ref,
    depth_ref,
    depth_t_ref,
    iz_ref,
    proj_ref,
    point_sem,
    cot_sem,
    grad_sem,
):
    z = plan.width_z
    parts = plan.channels // chunk
    steps = plan.slab * parts
    point_copy = functools.partial(chunk_copy, point_hbm, point_ref, point_sem, chunk)
    cot_copy = functools.partial(chunk_copy, cot_hbm, cot_ref, cot_sem, chunk)
    grad_copy = functools.partial(chunk_copy, grad_ref, grad_hbm, grad_sem, chunk)
    for index in range(min(TWO_STREAMS, steps)):
        point_copy(index).start()
        cot_copy(index).start()
    spread_depth(plan, base_t_ref, depth_t_ref, 0)
    spread_depth(plan, base_ref, depth_ref, 1)
    restore_depth(plan, math.sqrt(0.5), rows_ref, depth_t_ref, order_t_ref, iz_ref)
    tiles = plan.rows_yt // tile

    def step(row, carry):
        def project(channel, start, stop):
            values = jnp.concatenate(
                [grad_ref[row, channel, start:stop], grad_ref[row, channel + 1, start:stop]],
                axis=1,
            )
            return dot(y_ref[:, start:stop], values)

        def store(channel, values):
            store_projection(plan, proj_ref, row, channel * z, values.astype(BF16))

        half_rows = plan.rows_yt // 2
        for channel in range(0, plan.channels, 2):
            if channel % chunk == 0:
                index = row * parts + channel // chunk
                point_copy(index).wait()
                cot_copy(index).wait()
                run_ahead(point_copy, TWO_STREAMS, index, steps)
                run_ahead(cot_copy, TWO_STREAMS, index, steps)
            coefficients = iz_ref[row, :, channel * z : (channel + 2) * z]
            projected = None
            for place in range(tiles):
                span = slice(place * tile, (place + 1) * tile)
                spectral = dot(y_t_ref[span], coefficients)
                for half in range(2):
                    scaled = spectral[:, half * z : (half + 1) * z]
                    scaled = scaled + point_ref[row, channel + half, span].astype(F32)
                    grad = cot_ref[row, channel + half, span].astype(F32) * twice_slope(scaled)
                    grad_ref[row, channel + half, span] = grad.astype(BF16)
                if channel and place == tiles // 2 - 1:
                    projected = project(channel - 2, 0, half_rows)
            if channel:
                projected = projected + project(channel - 2, half_rows, 2 * half_rows)
                store(channel - 2, projected)
            if (channel + 2) % chunk == 0:
                grad_copy(row * parts + channel // chunk).start()
        store(plan.channels - 2, project(plan.channels - 2, 0, plan.rows_yt))
        return carry

    lax.fori_loop(0, plan.slab, step, 0)
    project_depth(plan, proj_ref, depth_ref, order_ref, out_ref)
    for index in range(steps):
        grad_copy(index).wait()


def final_kernel(
    plan,
    chunk,
    tile,
    scale,
    rows_ref,
    point_hbm,
    base_t_ref,
    y_t_ref,
    order_t_ref,
    out_hbm,
    sum_ref,
    point_ref,
    out_ref,
    depth_t_ref,
    iz_ref,
    point_sem,
    out_sem,
):
    z = plan.width_z
    steps = plan.slab * plan.channels // chunk
    copy = functools.partial(chunk_copy, point_hbm, point_ref, point_sem, chunk)
    for index in range(min(ONE_STREAM, steps)):
        copy(index).start()
    sum_ref[...] = unpack_sums(plan, rows_ref) * scale
    spread_depth(plan, base_t_ref, depth_t_ref, 0)
    restore_depth(plan, 1.0, rows_ref, depth_t_ref, order_t_ref, iz_ref)

    def step(index, carry):
        copy(index).wait()
        run_ahead(copy, ONE_STREAM, index, steps)
        row, first = chunk_place(plan, chunk, index)
        for pair in range(chunk // 2):
            channel = first + 2 * pair
            coefficients = iz_ref[row, :, pl.ds(pair_lane(plan, channel), 2 * z)]
            for start in range(0, plan.rows_yt, tile):
                span = slice(start, start + tile)
                spectral = dot(y_t_ref[span], coefficients)
                for half in range(2):
                    total = spectral[:, half * z : (half + 1) * z]
                    total = total + point_ref[row, channel + half, span].astype(F32)
                    out_ref[row, channel + half, span] = total.astype(BF16)
        chunk_copy(out_ref, out_hbm, out_sem, chunk, index).start()
        return carry

    lax.fori_loop(0, steps, step, 0)
    for index in range(steps):
        chunk_copy(out_ref, out_hbm, out_sem, chunk, index).wait()


def pack_rows(plan):
    return 2 * plan.slab


def pack_sums(plan, sums):
    rows = pack_rows(plan)
    count = -(-plan.channels // rows)
    high = sums.astype(BF16)
    low = (sums - high.astype(F32)).astype(BF16)
    pieces = []
    for part in (high.astype(F32), low.astype(F32)):
        spare = count * rows - plan.channels
        if spare:
            part = jnp.concatenate([part, jnp.zeros((spare, plan.channels), F32)], axis=0)
        pieces += [part[index * rows : (index + 1) * rows] for index in range(count)]
    used = 2 * count * plan.channels
    pieces.append(jnp.zeros((rows, plan.extra - used), F32))
    block = jnp.concatenate(pieces, axis=1)
    return jnp.concatenate([block] * plan.devices, axis=0).astype(BF16)


def unpack_sums(plan, rows_ref):
    rows = pack_rows(plan)
    count = -(-plan.channels // rows)
    block = jnp.zeros((rows, plan.extra), F32)
    values = rows_ref[:, plan.lanes : plan.lanes + plan.extra].astype(F32)
    for device in range(plan.devices):
        block = block + values[device * rows : (device + 1) * rows]
    width = plan.channels
    parts = []
    for index in range(count):
        high = block[:, index * width : (index + 1) * width]
        low = block[:, (count + index) * width : (count + index + 1) * width]
        parts.append(high + low)
    return jnp.concatenate(parts, axis=0)[: plan.channels]


def row_copy(source, target, sem, tile, index):
    parts = source.shape[2] // tile
    place = (index // parts, slice(None), pl.ds(lax.rem(index, parts) * tile, tile))
    return pltpu.make_async_copy(source.at[place], target.at[place], sem.at[index])


def row_block(ref, row, start, count):
    channels, z = ref.shape[1], ref.shape[3]
    parts = []
    for index in range(count):
        values = ref[row, :, pl.ds(start + index * TILE_ROWS, TILE_ROWS), :].astype(F32)
        for first in range(0, TILE_ROWS, ROW_GROUP):
            group = values[:, first : first + ROW_GROUP, :]
            parts.append(group.reshape(channels * ROW_GROUP, z).astype(BF16))
    return jnp.concatenate(parts, axis=1)


def spread_weight(side, weight_ref, same_ref, fold_ref, fold_t_ref, spread_ref):
    tall = lax.dot_general(
        fold_t_ref[...],
        weight_ref[...],
        (((1,), (side,)), ((), ())),
        preferred_element_type=F32,
    ).astype(BF16)
    spread_ref[...] = (dot(tall, fold_ref[...]) * same_ref[...]).astype(BF16)


def mix_rows(spread_ref, u_ref, out_ref, row, base, tile, scale):
    channels, z = u_ref.shape[1], u_ref.shape[3]
    for start in range(0, tile, TILE_ROWS):
        mixed = dot(spread_ref[...], row_block(u_ref, row, base + start, 1)) * scale
        groups = [
            mixed[:, first : first + z].reshape(channels, ROW_GROUP, z)
            for first in range(0, mixed.shape[1], z)
        ]
        values = jnp.concatenate(groups, axis=1).astype(BF16)
        out_ref[row, :, pl.ds(base + start, TILE_ROWS), :] = values


def point_kernel(
    tile, side, scale, head, weight_ref, same_ref, fold_ref, fold_t_ref, u_hbm, *rest
):
    out_hbm, u_ref, out_ref, spread_ref, u_sem, out_sem = rest[-6:]
    parts = u_hbm.shape[2] // tile
    steps = u_hbm.shape[0] * parts
    copy = functools.partial(row_copy, u_hbm, u_ref, u_sem, tile)
    for index in range(head, min(head + ONE_STREAM, steps)):
        copy(index).start()
    spread_weight(side, weight_ref, same_ref, fold_ref, fold_t_ref, spread_ref)

    def step(index, carry):
        copy(index).wait()
        run_ahead(copy, ONE_STREAM, index, steps)
        base = pl.multiple_of(lax.rem(index, parts) * tile, tile)
        mix_rows(spread_ref, u_ref, out_ref, index // parts, base, tile, scale)
        row_copy(out_ref, out_hbm, out_sem, tile, index).start()
        return carry

    lax.fori_loop(head, steps, step, 0)
    for index in range(head, steps):
        row_copy(out_ref, out_hbm, out_sem, tile, index).wait()


def point_sum_kernel(
    tile,
    head,
    mix_scale,
    u_hbm,
    g_hbm,
    weight_ref,
    same_ref,
    fold_ref,
    fold_b_ref,
    fold_b_t_ref,
    sum_ref,
    out_hbm,
    u_ref,
    g_ref,
    out_ref,
    spread_ref,
    total_ref,
    u_sem,
    g_sem,
    out_sem,
):
    parts = u_hbm.shape[2] // tile
    steps = u_hbm.shape[0] * parts
    u_copy = functools.partial(row_copy, u_hbm, u_ref, u_sem, tile)
    g_copy = functools.partial(row_copy, g_hbm, g_ref, g_sem, tile)
    out_copy = functools.partial(row_copy, out_ref, out_hbm, out_sem, tile)
    for index in range(min(TWO_STREAMS, steps)):
        u_copy(index).start()
        g_copy(index).start()
    spread_weight(0, weight_ref, same_ref, fold_b_ref, fold_b_t_ref, spread_ref)
    total_ref[...] = jnp.zeros_like(total_ref)

    def step(index, carry):
        u_copy(index).wait()
        g_copy(index).wait()
        run_ahead(u_copy, TWO_STREAMS, index, steps)
        run_ahead(g_copy, TWO_STREAMS, index, steps)
        row = index // parts
        base = pl.multiple_of(lax.rem(index, parts) * tile, tile)

        @pl.when(index < head)
        def _():
            mix_rows(spread_ref, g_ref, out_ref, row, base, tile, mix_scale)
            out_copy(index).start()

        for start in range(0, tile, 4 * TILE_ROWS):
            total_ref[...] += lax.dot_general(
                row_block(u_ref, row, base + start, 4),
                row_block(g_ref, row, base + start, 4),
                (((1,), (1,)), ((), ())),
                preferred_element_type=F32,
            )
        return carry

    lax.fori_loop(0, steps, step, 0)
    for index in range(head):
        out_copy(index).wait()
    kept = total_ref[...] * same_ref[...]
    folded = jnp.dot(
        fold_ref[...], kept, precision=lax.Precision.HIGHEST, preferred_element_type=F32
    )
    sum_ref[...] = lax.dot_general(
        folded,
        fold_ref[...],
        (((1,), (1,)), ((), ())),
        precision=lax.Precision.HIGHEST,
        preferred_element_type=F32,
    )


def mix_kernel(plan, adjoint, step, rows_ref, weight_in, x_ref, x_t_ref, *rest):
    if adjoint:
        sums_ref, *rest = rest
    modes_ref, out_ref, mixed_ref, weight_ref, weight_sem = rest
    steps = plan.channels // step

    def copy(index):
        part = pl.ds(index * step, step)
        place = (part,) if adjoint else (slice(None), part)
        return pltpu.make_async_copy(
            weight_in.at[place], weight_ref.at[place], weight_sem.at[index]
        )

    for index in range(min(WEIGHT_STREAM, steps)):
        copy(index).start()
    modes = dot(x_ref[...], rows_ref[...])
    for channel in range(plan.channels):
        pieces = []
        for index in range(plan.owned_units):
            lane = index * plan.unit_lanes + channel * plan.unit
            pieces.append(modes[:, lane : lane + plan.unit])
        joined = jnp.concatenate(pieces, axis=1)
        for part in range(2):
            modes_ref[channel, part] = joined[part * KX : (part + 1) * KX]

    def mix_one(index):
        real = jnp.zeros((KX, plan.owned), F32)
        imag = jnp.zeros((KX, plan.owned), F32)
        for channel in range(plan.channels):
            place = (index, channel) if adjoint else (channel, index)
            weight_real = weight_ref[place + (0,)].astype(F32)
            weight_imag = weight_ref[place + (1,)].astype(F32)
            mode_real = modes_ref[channel, 0]
            mode_imag = modes_ref[channel, 1]
            if adjoint:
                real += weight_real * mode_real + weight_imag * mode_imag
                imag += weight_real * mode_imag - weight_imag * mode_real
            else:
                real += weight_real * mode_real - weight_imag * mode_imag
                imag += weight_real * mode_imag + weight_imag * mode_real
        mixed_ref[index, 0] = real
        mixed_ref[index, 1] = imag

    def mix_step(index, carry):
        copy(index).wait()
        run_ahead(copy, WEIGHT_STREAM, index, steps)
        for part in range(step):
            mix_one(index * step + part)
        return carry

    lax.fori_loop(0, steps, mix_step, 0)
    for index in range(plan.owned_units):
        span = slice(index * plan.unit, (index + 1) * plan.unit)
        halves = []
        for part in range(2):
            pieces = [mixed_ref[channel, part][:, span] for channel in range(plan.channels)]
            spare = plan.unit_lanes - plan.channels * plan.unit
            if spare:
                pieces.append(jnp.zeros((KX, spare), F32))
            halves.append(jnp.concatenate(pieces, axis=1))
        columns = jnp.concatenate(halves, axis=0).astype(BF16)
        lanes = slice(index * plan.unit_lanes, (index + 1) * plan.unit_lanes)
        out_ref[:, lanes] = dot(x_t_ref[...], columns).astype(BF16)
    if adjoint:
        out_ref[:, plan.lanes :] = pack_sums(plan, sums_ref[...])


def weight_grad_kernel(block, channels, modes_ref, grads_ref, out_ref):
    for index in range(block):
        mode_real = modes_ref[index, 0]
        mode_imag = modes_ref[index, 1]
        for channel in range(channels):
            grad_real = grads_ref[channel, 0]
            grad_imag = grads_ref[channel, 1]
            out_ref[index, channel, 0] = grad_real * mode_real + grad_imag * mode_imag
            out_ref[index, channel, 1] = grad_imag * mode_real - grad_real * mode_imag


def whole(shape):
    return pl.BlockSpec(shape, lambda *_: (0,) * len(shape))


def params(mebibytes):
    return pltpu.CompilerParams(vmem_limit_bytes=mebibytes * MIB)


def cost(flops, moved, transcendentals=0):
    return pl.CostEstimate(
        flops=int(flops), bytes_accessed=int(moved), transcendentals=int(transcendentals)
    )


def shards(devices, plume_state, out_cotangent, spectral_weight, pointwise_weight):
    slab, channels, width_y, width_t, width_z = plume_state.shape
    plan = Plan(slab, channels, width_y, width_z, devices)
    rows = plan.rows_yt
    chunk = 10 if channels % 10 == 0 else channels
    steps = slab * (channels // chunk)
    flat = (slab, channels, rows, width_z)
    state = plume_state.reshape(flat)
    cotangent = out_cotangent.reshape(flat)
    field_bytes = 2 * math.prod(flat)
    exchanged = (devices * slab * 2, plan.lanes)
    exchanged_back = (devices * slab * 2, plan.lanes + plan.extra)

    y_table = jnp.asarray(plan.y_table())
    y_table_t = jnp.asarray(np.ascontiguousarray(plan.y_table().T))
    base = jnp.asarray(plan.depth_base())
    base_t = jnp.asarray(np.ascontiguousarray(plan.depth_base().T))
    order = jnp.asarray(plan.order())
    order_t = jnp.asarray(np.ascontiguousarray(plan.order().T))
    x_table = jnp.asarray(plan.x_table())
    x_table_half = jnp.asarray((plan.x_table().astype(np.float32) * 0.5).astype(ml_dtypes.bfloat16))
    x_table_t = jnp.asarray(np.ascontiguousarray(plan.x_table().T))

    hbm = pl.BlockSpec(memory_space=pl.ANY)
    vmem = pl.BlockSpec(memory_space=pltpu.VMEM)
    field_shape = jax.ShapeDtypeStruct(flat, BF16)
    field = pltpu.VMEM(flat, BF16)
    proj_shape = pltpu.VMEM((plan.kinds, slab * plan.kind_rows, channels * width_z), BF16)
    iz_shape = pltpu.VMEM((slab, plan.kinds * plan.kind_rows, channels * width_z), BF16)
    depth_shape = pltpu.VMEM((channels * width_z, base.shape[1]), BF16)
    depth_t_shape = pltpu.VMEM((base.shape[1], channels * width_z), BF16)
    transform_flops = 2 * math.prod(flat) * 96 * 2
    mode_shape = (channels, 2, KX, plan.owned)

    def sems(count):
        return pltpu.SemaphoreType.DMA((count,))

    def exchange(values):
        blocks = values.reshape(devices, slab * 2, values.shape[1])
        moved = lax.all_to_all(blocks, "gx", split_axis=0, concat_axis=0, tiled=True)
        return moved.reshape(values.shape)

    def mix(adjoint, moved, weight, *sums):
        sent = exchanged_back if adjoint else exchanged
        step = 4 if channels % 4 == 0 else channels
        scratch = [
            pltpu.VMEM(mode_shape, F32),
            pltpu.VMEM(weight.shape, BF16),
            sems(channels // step),
        ]
        return pl.pallas_call(
            functools.partial(mix_kernel, plan, adjoint, step),
            in_specs=[vmem, hbm] + [vmem] * (2 + len(sums)),
            out_specs=[vmem, vmem],
            out_shape=[
                jax.ShapeDtypeStruct(mode_shape, F32),
                jax.ShapeDtypeStruct(sent, BF16),
            ],
            scratch_shapes=scratch,
            compiler_params=params(53),
            cost_estimate=cost(8 * 864 * 400, 5e6),
            name="mix_back" if adjoint else "mix_modes",
        )(moved, weight, x_table_half if adjoint else x_table, x_table_t, *sums)

    sent = pl.pallas_call(
        functools.partial(forward_kernel, plan, chunk),
        in_specs=[hbm, hbm, hbm, hbm],
        out_specs=vmem,
        out_shape=jax.ShapeDtypeStruct(exchanged, BF16),
        scratch_shapes=[
            pltpu.VMEM(base.shape, BF16),
            pltpu.VMEM(y_table.shape, BF16),
            pltpu.VMEM(order.shape, BF16),
            field,
            depth_shape,
            proj_shape,
            sems(3),
            sems(steps),
        ],
        compiler_params=params(58),
        cost_estimate=cost(transform_flops, field_bytes),
        name="forward_rows",
    )(state, base, y_table, order)
    moved = exchange(sent)

    spread = channels * ROW_GROUP
    same = np.kron(np.ones((channels, channels)), np.eye(ROW_GROUP)).astype(np.float32)
    same = jnp.asarray(same)
    fold_rows = np.kron(np.eye(channels), np.ones((1, ROW_GROUP)))
    fold = jnp.asarray(fold_rows.astype(np.float32))
    fold_b = jnp.asarray(rounded(fold_rows))
    fold_b_t = jnp.asarray(rounded(np.ascontiguousarray(fold_rows.T)))
    tile = min(256, rows)
    row_steps = slab * (rows // tile)
    mixing_flops = 2 * math.prod(flat) * spread

    modes, mixed_rows = mix(False, moved, spectral_weight)
    later_state, mixed_rows = lax.optimization_barrier((state, mixed_rows))
    spread_shape = pltpu.VMEM((spread, spread), BF16)

    def point(side, scale, head, name, values, *begun):
        return pl.pallas_call(
            functools.partial(point_kernel, tile, side, scale, head),
            in_specs=[vmem] * 4 + [hbm] * (1 + len(begun)),
            out_specs=hbm,
            out_shape=field_shape,
            scratch_shapes=[field, field, spread_shape, sems(row_steps), sems(row_steps)],
            input_output_aliases={5: 0} if begun else {},
            compiler_params=params(FIELD_MIB),
            cost_estimate=cost(mixing_flops, 2 * field_bytes),
            name=name,
        )(pointwise_weight, same, fold_b, fold_b_t, values, *begun)

    point_state = point(1, math.sqrt(0.5), 0, "point_mix", later_state)

    restored = exchange(mixed_rows)

    slope_tile = min(128, rows)
    grad_pre, grad_rows = pl.pallas_call(
        functools.partial(middle_kernel, plan, chunk, slope_tile),
        in_specs=[vmem, hbm, hbm] + [vmem] * 6,
        out_specs=[hbm, vmem],
        out_shape=[field_shape, jax.ShapeDtypeStruct(exchanged, BF16)],
        scratch_shapes=[field, field, field, depth_shape, depth_t_shape, iz_shape, proj_shape]
        + [sems(steps)] * 3,
        compiler_params=params(FIELD_MIB),
        cost_estimate=cost(2 * transform_flops, 3 * field_bytes, 2 * math.prod(flat)),
        name="activation_grad",
    )(restored, point_state, cotangent, base, base_t, y_table, y_table_t, order, order_t)

    grad_moved = exchange(grad_rows)

    head = max(1, row_steps // 8)
    sums, begun_back = pl.pallas_call(
        functools.partial(point_sum_kernel, tile, head, 0.5),
        in_specs=[hbm, hbm] + [vmem] * 5,
        out_specs=[vmem, hbm],
        out_shape=[jax.ShapeDtypeStruct((channels, channels), F32), field_shape],
        scratch_shapes=[field, field, field, spread_shape, pltpu.VMEM((spread, spread), F32)]
        + [sems(row_steps)] * 3,
        compiler_params=params(FIELD_MIB),
        cost_estimate=cost(mixing_flops, 2 * field_bytes),
        name="point_sum",
    )(state, grad_pre, pointwise_weight, same, fold, fold_b, fold_b_t)

    grad_modes, back_rows = mix(True, grad_moved, spectral_weight, sums)
    back_moved = exchange(back_rows)

    later_grad, grad_modes = lax.optimization_barrier((grad_pre, grad_modes))
    point_back = point(0, 0.5, head, "point_back", later_grad, begun_back)
    point_back, grad_modes = lax.optimization_barrier((point_back, grad_modes))

    grad_shape = (channels, channels, 2, KX, plan.owned)
    block = 5 if channels % 5 == 0 else 1
    spectral_grad = pl.pallas_call(
        functools.partial(weight_grad_kernel, block, channels),
        grid=(channels // block,),
        in_specs=[
            pl.BlockSpec((block,) + mode_shape[1:], lambda i: (i, 0, 0, 0)),
            whole(mode_shape),
        ],
        out_specs=pl.BlockSpec((block,) + grad_shape[1:], lambda i: (i, 0, 0, 0, 0)),
        out_shape=jax.ShapeDtypeStruct(grad_shape, F32),
        compiler_params=params(14),
        cost_estimate=cost(6 * 864 * 400, 1e7),
        name="weight_grad",
    )(modes, grad_modes)

    scale = 0.5 / math.sqrt(plan.width_x * width_y * width_t * width_z)
    state_grad, pointwise_grad = pl.pallas_call(
        functools.partial(final_kernel, plan, chunk, slope_tile, scale),
        in_specs=[vmem, hbm, vmem, vmem, vmem],
        out_specs=[hbm, vmem],
        out_shape=[field_shape, jax.ShapeDtypeStruct((channels, channels), F32)],
        scratch_shapes=[field, field, depth_t_shape, iz_shape] + [sems(steps)] * 2,
        compiler_params=params(FIELD_MIB),
        cost_estimate=cost(transform_flops, 2 * field_bytes),
        name="state_grad",
    )(back_moved, point_back, base_t, y_table_t, order_t)
    return (state_grad.reshape(plume_state.shape), spectral_grad, pointwise_grad)


def solution(mesh):
    placed = (
        P(("groups", "gx"), None, None, None, None),
        P(("groups", "gx"), None, None, None, None),
        P(None, None, None, None, "gx"),
        P(),
    )
    return jax.shard_map(
        functools.partial(shards, mesh.shape["gx"]),
        mesh=mesh,
        in_specs=placed,
        out_specs=(
            P(("groups", "gx"), None, None, None, None),
            P("groups", None, None, None, "gx"),
            P("groups", None),
        ),
        check_vma=False,
    )
```
